32 devices in a mesh: dp: 8 (over z, y), seq: 4 (over x, core).
Axes of the slice: x: 2, y: 2, z: 4, core: 2. Of those that a mesh axis runs over, the one named last changes fastest.
Arguments:
- tokens: bfloat16 [8, 512, 2048], P('dp', 'seq'), may hold values from -6 to 6
- doc_ids: int32 [8, 512], P('dp', 'seq'), may hold values from 0 to 7, as said below
- query_key_value_weight: bfloat16 [2048, 4096], P(('dp', 'seq')), may hold values from -0.125 to 0.125
- out_weight: bfloat16 [2048, 2048], P(('dp', 'seq')), may hold values from -1 to 1
- gate_up_weight: bfloat16 [2048, 2, 6144], P(('dp', 'seq')), may hold values from -0.125 to 0.125
- down_weight: bfloat16 [2048, 6144], P(('dp', 'seq')), may hold values from -0.078125 to 0.078125
- attn_gain: bfloat16 [2048], P(('dp', 'seq')), may hold values from 0.5 to 1.5
- q_gain: bfloat16 [128], P(('dp', 'seq')), may hold values from 0.5 to 1.5
- k_gain: bfloat16 [128], P(('dp', 'seq')), may hold values from 0.5 to 1.5
- mlp_gain: bfloat16 [2048], P(('dp', 'seq')), may hold values from 0.5 to 1.5
- out_grad: bfloat16 [8, 512, 2048], P('dp', 'seq'), may hold values from -6 to 6
Outputs:
- output: bfloat16 [8, 512, 2048], P('dp', 'seq')
- token_grad: bfloat16 [8, 512, 2048], P('dp', 'seq')
- grad_qkv: float32 [2048, 4096], P(('dp', 'seq'))
- grad_out: float32 [2048, 2048], P(('dp', 'seq'))
- grad_gate_up: float32 [2048, 2, 6144], P(('dp', 'seq'))
- grad_down: float32 [2048, 6144], P(('dp', 'seq'))
- grad_attn_gain: float32 [2048], P(('dp', 'seq'))
- grad_q_gain: float32 [128], P(('dp', 'seq'))
- grad_k_gain: float32 [128], P(('dp', 'seq'))
- grad_mlp_gain: float32 [2048], P(('dp', 'seq'))
The draws below stay inside these ranges and needn't reach their ends.
Inputs may be any that keep to these rules, and one draw needn't show every extreme that they name: `doc_ids`: along each sequence the doc ids never fall; the first token has 0 and the last has the maximum; ids may skip values.
All inputs are finite; a program needn't handle non-finite values.
Results may differ from the reference program's by a relative error of at most 0.018.
Values may be sent and summed in bfloat16 or wider, within the bound.
No kernel may reach another device: no remote copies, remote signals or barrier semaphores. Data moves between devices by JAX's collectives and lax.ppermute only.
A program may use at most 704 MiB of HBM per device.

```python
import math
import jax
import jax.numpy as jnp
from jax import lax

MODEL_WIDTH = 2048
QUERY_HEADS = 16
KEY_VALUE_HEADS = 8
HEAD_SIZE = 128
FF = 6144
SEQS = 8
SEQ_LEN = 512


def draw_doc_ids(key, part):
    key = jax.random.fold_in(key, 11)
    key_cuts, key_late, key_pick = jax.random.split(key, 3)
    cuts = jax.random.randint(key_cuts, (SEQS, 7), 1, SEQ_LEN)
    late = jax.random.randint(key_late, (SEQS, 7), SEQ_LEN - SEQ_LEN // 16, SEQ_LEN)
    chosen = jax.random.randint(key_pick, (), 0, SEQS)
    sequence_index = jnp.arange(SEQS)
    cuts = jnp.where((sequence_index == chosen)[:, None], late, cuts)
    place = jnp.arange(SEQ_LEN)
    return jnp.sum((place[None, :, None] >= cuts[:, None, :]).astype(jnp.int32), axis=2).astype(jnp.int32)


def level_of(rng, extent, cuts, low, top_value):
    level, own = 1.0, jax.random.fold_in(rng, 6)
    for dim, blocks in cuts:
        steps = jnp.exp(jax.random.uniform(jax.random.fold_in(own, dim), (blocks,), jnp.float32, low / len(cuts), top_value / len(cuts)))
        level = level * jnp.repeat(steps, extent[dim] // blocks).reshape([-1 if axis == dim else 1 for axis in range(len(extent))])
    return level


def gaussian(stream_key, shape, deviation, reach, cuts=(), kind=jnp.bfloat16):
    array = deviation * jax.random.normal(stream_key, shape, jnp.float32)
    if cuts:
        array = array * level_of(stream_key, shape, cuts, -0.22, 0.18)
    return jnp.clip(array, -reach, reach).astype(kind)


def setup_inputs(seed: int = 0) -> dict:
    key_list = jax.random.split(jax.random.key(seed), 12)
    tokens = gaussian(key_list[0], (SEQS, SEQ_LEN, MODEL_WIDTH), 1.0, 6.0, ((0, 8), (1, 4)))
    doc_ids = draw_doc_ids(jax.random.fold_in(key_list[11], 71), 0)
    query_key_value_weight = gaussian(key_list[2], (MODEL_WIDTH, QUERY_HEADS * HEAD_SIZE + 2 * KEY_VALUE_HEADS * HEAD_SIZE), MODEL_WIDTH ** -0.5, 0.125, ((0, 32),))
    out_weight = gaussian(key_list[3], (MODEL_WIDTH, QUERY_HEADS * HEAD_SIZE), (HEAD_SIZE // 4) ** -0.5, 1.0, ((0, 32),))
    gate_up_weight = gaussian(key_list[4], (MODEL_WIDTH, 2, FF), MODEL_WIDTH ** -0.5, 0.125, ((0, 32),))
    down_weight = gaussian(key_list[5], (MODEL_WIDTH, FF), FF ** -0.5, 0.078125, ((0, 32),))
    attn_gain = jnp.clip(1.0 + 0.1 * jax.random.normal(key_list[6], (MODEL_WIDTH,), jnp.float32), 0.5, 1.5).astype(jnp.bfloat16)
    q_gain = jnp.clip(1.0 + 0.1 * jax.random.normal(key_list[7], (HEAD_SIZE,), jnp.float32), 0.5, 1.5).astype(jnp.bfloat16)
    k_gain = jnp.clip(1.0 + 0.1 * jax.random.normal(key_list[8], (HEAD_SIZE,), jnp.float32), 0.5, 1.5).astype(jnp.bfloat16)
    mlp_gain = jnp.clip(1.0 + 0.1 * jax.random.normal(key_list[9], (MODEL_WIDTH,), jnp.float32), 0.5, 1.5).astype(jnp.bfloat16)
    out_grad = gaussian(key_list[10], (SEQS, SEQ_LEN, MODEL_WIDTH), 1.0, 6.0, ((0, 8), (1, 4)))
    return dict(tokens=tokens, doc_ids=doc_ids, query_key_value_weight=query_key_value_weight, out_weight=out_weight, gate_up_weight=gate_up_weight, down_weight=down_weight, attn_gain=attn_gain, q_gain=q_gain, k_gain=k_gain, mlp_gain=mlp_gain, out_grad=out_grad)


EPS = 1e-06
THETA = 1000000.0
HIGH = lax.Precision.HIGHEST

@jax.custom_vjp
def lower_precision(v):
    return lax.optimization_barrier(v.astype(jnp.bfloat16)).astype(jnp.float32)

@jax.custom_vjp
def low_back(v):
    return v

def low_keep(v):
    return (lower_precision(v), None)

def low_pass(kept, grad):
    return (grad,)

def back_keep(v):
    return (v, None)

def back_low(kept, grad):
    return (lower_precision(grad),)
lower_precision.defvjp(low_keep, low_pass)
low_back.defvjp(back_keep, back_low)

def both_ways(value):
    return low_back(lower_precision(value))

def norm_rows(value, gain):
    return value * lax.rsqrt(lax.optimization_barrier(jnp.mean(value * value, axis=-1, keepdims=True)) + EPS) * gain

def rotate(value, position):
    half = value.shape[-1] // 2
    freqs = jnp.exp(jnp.arange(half).astype(jnp.float32) * (-math.log(THETA) / half))
    angle = position[:, None] * freqs[None, :]
    cosine = jnp.cos(angle)[:, None, :]
    sine = jnp.sin(angle)[:, None, :]
    first_half = value[..., :half]
    second_half = value[..., half:]
    return jnp.concatenate([first_half * cosine - second_half * sine, second_half * cosine + first_half * sine], axis=-1)

def attend_block(query_rows, query_index, query_doc, key_rows, value_rows, key_doc, score_scale):
    raw = jnp.einsum('qhgd,khd->hgqk', query_rows, key_rows, precision=HIGH)
    raw = low_back(raw)
    key_index = jnp.arange(key_rows.shape[0], dtype=jnp.int32)
    allowed = (key_doc[None, :] == query_doc[:, None]) & (key_index[None, :] <= query_index[:, None])
    scores = jnp.where(allowed[None, None], raw * score_scale, -1000000000.0)
    peak = lax.optimization_barrier(jnp.max(scores, axis=-1, keepdims=True))
    weights_exp = jnp.exp(scores - peak)
    probs = weights_exp / lax.optimization_barrier(jnp.sum(weights_exp, axis=-1, keepdims=True))
    return jnp.einsum('hgqk,khd->qhgd', lower_precision(probs), value_rows, precision=HIGH)

def layer(tokens_row, doc_row, w_qkv, w_out, w_gate_up, w_down, g_attn, g_query, g_key, g_mlp):
    sequence_length = tokens_row.shape[0]
    query_width = QUERY_HEADS * HEAD_SIZE
    key_value_width = KEY_VALUE_HEADS * HEAD_SIZE
    query_groups = QUERY_HEADS // KEY_VALUE_HEADS
    index = jnp.arange(sequence_length, dtype=jnp.int32)
    doc_start = lax.optimization_barrier(jnp.sum((doc_row[None, :] < doc_row[:, None]).astype(jnp.int32), axis=1))
    position = (index - doc_start).astype(jnp.float32)
    normed = lower_precision(norm_rows(tokens_row, g_attn))
    projected_output = low_back(jnp.dot(normed, w_qkv, precision=HIGH))
    query_rows = projected_output[:, :query_width].reshape(sequence_length, QUERY_HEADS, HEAD_SIZE)
    key_rows = projected_output[:, query_width:query_width + key_value_width].reshape(sequence_length, KEY_VALUE_HEADS, HEAD_SIZE)
    value_rows = lower_precision(projected_output[:, query_width + key_value_width:].reshape(sequence_length, KEY_VALUE_HEADS, HEAD_SIZE))
    query_rows = both_ways(rotate(norm_rows(query_rows, g_query), position))
    key_rows = both_ways(rotate(norm_rows(key_rows, g_key), position))
    rows_per_block = min(512, sequence_length)
    count_of_blocks = sequence_length // rows_per_block
    blocks_of_query = query_rows.reshape(count_of_blocks, rows_per_block, KEY_VALUE_HEADS, query_groups, HEAD_SIZE)

    def one_block(item):
        return attend_block(item[0], item[1], item[2], key_rows, value_rows, doc_row, HEAD_SIZE ** (-0.5))
    attended = lax.map(jax.checkpoint(one_block), (blocks_of_query, index.reshape(count_of_blocks, rows_per_block), doc_row.reshape(count_of_blocks, rows_per_block)))
    attended = both_ways(attended.reshape(sequence_length, query_width))
    branch = low_back(jnp.dot(attended, w_out.T, precision=HIGH))
    middle = tokens_row + branch
    normed_mid = lower_precision(norm_rows(middle, g_mlp))
    gate = low_back(jnp.dot(normed_mid, w_gate_up[:, 0, :], precision=HIGH))
    upward = low_back(jnp.dot(normed_mid, w_gate_up[:, 1, :], precision=HIGH))
    hidden = lower_precision(jax.nn.silu(gate) * upward)
    return middle + low_back(jnp.dot(hidden, w_down.T, precision=HIGH))

def reference(tokens, doc_ids, query_key_value_weight, out_weight, gate_up_weight, down_weight, attn_gain, q_gain, k_gain, mlp_gain, out_grad):
    weights = (query_key_value_weight.astype(jnp.float32), out_weight.astype(jnp.float32), gate_up_weight.astype(jnp.float32), down_weight.astype(jnp.float32), attn_gain.astype(jnp.float32), q_gain.astype(jnp.float32), k_gain.astype(jnp.float32), mlp_gain.astype(jnp.float32))

    def per_sequence(carry, item):
        tokens_row, doc_row, grad_row = item

        def forward(x_row, *params):
            return layer(x_row, doc_row, *params)
        result, pullback = jax.vjp(forward, tokens_row.astype(jnp.float32), *weights)
        grads = pullback(grad_row.astype(jnp.float32))
        carry = tuple((total + piece for total, piece in zip(carry, grads[1:])))
        return (carry, (result.astype(jnp.bfloat16), grads[0].astype(jnp.bfloat16)))
    zeros = tuple((jnp.zeros(w.shape, jnp.float32) for w in weights))
    totals, (output, token_grad) = lax.scan(per_sequence, zeros, (tokens, doc_ids, out_grad))
    return (output, token_grad, totals[0], totals[1], totals[2], totals[3], totals[4], totals[5], totals[6], totals[7])
```

```python
import math

import jax
import jax.numpy as jnp
from jax import lax
from jax.sharding import Mesh, PartitionSpec as P

QUERY_HEADS = 16
KEY_VALUE_HEADS = 8
HEAD_SIZE = 128
EPS = 1e-06
THETA = 1000000.0

F32 = jnp.float32
BF16 = jnp.bfloat16
SWAP = [(0, 1), (1, 0)]
DIAGONAL = [(0, 3), (1, 2), (2, 1), (3, 0)]
TEAM = ("zl", "xl", "c")
AXES = ("zh", "zl", "y", "xh", "xl", "c")
CHUNKS = 3


def dot(left, right):
    return lax.dot_general(left, right, (((1,), (0,)), ((), ())), preferred_element_type=F32)


def dot_nt(left, right):
    return lax.dot_general(left, right, (((1,), (1,)), ((), ())), preferred_element_type=F32)


def dot_tn(left, right):
    return lax.dot_general(left, right, (((0,), (0,)), ((), ())), preferred_element_type=F32)


def from_next(value, axis, size, step):
    return lax.ppermute(value, axis, [((i + step) % size, i) for i in range(size)])


def to_next(value, axis, size, step):
    return lax.ppermute(value, axis, [(i, (i + step) % size) for i in range(size)])


class Layout:
    def __init__(self, sizes):
        self.zh, self.y, self.xh = sizes["zh"], sizes["y"], sizes["xh"]
        self.groups = self.zh * self.y * self.xh

    def relative(self, value):
        lead = value.shape[:-1]
        cut = value.shape[-1] // (self.groups * 2)
        v = value.reshape(lead + (self.zh, 2, self.y, self.xh, cut))
        n = len(lead)
        for axis, name, size in ((n, "zh", self.zh), (n + 2, "y", self.y), (n + 3, "xh", self.xh)):
            if size > 1:
                v = jnp.roll(v, -lax.axis_index(name), axis=axis)
        v = jnp.moveaxis(v, n + 1, n + 3)
        return v.reshape(value.shape)

    def natural(self, value):
        lead = value.shape[:-1]
        cut = value.shape[-1] // (self.groups * 2)
        v = value.reshape(lead + (self.zh, self.y, self.xh, 2, cut))
        n = len(lead)
        v = jnp.moveaxis(v, n + 3, n + 1)
        for axis, name, size in ((n, "zh", self.zh), (n + 2, "y", self.y), (n + 3, "xh", self.xh)):
            if size > 1:
                v = jnp.roll(v, lax.axis_index(name), axis=axis)
        return v.reshape(value.shape)

    def gather(self, block):
        found = {(0, 0, 0): block}
        for k in range(1, self.zh):
            found[k, 0, 0] = from_next(block, "zh", self.zh, k)
        for k in range(self.zh):
            for j in range(1, self.y):
                found[k, j, 0] = from_next(found[k, 0, 0], "y", self.y, j)
        for k in range(self.zh):
            for j in range(self.y):
                for i in range(1, self.xh):
                    found[k, j, i] = from_next(found[k, j, 0], "xh", self.xh, i)
        return jnp.concatenate([found[key] for key in sorted(found)], axis=0)

    def scatter(self, terms):
        rows = terms.shape[0] // self.groups
        part = {}
        for k in range(self.zh):
            for j in range(self.y):
                for i in range(self.xh):
                    at = ((k * self.y + j) * self.xh + i) * rows
                    part[k, j, i] = terms[at : at + rows]
        for k in reversed(range(self.zh)):
            for j in reversed(range(self.y)):
                for i in range(1, self.xh):
                    part[k, j, 0] = part[k, j, 0] + to_next(
                        part[k, j, i].astype(BF16), "xh", self.xh, i
                    ).astype(F32)
        for k in reversed(range(self.zh)):
            for j in range(1, self.y):
                part[k, 0, 0] = part[k, 0, 0] + to_next(
                    part[k, j, 0].astype(BF16), "y", self.y, j
                ).astype(F32)
        for k in range(1, self.zh):
            part[0, 0, 0] = part[0, 0, 0] + to_next(
                part[k, 0, 0].astype(BF16), "zh", self.zh, k
            ).astype(F32)
        return part[0, 0, 0]


def team_gather(block):
    far = lax.ppermute(block, ("zl", "xl"), DIAGONAL)
    over_z = lax.ppermute(block, "zl", SWAP)
    over_x = lax.ppermute(block, "xl", SWAP)
    half = jnp.concatenate([block, over_x, over_z, far], axis=0)
    return jnp.concatenate([half, lax.ppermute(half, "c", SWAP)], axis=0)


def team_scatter(term):
    other = lax.ppermute(term(1).astype(BF16), "c", SWAP)
    mine = term(0) + other.astype(F32)
    rows = mine.shape[0] // 4
    far = lax.ppermute(mine[3 * rows :].astype(BF16), ("zl", "xl"), DIAGONAL)
    over_z = lax.ppermute(mine[2 * rows : 3 * rows].astype(BF16), "zl", SWAP)
    over_x = lax.ppermute(mine[rows : 2 * rows].astype(BF16), "xl", SWAP)
    return mine[:rows] + over_x.astype(F32) + over_z.astype(F32) + far.astype(F32)


def exchange(value):
    return lax.all_to_all(value, TEAM, 0, 0, tiled=True)


def all_sum(value, sizes):
    for axis in ("c", "xl", "zl", "y", "xh", "zh"):
        total = value
        for k in range(1, sizes[axis]):
            total = total + from_next(value, axis, sizes[axis], k)
        value = total
    return value


def device_index(sizes):
    index = 0
    for axis in AXES:
        index = index * sizes[axis] + lax.axis_index(axis)
    return index


def inverse_rms(value):
    return lax.rsqrt(jnp.mean(value * value, axis=-1, keepdims=True) + EPS)


def norm_input_gradient(normed, inverse, e):
    return inverse * (e - normed * jnp.mean(e * normed, axis=-1, keepdims=True))


def turn(value, cosine, sine):
    half = value.shape[-1] // 2
    a, b = value[..., :half], value[..., half:]
    return jnp.concatenate([a * cosine - b * sine, b * cosine + a * sine], axis=-1)


def layer(
    sizes,
    tokens,
    doc_ids,
    w_qkv_rows,
    w_out_rows,
    w_gate_up_rows,
    w_down_rows,
    attn_gain,
    q_gain,
    k_gain,
    mlp_gain,
    out_grad,
):
    layout = Layout(sizes)
    rows = tokens.shape[1]
    width = tokens.shape[2]
    team = 8
    owned = w_qkv_rows.shape[0]
    devices = width // owned
    heads = QUERY_HEADS // team
    q_width = heads * HEAD_SIZE
    ff = w_down_rows.shape[1]
    slice_ff = ff // team
    chunk = slice_ff // CHUNKS
    scale = HEAD_SIZE ** (-0.5)
    team_tokens = team * rows

    q_cols = QUERY_HEADS * HEAD_SIZE
    kv_cols = KEY_VALUE_HEADS * HEAD_SIZE

    def per_member(value):
        return jnp.moveaxis(value.reshape(owned, team, -1), 1, 0)

    send_qkv = jnp.concatenate(
        [
            per_member(w_qkv_rows[:, :q_cols]),
            per_member(w_qkv_rows[:, q_cols : q_cols + kv_cols]),
            per_member(w_qkv_rows[:, q_cols + kv_cols :]),
        ],
        axis=2,
    )
    w_qkv = layout.gather(exchange(send_qkv).reshape(team * owned, -1))
    w_out = layout.gather(exchange(per_member(w_out_rows)).reshape(team * owned, -1))
    gate_all = w_gate_up_rows[:, 0, :].reshape(owned, team, CHUNKS, chunk)
    up_all = w_gate_up_rows[:, 1, :].reshape(owned, team, CHUNKS, chunk)
    down_all = w_down_rows.reshape(owned, team, CHUNKS, chunk)
    w_mlp = []
    for j in range(CHUNKS):
        send = jnp.concatenate(
            [jnp.moveaxis(w[:, :, j, :], 1, 0) for w in (gate_all, up_all, down_all)], axis=2
        )
        w_mlp.append(layout.gather(exchange(send).reshape(team * owned, -1)))

    gains = jnp.concatenate([attn_gain, mlp_gain, q_gain, k_gain])[None]
    table = jnp.zeros((devices, gains.shape[1]), BF16)
    table = lax.dynamic_update_slice(table, gains, (device_index(sizes), 0))
    table = all_sum(table, sizes).astype(F32)
    small = q_gain.shape[0]
    g_attn = layout.relative(table[:, :owned].reshape(1, width))
    g_mlp = layout.relative(table[:, owned : 2 * owned].reshape(1, width))
    g_q = table[:, 2 * owned : 2 * owned + small].reshape(-1)
    g_k = table[:, 2 * owned + small :].reshape(-1)

    doc_team = team_gather(doc_ids.reshape(1, rows))
    place = (
        lax.axis_index("xh") * 4
        + (lax.axis_index("xl") ^ jnp.arange(2))[None, :] * 2
        + (lax.axis_index("c") ^ jnp.arange(2))[:, None]
    )
    index_own = (place[:, :, None] * rows + jnp.arange(rows)).reshape(-1).astype(jnp.int32)

    def by_sequence(value):
        tail = value.shape[1:]
        v = value.reshape((2, 2, 2, rows) + tail)
        return jnp.moveaxis(v, 1, 0).reshape((2, 4 * rows) + tail)

    def by_core(value):
        tail = value.shape[2:]
        v = value.reshape((2, 2, 2, rows) + tail)
        return jnp.moveaxis(v, 0, 1).reshape((8 * rows,) + tail)

    def all_keys(value):
        if sizes["xh"] == 1:
            return value
        return lax.all_gather(value, "xh", axis=1, tiled=True)

    doc_q = by_sequence(doc_team.reshape(-1))
    doc_k = all_keys(doc_q)
    index_k = all_keys(jnp.broadcast_to(index_own, doc_q.shape))
    doc_start = jnp.sum((doc_k[:, None, :] < doc_q[:, :, None]).astype(jnp.int32), axis=2)
    position = (index_own - doc_start).astype(F32)
    allowed = (doc_k[:, None, :] == doc_q[:, :, None]) & (index_k[:, None, :] <= index_own[None, :, None])
    half = HEAD_SIZE // 2
    freqs = jnp.exp(jnp.arange(half).astype(F32) * (-math.log(THETA) / half))
    angle = position.reshape(2, -1, 1) * freqs
    cosine, sine = jnp.cos(angle)[:, :, None, :], jnp.sin(angle)[:, :, None, :]

    x_own = layout.relative(tokens[0])
    dy_own = layout.relative(out_grad[0])
    x_team = team_gather(x_own).astype(F32)
    normed_in = (x_team * inverse_rms(x_team) * g_attn).astype(BF16)
    projected = by_sequence(dot(normed_in, w_qkv))
    q_raw = projected[:, :, :q_width].reshape(2, -1, heads, HEAD_SIZE)
    k_raw = projected[:, :, q_width : q_width + HEAD_SIZE].reshape(2, -1, 1, HEAD_SIZE)
    value_own = projected[:, :, q_width + HEAD_SIZE :].astype(BF16)
    q_inverse, k_inverse = inverse_rms(q_raw), inverse_rms(k_raw)
    q_normed, k_normed = q_raw * q_inverse, k_raw * k_inverse
    queries = turn(q_normed * g_q, cosine, sine).astype(BF16)
    keys_own = turn(k_normed * g_k, cosine, sine).astype(BF16)[:, :, 0]
    keys, values = all_keys(keys_own), all_keys(value_own)
    queries = jnp.moveaxis(queries, 2, 1)

    def pair(left, right, spec):
        return jnp.einsum(spec, left, right, preferred_element_type=F32)

    scores = jnp.where(allowed[:, None], pair(queries, keys, "shqd,skd->shqk") * scale, -1e9)
    peak = jnp.max(scores, axis=-1, keepdims=True)
    weights_exp = jnp.exp(scores - peak)
    probs = weights_exp / jnp.sum(weights_exp, axis=-1, keepdims=True)
    probs_b = probs.astype(BF16)
    attended = pair(probs_b, values, "shqk,skd->sqhd").astype(BF16)
    attended = by_core(attended.reshape(2, -1, q_width))

    cut = team_tokens // 2

    def of_core(value, which):
        return value[which * cut : (which + 1) * cut]

    branch = team_scatter(lambda which: dot_nt(of_core(attended, which), w_out))
    middle = x_own.astype(F32) + branch
    mid_inverse = inverse_rms(middle)
    mid_normed = middle * mid_inverse

    nm = team_gather((mid_normed * g_mlp).astype(BF16))
    dy = team_gather(dy_own)
    hidden, d_gate_up = [], []
    grads_mlp = []
    for j in range(CHUNKS):
        w = w_mlp[j]
        gate, upward = dot(nm, w[:, :chunk]), dot(nm, w[:, chunk : 2 * chunk])
        d_hidden = dot(dy, w[:, 2 * chunk :])
        sigma = jax.nn.sigmoid(gate)
        silu = gate * sigma
        hidden.append((silu * upward).astype(BF16))
        d_gate = (d_hidden * upward * (sigma * (1.0 + gate * (1.0 - sigma)))).astype(BF16)
        d_up = (d_hidden * silu).astype(BF16)
        d_gate_up.append(jnp.concatenate([d_gate, d_up], axis=1))
        terms = jnp.concatenate([dot_tn(nm, d_gate_up[j]), dot_tn(dy, hidden[j])], axis=1)
        grads_mlp.append(layout.scatter(terms))

    def sum_chunks(part):
        total = part(0)
        for j in range(1, CHUNKS):
            total = total + part(j)
        return total

    d_normed_mid = team_scatter(
        lambda which: sum_chunks(lambda j: dot_nt(of_core(d_gate_up[j], which), w_mlp[j][:, : 2 * chunk]))
    )
    output = middle + team_scatter(
        lambda which: sum_chunks(lambda j: dot_nt(of_core(hidden[j], which), w_mlp[j][:, 2 * chunk :]))
    )
    d_middle = dy_own.astype(F32) + norm_input_gradient(mid_normed, mid_inverse, d_normed_mid * g_mlp)

    d_branch = team_gather(d_middle.astype(BF16))
    grad_out_sum = layout.scatter(dot_tn(d_branch, attended))
    d_attended = by_sequence(dot(d_branch, w_out).astype(BF16)).reshape(2, -1, heads, HEAD_SIZE)
    d_attended = jnp.moveaxis(d_attended, 2, 1)
    d_probs = pair(d_attended, values, "shqd,skd->shqk")
    row_dot = jnp.sum(probs * d_probs, axis=-1, keepdims=True)
    d_raw = (probs * (d_probs - row_dot) * scale).astype(BF16)
    d_queries = pair(d_raw, keys, "shqk,skd->sqhd").astype(BF16).astype(F32)
    d_keys = pair(d_raw, queries, "shqk,shqd->skd").astype(BF16)
    d_values = pair(probs_b, d_attended, "shqk,shqd->skd").astype(BF16)
    if sizes["xh"] > 1:
        d_keys = lax.psum_scatter(d_keys, "xh", scatter_dimension=1, tiled=True)
        d_values = lax.psum_scatter(d_values, "xh", scatter_dimension=1, tiled=True)
    d_q_rot = turn(d_queries, cosine, -sine)
    d_k_rot = turn(d_keys.astype(F32)[:, :, None], cosine, -sine)
    head_gains = jnp.stack(
        [jnp.sum(d_q_rot * q_normed, axis=(0, 1, 2)), jnp.sum(d_k_rot * k_normed, axis=(0, 1, 2))]
    )
    head_gains = all_sum(head_gains, sizes)
    d_q = norm_input_gradient(q_normed, q_inverse, d_q_rot * g_q)
    d_k = norm_input_gradient(k_normed, k_inverse, d_k_rot * g_k)
    d_projected = jnp.concatenate(
        [d_q.reshape(2, -1, q_width), d_k[:, :, 0], d_values.astype(F32)], axis=2
    ).astype(BF16)
    d_projected = by_core(d_projected)
    grad_qkv_sum = layout.scatter(dot_tn(normed_in, d_projected))
    d_normed_in = team_scatter(lambda which: dot_nt(of_core(d_projected, which), w_qkv))
    x_own = x_own.astype(F32)
    x_inverse = inverse_rms(x_own)
    token_grad = d_middle + norm_input_gradient(x_own * x_inverse, x_inverse, d_normed_in * g_attn)

    def to_owner(total):
        return exchange(total.astype(BF16).reshape(team, owned, -1)).astype(F32)

    def side_by_side(value):
        return jnp.moveaxis(value, 0, 1).reshape(owned, -1)

    back = to_owner(grad_qkv_sum)
    grad_qkv = jnp.concatenate(
        [
            side_by_side(back[:, :, :q_width]),
            side_by_side(back[:, :, q_width : q_width + HEAD_SIZE]),
            side_by_side(back[:, :, q_width + HEAD_SIZE :]),
        ],
        axis=1,
    )
    grad_out = side_by_side(to_owner(grad_out_sum))
    backs = jnp.stack([to_owner(g) for g in grads_mlp], axis=2)
    grad_gate_up = jnp.stack(
        [side_by_side(backs[..., i * chunk : (i + 1) * chunk].reshape(team, owned, -1)) for i in (0, 1)], axis=1
    )
    grad_down = side_by_side(backs[..., 2 * chunk :].reshape(team, owned, -1))
    grad_attn_gain = jnp.sum(grad_qkv * w_qkv_rows.astype(F32), axis=1) / attn_gain.astype(F32)
    grad_mlp_gain = jnp.sum(grad_gate_up * w_gate_up_rows.astype(F32), axis=(1, 2)) / mlp_gain.astype(F32)
    at = device_index(sizes) * small
    grad_q_gain = lax.dynamic_slice(head_gains[0], (at,), (small,))
    grad_k_gain = lax.dynamic_slice(head_gains[1], (at,), (small,))
    return (
        layout.natural(output.astype(BF16))[None],
        layout.natural(token_grad.astype(BF16))[None],
        grad_qkv,
        grad_out,
        grad_gate_up,
        grad_down,
        grad_attn_gain,
        grad_q_gain,
        grad_k_gain,
        grad_mlp_gain,
    )


def solution(mesh):
    dp, seq = mesh.shape["dp"], mesh.shape["seq"]
    fine = Mesh(mesh.devices.reshape(dp // 4, 2, 2, seq // 4, 2, 2), AXES)
    sizes = dict(fine.shape)
    dp_axes, seq_axes = ("zh", "zl", "y"), ("xh", "xl", "c")
    token, weight, vector = P(dp_axes, seq_axes, None), P(AXES, None), P(AXES)
    wide = P(AXES, None, None)

    def shards(*args):
        return layer(sizes, *args)

    return jax.shard_map(
        shards,
        mesh=fine,
        in_specs=(token, P(dp_axes, seq_axes), weight, weight, wide, weight, vector, vector, vector, vector, token),
        out_specs=(token, token, weight, weight, wide, weight, vector, vector, vector, vector),
        check_vma=False,
    )
```

```python
import math

import jax
import jax.numpy as jnp
from jax import lax
from jax.experimental import pallas as pl
from jax.experimental.pallas import tpu as pltpu
from jax.sharding import Mesh, PartitionSpec as P

QUERY_HEADS = 16
KEY_VALUE_HEADS = 8
HEAD_SIZE = 128
EPS = 1e-06
THETA = 1000000.0

F32 = jnp.float32
BF16 = jnp.bfloat16
SWAP = [(0, 1), (1, 0)]
DIAGONAL = [(0, 3), (1, 2), (2, 1), (3, 0)]
TEAM = ("zl", "xl", "c")
TEAM_SIZE = 8
AXES = ("zh", "zl", "y", "xh", "xl", "c")
CHUNKS = 3
VMEM_LIMIT = 48 << 20
WEIGHT = 100
FORWARD_STEPS = 4
BACK_STEPS = 2


def hold(*values):
    return lax.optimization_barrier(values)


class Layout:
    def __init__(self, sizes):
        self.zh, self.y, self.xh = sizes["zh"], sizes["y"], sizes["xh"]
        self.near = self.y * self.xh
        self.groups = self.zh * self.near

    def order(self):
        zh, y, xh = (lax.axis_index(name) for name in ("zh", "y", "xh"))
        places = []
        for j in range(self.y):
            for i in range(self.xh):
                for k in range(self.zh):
                    for low in range(2):
                        at = ((zh + k) % self.zh * 2 + low) * self.y + (y + j) % self.y
                        places.append(at * self.xh + (xh + i) % self.xh)
        return jnp.stack(places).astype(jnp.int32)

    def far_blocks(self, block):
        return [
            lax.ppermute(block, "zh", [((i + k) % self.zh, i) for i in range(self.zh)]) for k in range(1, self.zh)
        ]

    def shifted(self, n):
        j, i = n // self.xh, n % self.xh
        return [
            (a * self.xh + b, (a + j) % self.y * self.xh + (b + i) % self.xh)
            for a in range(self.y)
            for b in range(self.xh)
        ]

    def near_blocks(self, block):
        return [
            lax.ppermute(block, ("y", "xh"), [(b, a) for a, b in self.shifted(n)]) for n in range(1, self.near)
        ]

    def to_near(self, value, n):
        return lax.ppermute(value, ("y", "xh"), self.shifted(n))

    def to_far(self, value, k):
        return lax.ppermute(value, "zh", [(i, (i + k) % self.zh) for i in range(self.zh)])


def among_four(value):
    return lax.all_to_all(value, ("zl", "xl"), 0, 0, tiled=True)


def spread(copies):
    return among_four(copies).reshape(-1, copies.shape[-1])


def other_core(value):
    return lax.ppermute(value, "c", SWAP)


def exchange(value):
    return lax.all_to_all(value, TEAM, 0, 0, tiled=True)


def all_sum(value, sizes, axes):
    for axis in axes:
        total = value
        for k in range(1, sizes[axis]):
            total = total + lax.ppermute(value, axis, [((i + k) % sizes[axis], i) for i in range(sizes[axis])])
        value = total
    return value


def device_index(sizes):
    index = 0
    for axis in AXES:
        index = index * sizes[axis] + lax.axis_index(axis)
    return index


def dot(left, right):
    return lax.dot_general(left, right, (((1,), (0,)), ((), ())), preferred_element_type=F32)


def dot_nt(left, right):
    return lax.dot_general(left, right, (((1,), (1,)), ((), ())), preferred_element_type=F32)


def dot_tn(left, right):
    return lax.dot_general(left, right, (((0,), (0,)), ((), ())), preferred_element_type=F32)


def shape(dims, dtype):
    return jax.ShapeDtypeStruct(tuple(dims), dtype)


def run(kernel, grid, in_specs, out_specs, out_shape, args, flops=0):
    outs = jax.tree.leaves(out_shape)
    size = sum(math.prod(a.shape) * a.dtype.itemsize for a in list(args) + outs)
    return pl.pallas_call(
        kernel,
        grid=grid,
        in_specs=in_specs,
        out_specs=out_specs,
        out_shape=out_shape,
        compiler_params=pltpu.CompilerParams(
            vmem_limit_bytes=VMEM_LIMIT, dimension_semantics=("arbitrary",) * len(grid)
        ),
        cost_estimate=pl.CostEstimate(
            flops=WEIGHT * int(flops), bytes_accessed=WEIGHT * int(size), transcendentals=0
        ),
    )(*args)


def whole(array):
    return pl.BlockSpec(array.shape, lambda *_, n=len(array.shape): (0,) * n)


def inverse_rms(value):
    return lax.rsqrt(jnp.mean(value * value, axis=-1, keepdims=True) + EPS)


def norm_input_gradient(normed, inverse, e):
    return inverse * (e - normed * jnp.mean(e * normed, axis=-1, keepdims=True))


def reorder(values, places, inverse, copies=0):
    count = places.shape[0]
    width = values[0].shape[-1]
    cut = width // count
    if cut % 128:
        at = jnp.argsort(places) if inverse else places
        moved = [jnp.take(v.reshape(v.shape[:-1] + (count, cut)), at, axis=-2).reshape(v.shape) for v in values]
        if copies:
            side = jnp.concatenate(moved, axis=-1)
            return jnp.broadcast_to(side[None], (copies,) + side.shape)
        return moved
    if copies:
        outs = [shape((copies, values[0].shape[0], width * len(values)), values[0].dtype)]
    else:
        outs = [shape(v.shape, v.dtype) for v in values]

    def kernel(places_ref, *refs):
        for n, source in enumerate(refs[: len(values)]):
            for i in range(count):
                place = places_ref[i] * cut
                if copies:
                    value = source[:, pl.ds(pl.multiple_of(place, 128), cut)]
                    for copy in range(copies):
                        refs[-1][copy, :, n * width + i * cut : n * width + (i + 1) * cut] = value
                else:
                    moving = pl.ds(pl.multiple_of(place, 128), cut)
                    still = pl.ds(i * cut, cut)
                    target = refs[len(values) + n]
                    target[:, moving if inverse else still] = source[:, still if inverse else moving]

    size = sum(math.prod(a.shape) * a.dtype.itemsize for a in list(values) + outs)
    result = pl.pallas_call(
        kernel,
        grid_spec=pltpu.PrefetchScalarGridSpec(
            num_scalar_prefetch=1,
            grid=(1,),
            in_specs=[whole(v) for v in values],
            out_specs=[whole(o) for o in outs],
        ),
        out_shape=outs,
        compiler_params=pltpu.CompilerParams(vmem_limit_bytes=VMEM_LIMIT),
        cost_estimate=pl.CostEstimate(flops=0, bytes_accessed=WEIGHT * size, transcendentals=0),
    )(places, *values)
    return result[0] if copies else result


def pack_attention(w_qkv, w_out):
    owned, columns = w_qkv.shape
    q_cols, kv_cols = QUERY_HEADS * HEAD_SIZE, KEY_VALUE_HEADS * HEAD_SIZE
    q_width = q_cols // TEAM_SIZE

    def kernel(w_ref, w_out_ref, out_ref):
        for r in range(TEAM_SIZE):
            out_ref[r, :, :q_width] = w_ref[:, r * q_width : (r + 1) * q_width]
            for part in range(2):
                at = q_cols + part * kv_cols + r * HEAD_SIZE
                to = q_width + part * HEAD_SIZE
                out_ref[r, :, to : to + HEAD_SIZE] = w_ref[:, at : at + HEAD_SIZE]
            out_ref[r, :, columns // TEAM_SIZE :] = w_out_ref[:, r * q_width : (r + 1) * q_width]

    out = shape((TEAM_SIZE, owned, columns // TEAM_SIZE + q_width), BF16)
    return run(kernel, (1,), [whole(w_qkv), whole(w_out)], whole(out), out, [w_qkv, w_out])


def pack_chunks(w_gate_up, w_down, chunk):
    owned = w_down.shape[0]
    per = w_down.shape[1] // TEAM_SIZE

    def kernel(gate_up_ref, down_ref, target):
        for j in range(CHUNKS):
            to = 3 * chunk * j
            for r in range(TEAM_SIZE):
                at = slice(r * per + j * chunk, r * per + (j + 1) * chunk)
                target[r, :, to : to + chunk] = gate_up_ref[:, 0, at]
                target[r, :, to + chunk : to + 2 * chunk] = gate_up_ref[:, 1, at]
                target[r, :, to + 2 * chunk : to + 3 * chunk] = down_ref[:, at]

    out = shape((TEAM_SIZE, owned, 3 * chunk * CHUNKS), BF16)
    args = [w_gate_up, w_down]
    return run(kernel, (1,), [whole(a) for a in args], whole(out), out, args)


def unpack_chunks(back, w_gate_up, gain, chunk):
    owned = back.shape[1]
    per = CHUNKS * chunk

    def kernel(back_ref, w_ref, gain_ref, gate_up_ref, down_ref, out_ref):
        r = pl.program_id(0)
        total = jnp.zeros((owned, 1), F32)
        for j in range(CHUNKS):
            at, to = 3 * chunk * j, slice(j * chunk, (j + 1) * chunk)
            for part in range(2):
                value = back_ref[0, :, at + part * chunk : at + (part + 1) * chunk].astype(F32)
                gate_up_ref[:, part, to] = value
                total = total + jnp.sum(value * w_ref[:, part, to].astype(F32), axis=1, keepdims=True)
            down_ref[:, to] = back_ref[0, :, at + 2 * chunk : at + 3 * chunk].astype(F32)
        total = total / gain_ref[...]

        @pl.when(r == 0)
        def _():
            out_ref[...] = total

        @pl.when(r > 0)
        def _():
            out_ref[...] += total

    outs = [
        shape((owned, 2, TEAM_SIZE * per), F32),
        shape((owned, TEAM_SIZE * per), F32),
        shape((owned, 1), F32),
    ]
    wide = pl.BlockSpec((owned, 2, per), lambda r: (0, 0, r))
    return run(
        kernel,
        (TEAM_SIZE,),
        [pl.BlockSpec((1, owned, 3 * per), lambda r: (r, 0, 0)), wide, whole(gain)],
        [wide, pl.BlockSpec((owned, per), lambda r: (0, r)), whole(gain)],
        outs,
        [back, w_gate_up, gain],
    )


def unpack_attention(back, w_qkv, gain):
    owned, columns = w_qkv.shape
    q_cols, kv_cols = QUERY_HEADS * HEAD_SIZE, KEY_VALUE_HEADS * HEAD_SIZE
    q_width = q_cols // TEAM_SIZE

    def kernel(back_ref, w_ref, gain_ref, qkv_ref, out_weight_ref, out_ref):
        total = jnp.zeros((owned, 1), F32)
        for r in range(TEAM_SIZE):
            spans = [(0, r * q_width, q_width)]
            for part in range(2):
                spans.append((q_width + part * HEAD_SIZE, q_cols + part * kv_cols + r * HEAD_SIZE, HEAD_SIZE))
            for at, to, n in spans:
                value = back_ref[r, :, at : at + n].astype(F32)
                qkv_ref[:, to : to + n] = value
                total = total + jnp.sum(value * w_ref[:, to : to + n].astype(F32), axis=1, keepdims=True)
            out_weight_ref[:, r * q_width : (r + 1) * q_width] = back_ref[
                r, :, q_width + 2 * HEAD_SIZE :
            ].astype(F32)
        out_ref[...] = total / gain_ref[...]

    outs = [shape((owned, columns), F32), shape((owned, q_cols), F32), shape((owned, 1), F32)]
    args = [back, w_qkv, gain]
    return run(kernel, (1,), [whole(a) for a in args], [whole(o) for o in outs], outs, args)


def either(step, steps, refs, body):
    per = steps // 2

    @pl.when(step < per)
    def _():
        body(*[r[0] for r in refs])

    @pl.when(step >= per)
    def _():
        body(*[r[1] for r in refs])


def half_specs(side, width, steps):
    halves, column = side
    per = steps // 2
    rows = halves[0].shape[0]
    return [
        pl.BlockSpec((rows // per, width), lambda i: (jnp.minimum(i, per - 1), column)),
        pl.BlockSpec((rows // per, width), lambda i: (jnp.maximum(i - per, 0), column)),
    ]


def turned(value, cosine, sine):
    return value * cosine + pltpu.roll(value, HEAD_SIZE // 2, 1) * sine


def project(x_side, blocks, g_attn, g_q, g_k, cosine, sine, q_width):
    count = len(blocks)
    tokens, width = 2 * x_side[0][0].shape[0], count * blocks[0].shape[0]
    columns = q_width + 2 * HEAD_SIZE
    steps = 4
    rows = tokens // steps

    def kernel(x0, x1, *refs):
        w_refs = refs[:count]
        g_attn_ref, g_q_ref, g_k_ref, cos_ref, sin_ref, normed_ref, raw_ref, qkv_ref = refs[count:]

        def body(x_ref):
            x = x_ref[...].astype(F32)
            normed_ref[...] = (x * inverse_rms(x) * g_attn_ref[...]).astype(BF16)

        either(pl.program_id(0), steps, [(x0, x1)], body)
        per = width // count
        total = dot(normed_ref[:, :per], w_refs[0][...])
        for b in range(1, count):
            total = total + dot(normed_ref[:, b * per : (b + 1) * per], w_refs[b][...])
        raw_ref[...] = total[:, : q_width + HEAD_SIZE]
        cos, sin = cos_ref[...], sin_ref[...]
        for at in range(0, q_width + HEAD_SIZE, HEAD_SIZE):
            head = total[:, at : at + HEAD_SIZE]
            gain = g_q_ref[...] if at < q_width else g_k_ref[...]
            qkv_ref[:, at : at + HEAD_SIZE] = turned(head * inverse_rms(head) * gain, cos, sin).astype(BF16)
        qkv_ref[:, q_width + HEAD_SIZE :] = total[:, q_width + HEAD_SIZE :].astype(BF16)

    row = lambda n: pl.BlockSpec((rows, n), lambda i: (i, 0))
    outs = [
        shape((tokens, width), BF16),
        shape((tokens, q_width + HEAD_SIZE), F32),
        shape((tokens, columns), BF16),
    ]
    gains = [g_attn, g_q, g_k]
    return run(
        kernel,
        (steps,),
        half_specs(x_side, width, steps)
        + [pl.BlockSpec((w.shape[0], columns), lambda i: (0, 0)) for w in blocks]
        + [whole(g) for g in gains]
        + [row(HEAD_SIZE), row(HEAD_SIZE)],
        [row(o.shape[1]) for o in outs],
        outs,
        [*x_side[0], *blocks, *gains, cosine, sine],
        flops=2 * tokens * width * columns,
    )


def masked(q, k, allowed, scale):
    return jnp.where(allowed, dot_nt(q, k) * scale, -1e9)


def attention_specs(qkv, kv, kv_block, q_width, quarter, keys):
    parts = kv.shape[0]
    return [
        pl.BlockSpec((2, 1, quarter, q_width), lambda s: (0, s, 0, 0)),
        pl.BlockSpec((parts, 2, 1, quarter, 2 * HEAD_SIZE), lambda s: (0, 0, s, 0, kv_block)),
        pl.BlockSpec((1, 2 * quarter, 2), lambda s: (s, 0, 0)),
        pl.BlockSpec((1, 2, keys), lambda s: (s, 0, 0)),
    ]


def allowed_pairs(q_info, k_info):
    doc_q, index_q = q_info[:, 0:1], q_info[:, 1:2]
    doc_k, index_k = k_info[0:1, :], k_info[1:2, :]
    return (doc_q == doc_k) & (index_k <= index_q)


def attend(qkv, kv, kv_block, q_info, k_info, q_width):
    quarter = qkv.shape[2]
    keys = kv.shape[0] * 2 * quarter
    heads = q_width // HEAD_SIZE
    scale = HEAD_SIZE ** (-0.5)

    def kernel(q_ref, kv_ref, q_info_ref, k_info_ref, out_ref, lse_ref):
        allowed = allowed_pairs(q_info_ref[0], k_info_ref[0])
        pairs = kv_ref[...].reshape(keys, 2 * HEAD_SIZE)
        for h in range(heads):
            at = slice(h * HEAD_SIZE, (h + 1) * HEAD_SIZE)
            q = q_ref[:, 0, :, at].reshape(2 * quarter, HEAD_SIZE)
            scores = masked(q, pairs[:, :HEAD_SIZE], allowed, scale)
            peak = jnp.max(scores, axis=-1, keepdims=True)
            weights = jnp.exp(scores - peak)
            total = jnp.sum(weights, axis=-1, keepdims=True)
            probs = (weights * (1.0 / total)).astype(BF16)
            lse_ref[0, :, h : h + 1] = peak + jnp.log(total)
            attended = dot(probs, pairs[:, HEAD_SIZE:]).astype(BF16)
            out_ref[:, 0, :, at] = attended.reshape(2, quarter, HEAD_SIZE)

    outs = [shape((2, 2, quarter, q_width), BF16), shape((2, 2 * quarter, heads), F32)]
    return run(
        kernel,
        (2,),
        attention_specs(qkv, kv, kv_block, q_width, quarter, keys),
        [
            pl.BlockSpec((2, 1, quarter, q_width), lambda s: (0, s, 0, 0)),
            pl.BlockSpec((1, 2 * quarter, heads), lambda s: (s, 0, 0)),
        ],
        outs,
        [qkv, kv, q_info, k_info],
        flops=4 * 2 * heads * 2 * quarter * keys * HEAD_SIZE,
    )


def attend_back(qkv, kv, kv_block, q_info, k_info, q_width, lse, d_attended):
    quarter = qkv.shape[2]
    parts = kv.shape[0]
    keys = parts * 2 * quarter
    heads = q_width // HEAD_SIZE
    scale = HEAD_SIZE ** (-0.5)

    def kernel(q_ref, kv_ref, q_info_ref, k_info_ref, lse_ref, da_ref, dq_ref, dk_ref, dv_ref):
        allowed = allowed_pairs(q_info_ref[0], k_info_ref[0])
        pairs = kv_ref[...].reshape(keys, 2 * HEAD_SIZE)
        k, v = pairs[:, :HEAD_SIZE], pairs[:, HEAD_SIZE:]
        d_k = d_v = None
        for h in range(heads):
            at = slice(h * HEAD_SIZE, (h + 1) * HEAD_SIZE)
            q = q_ref[:, 0, :, at].reshape(2 * quarter, HEAD_SIZE)
            da = da_ref[:, 0, :, at].reshape(2 * quarter, HEAD_SIZE)
            probs = jnp.exp(masked(q, k, allowed, scale) - lse_ref[0, :, h : h + 1])
            d_probs = dot_nt(da, v)
            row_dot = jnp.sum(probs * d_probs, axis=-1, keepdims=True)
            d_raw = (probs * (d_probs - row_dot) * scale).astype(BF16)
            dq_ref[:, 0, :, at] = dot(d_raw, k).astype(BF16).reshape(2, quarter, HEAD_SIZE)
            k_term, v_term = dot_tn(d_raw, q), dot_tn(probs.astype(BF16), da)
            d_k = k_term if d_k is None else d_k + k_term
            d_v = v_term if d_v is None else d_v + v_term
        dk_ref[...] = d_k.astype(BF16).reshape(parts, 2, 1, quarter, HEAD_SIZE)
        dv_ref[...] = d_v.astype(BF16).reshape(parts, 2, 1, quarter, HEAD_SIZE)

    part = pl.BlockSpec((parts, 2, 1, quarter, HEAD_SIZE), lambda s: (0, 0, s, 0, 0))
    query = pl.BlockSpec((2, 1, quarter, q_width), lambda s: (0, s, 0, 0))
    part_shape = shape((parts, 2, 2, quarter, HEAD_SIZE), BF16)
    return run(
        kernel,
        (2,),
        attention_specs(qkv, kv, kv_block, q_width, quarter, keys)
        + [pl.BlockSpec((1, 2 * quarter, heads), lambda s: (s, 0, 0)), query],
        [query, part, part],
        [shape((2, 2, quarter, q_width), BF16), part_shape, part_shape],
        [qkv, kv, q_info, k_info, lse, d_attended],
        flops=10 * 2 * heads * 2 * quarter * keys * HEAD_SIZE,
    )


def project_back(raw, d_q, d_k, d_v, g_q, g_k, cosine, sine, q_width):
    tokens = raw.shape[0]
    steps = 4
    rows = tokens // steps

    def kernel(raw_ref, dq_ref, dk_ref, dv_ref, g_q_ref, g_k_ref, cos_ref, sin_ref, out_ref, gain_ref):
        cos, sin = cos_ref[...], sin_ref[...]
        gains = [jnp.zeros((1, HEAD_SIZE), F32), jnp.zeros((1, HEAD_SIZE), F32)]
        for at in range(0, q_width + HEAD_SIZE, HEAD_SIZE):
            is_key = int(at >= q_width)
            incoming = (dk_ref[...] if is_key else dq_ref[:, at : at + HEAD_SIZE]).astype(F32)
            back = turned(incoming, cos, -sin)
            head = raw_ref[:, at : at + HEAD_SIZE]
            inverse = inverse_rms(head)
            normed = head * inverse
            gains[is_key] = gains[is_key] + jnp.sum(back * normed, axis=0, keepdims=True)
            gain = g_k_ref[...] if is_key else g_q_ref[...]
            out_ref[:, at : at + HEAD_SIZE] = norm_input_gradient(normed, inverse, back * gain).astype(BF16)
        out_ref[:, q_width + HEAD_SIZE :] = dv_ref[...]

        @pl.when(pl.program_id(0) == 0)
        def _():
            gain_ref[...] = jnp.zeros_like(gain_ref)

        gain_ref[0:1, :] += gains[0]
        gain_ref[1:2, :] += gains[1]

    row = lambda n: pl.BlockSpec((rows, n), lambda i: (i, 0))
    outs = [shape((tokens, q_width + 2 * HEAD_SIZE), BF16), shape((8, HEAD_SIZE), F32)]
    args = [raw, d_q, d_k, d_v, g_q, g_k, cosine, sine]
    in_specs = [row(a.shape[1]) for a in args[:4]] + [whole(g_q), whole(g_k), row(HEAD_SIZE), row(HEAD_SIZE)]
    return run(kernel, (steps,), in_specs, [row(outs[0].shape[1]), whole(outs[1])], outs, args)


def back_rows(which, pairs, received=None):
    tokens = pairs[0][0].shape[0]
    half = tokens // 2
    steps = BACK_STEPS
    rows = half // steps
    count = len(pairs[0][1])
    per = pairs[0][1][0].shape[0]
    width = count * per
    left = [p[0] for p in pairs]
    blocks = [b for p in pairs for b in p[1]]

    def kernel(*refs):
        left_refs, w_refs = refs[: len(left)], refs[len(left) : len(left) + len(blocks)]
        out_ref = refs[-1]
        for b in range(count):
            at = slice(b * per, (b + 1) * per)
            total = None
            for i, l in enumerate(left_refs):
                term = dot_nt(l[...], w_refs[i * count + b][...])
                total = term if total is None else total + term
            if received is not None:
                total = total + refs[-2][:, at].astype(F32)
            out_ref[:, at] = total.astype(BF16)

    out = shape((half, width), BF16)
    out_spec = pl.BlockSpec((rows, width), lambda i: (i, 0))
    in_specs = [pl.BlockSpec((rows, p[0].shape[1]), lambda i: (which * steps + i, 0)) for p in pairs]
    for _, group, column, n in pairs:
        in_specs += [pl.BlockSpec((per, n), lambda i, column=column: (0, column)) for _ in group]
    args = left + blocks
    if received is not None:
        in_specs.append(out_spec)
        args = args + [received]
    flops = sum(2 * half * width * p[3] for p in pairs)
    return run(kernel, (steps,), in_specs, out_spec, out, args, flops=flops)


def feed_forward(nm, dy, blocks, chunk):
    count = len(blocks)
    per = blocks[0].shape[0]
    tokens, width = 2 * nm[0][0].shape[0], count * per
    steps = FORWARD_STEPS
    rows = tokens // steps

    def kernel(nm0, nm1, dy0, dy1, *refs):
        w_refs, (hidden_ref, d_ref) = refs[:count], refs[count:]

        def body(nm_ref, dy_ref):
            both = d_hidden = None
            for b in range(count):
                at = slice(b * per, (b + 1) * per)
                one = dot(nm_ref[:, at], w_refs[b][:, : 2 * chunk])
                two = dot(dy_ref[:, at], w_refs[b][:, 2 * chunk : 3 * chunk])
                both = one if both is None else both + one
                d_hidden = two if d_hidden is None else d_hidden + two
            gate, upward = both[:, :chunk], both[:, chunk:]
            sigma = 1.0 / (1.0 + jnp.exp(-gate))
            silu = gate * sigma
            hidden_ref[...] = (silu * upward).astype(BF16)
            d_ref[:, :chunk] = (d_hidden * upward * (sigma * (1.0 + gate * (1.0 - sigma)))).astype(BF16)
            d_ref[:, chunk:] = (d_hidden * silu).astype(BF16)

        either(pl.program_id(0), steps, [(nm0, nm1), (dy0, dy1)], body)

    row = lambda n: pl.BlockSpec((rows, n), lambda i: (i, 0))
    outs = [shape((tokens, chunk), BF16), shape((tokens, 2 * chunk), BF16)]
    w_specs = [pl.BlockSpec((per, 3 * chunk), lambda i: (0, 0)) for _ in blocks]
    return run(
        kernel,
        (steps,),
        half_specs(nm, width, steps) + half_specs(dy, width, steps) + w_specs,
        [row(chunk), row(2 * chunk)],
        outs,
        [*nm[0], *dy[0], *blocks],
        flops=2 * tokens * width * 3 * chunk,
    )


def weight_terms(layout, width, n, pairs, received=None):
    tile = width // layout.groups
    cuts = [p[1].shape[1] for p in pairs]
    columns = sum(cuts)
    tokens = pairs[0][1].shape[0]
    left = [(a, p[0][1]) for p in pairs for a in p[0][0]]

    def kernel(*refs):
        refs = list(refs)
        l_refs = [[refs.pop(0) for _ in p[0][0]] for p in pairs]
        d_refs = [refs.pop(0) for _ in pairs]
        in_refs = [refs.pop(0) for _ in (received or ())]
        column = 0
        for sources, d_ref, cut in zip(l_refs, d_refs, cuts):
            total, at = None, 0
            for source in sources:
                count = source.shape[0]
                term = dot_tn(source[...], d_ref[at : at + count, :])
                total = term if total is None else total + term
                at += count
            span = slice(column, column + cut)
            column += cut
            for r in in_refs:
                total = total + r[:, span].astype(F32)
            if received is None:
                refs[0][:, span] = total.astype(BF16)
                continue
            for k, out_ref in enumerate(refs):

                @pl.when(pl.program_id(0) == k)
                def _(out_ref=out_ref, total=total, span=span):
                    out_ref[:, span] = total.astype(BF16)

    in_specs = [
        pl.BlockSpec((a.shape[0], tile), lambda k, column=column: (0, column * layout.groups + n * layout.zh + k))
        for a, column in left
    ]
    in_specs += [whole(p[1]) for p in pairs]
    args = [a for a, _ in left] + [p[1] for p in pairs]
    row = pl.BlockSpec((tile, columns), lambda k: (k, 0))
    if received is None:
        outs, out_specs = shape((layout.zh * tile, columns), BF16), row
    else:
        args += received
        in_specs += [row] * len(received)
        outs = [shape((tile, columns), BF16)] * layout.zh
        out_specs = [whole(o) for o in outs]
    return run(
        kernel, (layout.zh,), in_specs, out_specs, outs, args, flops=2 * tokens * layout.zh * tile * columns
    )


def one_copy(value, width, column=0):
    if len(value.shape) == 2:
        return whole(value)
    return pl.BlockSpec((1, value.shape[1], width), lambda *_: (0, 0, column))


def rows_of(ref):
    return ref[...].reshape(ref.shape[-2:])


def middle_step(parts, x, gain):
    rows, width = x.shape[-2], gain.shape[1]

    def kernel(parts_ref, x_ref, gain_ref, middle_ref, nm_ref):
        middle = rows_of(x_ref).astype(F32)
        for i in range(4):
            middle = middle + parts_ref[i].astype(F32)
        middle_ref[...] = middle
        nm = (middle * inverse_rms(middle) * gain_ref[...]).astype(BF16)
        for i in range(4):
            nm_ref[i] = nm

    outs = [shape((rows, width), F32), shape((4, rows, width), BF16)]
    args = [parts, x, gain]
    return run(kernel, (1,), [whole(parts), one_copy(x, width), whole(gain)], [whole(o) for o in outs], outs, args)


def norm_back_step(parts, base, passed, passed_column, gain, copies):
    rows, width = base.shape[-2], gain.shape[1]

    def kernel(parts_ref, base_ref, passed_ref, gain_ref, *out_refs):
        total = parts_ref[0].astype(F32)
        for i in range(1, 4):
            total = total + parts_ref[i].astype(F32)
        value = rows_of(base_ref).astype(F32)
        inverse = inverse_rms(value)
        result = rows_of(passed_ref).astype(F32) + norm_input_gradient(
            value * inverse, inverse, total * gain_ref[...]
        )
        rounded = result.astype(BF16)
        if copies == 1:
            out_refs[0][...] = rounded
            return
        out_refs[0][...] = result
        for i in range(copies):
            out_refs[1][i] = rounded

    outs = [shape((rows, width), F32), shape((copies, rows, width), BF16)]
    if copies == 1:
        outs = [shape((rows, width), BF16)]
    args = [parts, base, passed, gain]
    return run(kernel, (1,), [whole(parts), one_copy(base, width), one_copy(passed, width, passed_column), whole(gain)], [whole(o) for o in outs], outs, args)


def plain_sum(parts, base):
    def kernel(parts_ref, base_ref, out_ref):
        total = base_ref[...]
        for i in range(4):
            total = total + parts_ref[i].astype(F32)
        out_ref[...] = total.astype(BF16)

    out = shape(base.shape, BF16)
    return run(kernel, (1,), [whole(parts), whole(base)], whole(out), out, [parts, base])


def attended_gradient(d_branch, blocks, column, n):
    count = len(blocks)
    per = blocks[0].shape[0]
    tokens, width = 2 * d_branch[0][0].shape[0], count * per
    steps = 4

    def kernel(d0, d1, *refs):
        w_refs, out_ref = refs[:count], refs[count]

        def body(d_ref):
            total = dot(d_ref[:, :per], w_refs[0][...])
            for b in range(1, count):
                total = total + dot(d_ref[:, b * per : (b + 1) * per], w_refs[b][...])
            out_ref[...] = total.astype(BF16)

        either(pl.program_id(0), steps, [(d0, d1)], body)

    out = shape((tokens, n), BF16)
    return run(
        kernel,
        (steps,),
        half_specs(d_branch, width, steps) + [pl.BlockSpec((per, n), lambda i: (0, column)) for _ in blocks],
        pl.BlockSpec((tokens // steps, n), lambda i: (i, 0)),
        out,
        [*d_branch[0], *blocks],
        flops=2 * tokens * width * n,
    )


def layer(
    sizes,
    tokens,
    doc_ids,
    w_qkv_rows,
    w_out_rows,
    w_gate_up_rows,
    w_down_rows,
    attn_gain,
    q_gain,
    k_gain,
    mlp_gain,
    out_grad,
):
    layout = Layout(sizes)
    rows = tokens.shape[1]
    width = tokens.shape[2]
    owned = w_qkv_rows.shape[0]
    devices = width // owned
    q_width = QUERY_HEADS // TEAM_SIZE * HEAD_SIZE
    chunk = w_down_rows.shape[1] // TEAM_SIZE // CHUNKS
    small = q_gain.shape[0]
    places = layout.order()

    def arrived(value):
        return value.reshape(TEAM_SIZE * owned, -1)

    def gathered(near, far):
        columns = [near] + far
        return [columns[k][n] for n in range(layout.near) for k in range(layout.zh)]

    def with_near(block):
        return [block] + layout.near_blocks(block)

    copies = reorder([tokens[0], out_grad[0]], places, False, 4)
    part_attn = arrived(exchange(pack_attention(w_qkv_rows, w_out_rows)))
    send_mlp = pack_chunks(w_gate_up_rows, w_down_rows, chunk)
    mine = jnp.concatenate([attn_gain, mlp_gain, q_gain, k_gain, doc_ids.reshape(-1).astype(BF16)])[None]
    table = jnp.zeros((devices, mine.shape[1]), BF16)
    table = lax.dynamic_update_slice(table, mine, (device_index(sizes), 0))
    table = all_sum(table, sizes, ("c", "xl", "zl"))
    part_attn, copies, send_mlp, table = hold(part_attn, copies, send_mlp, table)

    attn_near, attn_far = with_near(part_attn), layout.far_blocks(part_attn)
    rest = arrived(exchange(send_mlp))
    table = all_sum(table, sizes, ("y", "xh", "zh"))
    attn_near, attn_far, rest, table, copies = hold(attn_near, attn_far, rest, table, copies)
    parts = [rest[:, j * 3 * chunk : (j + 1) * 3 * chunk] for j in range(CHUNKS)]

    near, far = {}, {}
    w_attn = gathered(attn_near, [with_near(b) for b in attn_far])
    near[0], far[0] = with_near(parts[0]), layout.far_blocks(parts[0])
    token_half = spread(copies)

    table = table.astype(F32)
    natural = jnp.stack([table[:, :owned].reshape(width), table[:, owned : 2 * owned].reshape(width)])
    count = places.shape[0]
    g_attn, g_mlp = jnp.split(
        jnp.take(natural.reshape(2, count, -1), places, axis=1).reshape(2, width), 2, axis=0
    )
    g_q = table[:, 2 * owned : 2 * owned + small].reshape(1, -1)
    g_k = table[:, 2 * owned + small : 2 * owned + 2 * small].reshape(1, -1)
    docs = table[:, 2 * owned + 2 * small :].astype(jnp.int32)
    docs = docs.reshape(sizes["zh"], 2, sizes["y"], sizes["xh"], 2, 2, rows)
    docs = lax.dynamic_slice(
        docs, (lax.axis_index("zh"), 0, lax.axis_index("y"), 0, 0, 0, 0), (1, 2, 1) + docs.shape[3:]
    )[0, :, 0]
    docs = jnp.moveaxis(jnp.roll(docs, -lax.axis_index("c"), axis=3), 3, 2)
    place = (
        jnp.arange(sizes["xh"])[:, None, None] * 4
        + jnp.arange(2)[None, None, :] * 2
        + (lax.axis_index("c") ^ jnp.arange(2))[None, :, None]
    )
    index = (place[..., None] * rows + jnp.arange(rows)).astype(jnp.int32)
    index = jnp.broadcast_to(index[None], docs.shape)
    k_info = jnp.stack([docs.reshape(2, -1), index.reshape(2, -1)], axis=1)
    q_info = lax.dynamic_slice(
        jnp.stack([docs, index], axis=-1), (0, lax.axis_index("xh"), 0, 0, 0, 0), (2, 1, 2, 2, rows, 2)
    ).reshape(2, -1, 2)
    doc_start = jnp.sum((k_info[:, 0, None, :] < q_info[:, :, 0, None]).astype(jnp.int32), axis=2)
    position = (q_info[:, :, 1] - doc_start).astype(F32)
    position = jnp.moveaxis(position.reshape(2, 2, 2 * rows), 1, 0).reshape(-1, 1)
    half_head = HEAD_SIZE // 2
    freqs = jnp.exp(jnp.arange(half_head).astype(F32) * (-math.log(THETA) / half_head))
    angle = position * freqs
    cosine, sine = jnp.cos(angle), jnp.sin(angle)
    cosine = jnp.concatenate([cosine, cosine], axis=1)
    sine = jnp.concatenate([-sine, sine], axis=1)
    token_half, w_attn, cosine, sine, g_attn, g_mlp, k_info, q_info, near[0], far[0], parts = hold(
        token_half, w_attn, cosine, sine, g_attn, g_mlp, k_info, q_info, near[0], far[0], parts
    )

    near[1], far[1] = with_near(parts[1]), layout.far_blocks(parts[1])
    weights = [gathered(near[0], [with_near(b) for b in far[0]])]
    team = [token_half, other_core(token_half)]
    x_side, dy = (team, 0), (team, 1)
    normed_in, raw, qkv = project(x_side, w_attn, g_attn, g_q, g_k, cosine, sine, q_width)
    qkv4 = qkv.reshape(2, 2, 2 * rows, -1)
    if sizes["xh"] == 1:
        kv, kv_block = qkv4[None], 1
    else:
        kv, kv_block = lax.all_gather(qkv4[..., q_width:], "xh", axis=0, tiled=False), 0
    attended, lse = attend(qkv4, kv, kv_block, q_info, k_info, q_width)
    attended = attended.reshape(-1, q_width)
    out_column = (q_width + 2 * HEAD_SIZE) // q_width
    out_pair = [(attended, w_attn, out_column, q_width)]
    received = other_core(back_rows(1, out_pair))
    branch = among_four(back_rows(0, out_pair, received).reshape(4, rows, width))
    middle, nm_copies = middle_step(branch, copies, g_mlp)
    nm_copies, weights[0], near[1], far[1], parts[2] = hold(nm_copies, weights[0], near[1], far[1], parts[2])

    near[2], far[2] = with_near(parts[2]), layout.far_blocks(parts[2])
    weights.append(gathered(near[1], [with_near(b) for b in far[1]]))
    nm_half = spread(nm_copies)
    nm_half, weights[1], near[2], far[2] = hold(nm_half, weights[1], near[2], far[2])

    def near_send(*pairs):
        return [weight_terms(layout, width, n, pairs) for n in range(1, layout.near)]

    def to_near(terms):
        return [layout.to_near(t, n + 1) for n, t in enumerate(terms)]

    def own_terms(received, *pairs):
        return weight_terms(layout, width, 0, pairs, received=received)

    def to_far(sums):
        return [layout.to_far(sums[k], k) for k in range(1, layout.zh)]

    def far_total(own, received):
        total = own.astype(F32)
        for r in received:
            total = total + r.astype(F32)
        return total.astype(BF16).reshape(TEAM_SIZE, owned, -1)

    weights.append(gathered(near[2], [with_near(b) for b in far[2]]))
    nm = ([nm_half, other_core(nm_half)], 0)
    hidden, d_gate_up, mlp, going, arriving, sums, arrived_far = [], [], [], {}, {}, {}, {}

    def chunk_step(j):
        h, d = feed_forward(nm, dy, weights[j], chunk)
        hidden.append(h)
        d_gate_up.append(d)
        mlp.append([(nm, d), (dy, h)])

    chunk_step(0)
    chunk_step(1)
    going[0] = near_send(*mlp[0])
    weights[2], going[0], d_gate_up[1] = hold(weights[2], going[0], d_gate_up[1])

    arriving[0] = to_near(going[0])
    chunk_step(2)
    mid_pairs = [(d_gate_up[j], weights[j], 0, 2 * chunk) for j in range(CHUNKS)]
    out_pairs = [(hidden[j], weights[j], 2, chunk) for j in range(CHUNKS)]
    received = other_core(back_rows(1, mid_pairs))
    terms = among_four(back_rows(0, mid_pairs, received).reshape(4, rows, width))
    going[1] = near_send(*mlp[1])
    d_middle, d_copies = norm_back_step(terms, middle, copies, 1, g_mlp, 4)
    d_copies, going[1], arriving[0] = hold(d_copies, going[1], arriving[0])

    sums[0] = own_terms(arriving[0], *mlp[0])
    arrived_far[0] = to_far(sums[0])
    arriving[1] = to_near(going[1])
    d_half = spread(d_copies)
    going[2] = near_send(*mlp[2])
    received = other_core(back_rows(1, out_pairs))
    out_total = back_rows(0, out_pairs, received)
    d_half, arriving[1], arrived_far[0], going[2], out_total = hold(
        d_half, arriving[1], arrived_far[0], going[2], out_total
    )

    sums[1] = own_terms(arriving[1], *mlp[1])
    arrived_far[1] = to_far(sums[1])
    arriving[2] = to_near(going[2])
    out_total = among_four(out_total.reshape(4, rows, width))
    d_branch = ([d_half, other_core(d_half)], 0)
    d_attended = attended_gradient(d_branch, w_attn, out_column, q_width)
    d_attended = d_attended.reshape(2, 2, 2 * rows, q_width)
    d_q, d_k, d_v = attend_back(qkv4, kv, kv_block, q_info, k_info, q_width, lse, d_attended)
    if sizes["xh"] > 1:
        d_k = lax.psum_scatter(d_k, "xh", scatter_dimension=0, tiled=True)
        d_v = lax.psum_scatter(d_v, "xh", scatter_dimension=0, tiled=True)
    d_projected, head_gains = project_back(
        raw,
        d_q.reshape(-1, q_width),
        d_k.reshape(-1, HEAD_SIZE),
        d_v.reshape(-1, HEAD_SIZE),
        g_q,
        g_k,
        cosine,
        sine,
        q_width,
    )
    in_pair = [(d_projected, w_attn, 0, q_width + 2 * HEAD_SIZE)]
    received = other_core(back_rows(1, in_pair))
    terms = back_rows(0, in_pair, received)
    attention = [(([normed_in], 0), d_projected), (d_branch, attended)]
    going[3] = near_send(*attention)
    terms, arriving[2], arrived_far[1], out_total, going[3] = hold(
        terms, arriving[2], arrived_far[1], out_total, going[3]
    )

    arriving[3] = to_near(going[3])
    sums[2] = own_terms(arriving[2], *mlp[2])
    arrived_far[2] = to_far(sums[2])
    terms = among_four(terms.reshape(4, rows, width))
    output = plain_sum(out_total, middle)
    head_gains = all_sum(head_gains, sizes, ("c", "xl"))
    terms, arriving[3], arrived_far[2], head_gains = hold(terms, arriving[3], arrived_far[2], head_gains)

    sums[3] = own_terms(arriving[3], *attention)
    arrived_far[3] = to_far(sums[3])
    back = jnp.concatenate([far_total(sums[j][0], arrived_far[j]) for j in range(CHUNKS)], axis=2)
    back = exchange(back)
    (token_grad,) = norm_back_step(terms, copies, d_middle, 0, g_attn, 1)
    token_grad, output = reorder([token_grad, output], places, True)
    head_gains = all_sum(head_gains, sizes, ("zl", "y"))
    back, arrived_far[3], head_gains = hold(back, arrived_far[3], head_gains)

    last = exchange(far_total(sums[3][0], arrived_far[3]))
    head_gains = all_sum(head_gains, sizes, ("xh", "zh"))
    grad_gate_up, grad_down, grad_mlp_gain = unpack_chunks(
        back, w_gate_up_rows, mlp_gain.astype(F32).reshape(owned, 1), chunk
    )
    grad_qkv, grad_out, grad_attn_gain = unpack_attention(
        last, w_qkv_rows, attn_gain.astype(F32).reshape(owned, 1)
    )
    at = device_index(sizes) * small
    grad_q_gain = lax.dynamic_slice(head_gains[0], (at,), (small,))
    grad_k_gain = lax.dynamic_slice(head_gains[1], (at,), (small,))
    return (
        output[None],
        token_grad[None],
        grad_qkv,
        grad_out,
        grad_gate_up,
        grad_down,
        grad_attn_gain.reshape(owned),
        grad_q_gain,
        grad_k_gain,
        grad_mlp_gain.reshape(owned),
    )


def solution(mesh):
    dp, seq = mesh.shape["dp"], mesh.shape["seq"]
    fine = Mesh(mesh.devices.reshape(dp // 4, 2, 2, seq // 4, 2, 2), AXES)
    sizes = dict(fine.shape)
    dp_axes, seq_axes = ("zh", "zl", "y"), ("xh", "xl", "c")
    token, weight, vector = P(dp_axes, seq_axes, None), P(AXES, None), P(AXES)
    wide = P(AXES, None, None)

    def shards(*args):
        return layer(sizes, *args)

    return jax.shard_map(
        shards,
        mesh=fine,
        in_specs=(token, P(dp_axes, seq_axes), weight, weight, wide, weight, vector, vector, vector, vector, token),
        out_specs=(token, token, weight, weight, wide, weight, vector, vector, vector, vector),
        check_vma=False,
    )
```

```python
import math

import jax
import jax.numpy as jnp
from jax import lax
from jax.experimental import pallas as pl
from jax.experimental.pallas import tpu as pltpu
from jax.sharding import Mesh, PartitionSpec as P

QUERY_HEADS = 16
KEY_VALUE_HEADS = 8
HEAD_SIZE = 128
EPS = 1e-06
THETA = 1000000.0

F32 = jnp.float32
BF16 = jnp.bfloat16
SWAP = [(0, 1), (1, 0)]
TEAM = ("zl", "xl", "c")
TEAM_SIZE = 8
AXES = ("zh", "zl", "y", "xh", "xl", "c")
CHUNKS = 3
VMEM_LIMIT = 32 << 20
WEIGHT = 100
FORWARD_STEPS = 4
BACK_STEPS = 2


def hold(*values):
    return lax.optimization_barrier(values)


class Layout:
    def __init__(self, sizes):
        self.zh, self.y, self.xh = sizes["zh"], sizes["y"], sizes["xh"]
        self.near = self.y * self.xh
        self.groups = self.zh * self.near

    def order(self):
        zh, y, xh = (lax.axis_index(name) for name in ("zh", "y", "xh"))
        places = []
        for j in range(self.y):
            for i in range(self.xh):
                for k in range(self.zh):
                    for low in range(2):
                        at = ((zh + k) % self.zh * 2 + low) * self.y + (y + j) % self.y
                        places.append(at * self.xh + (xh + i) % self.xh)
        return jnp.stack(places).astype(jnp.int32)

    def far_blocks(self, block):
        return [
            lax.ppermute(block, "zh", [((i + k) % self.zh, i) for i in range(self.zh)]) for k in range(1, self.zh)
        ]

    def shifted(self, n):
        j, i = n // self.xh, n % self.xh
        return [
            (a * self.xh + b, (a + j) % self.y * self.xh + (b + i) % self.xh)
            for a in range(self.y)
            for b in range(self.xh)
        ]

    def near_blocks(self, block):
        return [
            lax.ppermute(block, ("y", "xh"), [(b, a) for a, b in self.shifted(n)]) for n in range(1, self.near)
        ]

    def to_near(self, value, n):
        return lax.ppermute(value, ("y", "xh"), self.shifted(n))

    def to_far(self, value, k):
        return lax.ppermute(value, "zh", [(i, (i + k) % self.zh) for i in range(self.zh)])


def among_four(value):
    return lax.all_to_all(value, ("zl", "xl"), 0, 0, tiled=True)


def spread(copies):
    return among_four(copies).reshape(-1, copies.shape[-1])


def other_core(value):
    return lax.ppermute(value, "c", SWAP)


def other_x(value):
    return lax.ppermute(value, "xl", SWAP)


def other_z(value):
    return lax.ppermute(value, "zl", SWAP)


def exchange(value):
    return lax.all_to_all(value, TEAM, 0, 0, tiled=True)


def all_sum(value, sizes, axes):
    for axis in axes:
        total = value
        for k in range(1, sizes[axis]):
            total = total + lax.ppermute(value, axis, [((i + k) % sizes[axis], i) for i in range(sizes[axis])])
        value = total
    return value


def device_index(sizes):
    index = 0
    for axis in AXES:
        index = index * sizes[axis] + lax.axis_index(axis)
    return index


def dot(left, right):
    return lax.dot_general(left, right, (((1,), (0,)), ((), ())), preferred_element_type=F32)


def dot_nt(left, right):
    return lax.dot_general(left, right, (((1,), (1,)), ((), ())), preferred_element_type=F32)


def dot_tn(left, right):
    return lax.dot_general(left, right, (((0,), (0,)), ((), ())), preferred_element_type=F32)


def joined(values, axis=0):
    return values[0] if len(values) == 1 else jnp.concatenate(values, axis=axis)


def shape(dims, dtype):
    return jax.ShapeDtypeStruct(tuple(dims), dtype)


def run(kernel, grid, in_specs, out_specs, out_shape, args, flops=0):
    outs = jax.tree.leaves(out_shape)
    size = sum(math.prod(a.shape) * a.dtype.itemsize for a in list(args) + outs)
    return pl.pallas_call(
        kernel,
        grid=grid,
        in_specs=in_specs,
        out_specs=out_specs,
        out_shape=out_shape,
        compiler_params=pltpu.CompilerParams(
            vmem_limit_bytes=VMEM_LIMIT, dimension_semantics=("arbitrary",) * len(grid)
        ),
        cost_estimate=pl.CostEstimate(
            flops=WEIGHT * int(flops), bytes_accessed=WEIGHT * int(size), transcendentals=0
        ),
    )(*args)


def whole(array):
    return pl.BlockSpec(array.shape, lambda *_, n=len(array.shape): (0,) * n)


def inverse_rms(value):
    return lax.rsqrt(jnp.mean(value * value, axis=-1, keepdims=True) + EPS)


def norm_input_gradient(normed, inverse, e):
    return inverse * (e - normed * jnp.mean(e * normed, axis=-1, keepdims=True))


def reorder(values, places, inverse, copies=0):
    count = places.shape[0]
    width = values[0].shape[-1]
    cut = width // count
    if cut % 128:
        at = jnp.argsort(places) if inverse else places
        moved = [jnp.take(v.reshape(v.shape[:-1] + (count, cut)), at, axis=-2).reshape(v.shape) for v in values]
        if copies:
            moved = [jnp.broadcast_to(v[None], (copies,) + v.shape) for v in moved]
        return moved
    outs = [shape(((copies,) if copies else ()) + v.shape, v.dtype) for v in values]

    def kernel(places_ref, *refs):
        for source, target in zip(refs[: len(values)], refs[len(values) :]):
            for i in range(count):
                moving = pl.ds(pl.multiple_of(places_ref[i] * cut, 128), cut)
                still = pl.ds(i * cut, cut)
                if copies:
                    value = source[:, moving]
                    for copy in range(copies):
                        target[copy, :, still] = value
                else:
                    target[:, moving if inverse else still] = source[:, still if inverse else moving]

    size = sum(math.prod(a.shape) * a.dtype.itemsize for a in list(values) + outs)
    return pl.pallas_call(
        kernel,
        grid_spec=pltpu.PrefetchScalarGridSpec(
            num_scalar_prefetch=1,
            grid=(1,),
            in_specs=[whole(v) for v in values],
            out_specs=[whole(o) for o in outs],
        ),
        out_shape=outs,
        compiler_params=pltpu.CompilerParams(vmem_limit_bytes=VMEM_LIMIT),
        cost_estimate=pl.CostEstimate(flops=0, bytes_accessed=WEIGHT * size, transcendentals=0),
    )(places, *values)


def pack_attention(w_qkv, w_out):
    owned, columns = w_qkv.shape
    q_cols, kv_cols = QUERY_HEADS * HEAD_SIZE, KEY_VALUE_HEADS * HEAD_SIZE
    q_width = q_cols // TEAM_SIZE

    def kernel(w_ref, w_out_ref, out_ref):
        for r in range(TEAM_SIZE):
            out_ref[r, :, :q_width] = w_ref[:, r * q_width : (r + 1) * q_width]
            for part in range(2):
                at = q_cols + part * kv_cols + r * HEAD_SIZE
                to = q_width + part * HEAD_SIZE
                out_ref[r, :, to : to + HEAD_SIZE] = w_ref[:, at : at + HEAD_SIZE]
            out_ref[r, :, columns // TEAM_SIZE :] = w_out_ref[:, r * q_width : (r + 1) * q_width]

    out = shape((TEAM_SIZE, owned, columns // TEAM_SIZE + q_width), BF16)
    return run(kernel, (1,), [whole(w_qkv), whole(w_out)], whole(out), out, [w_qkv, w_out])


def pack_chunks(w_gate_up, w_down, chunk):
    owned = w_down.shape[0]
    per = w_down.shape[1] // TEAM_SIZE

    def kernel(gate_up_ref, down_ref, *targets):
        for j in range(CHUNKS):
            target = targets[min(j, 1)]
            to = 3 * chunk * max(j - 1, 0)
            for r in range(TEAM_SIZE):
                at = slice(r * per + j * chunk, r * per + (j + 1) * chunk)
                target[r, :, to : to + chunk] = gate_up_ref[:, 0, at]
                target[r, :, to + chunk : to + 2 * chunk] = gate_up_ref[:, 1, at]
                target[r, :, to + 2 * chunk : to + 3 * chunk] = down_ref[:, at]

    outs = [shape((TEAM_SIZE, owned, 3 * chunk * n), BF16) for n in (1, CHUNKS - 1)]
    args = [w_gate_up, w_down]
    return run(kernel, (1,), [whole(a) for a in args], [whole(o) for o in outs], outs, args)


def unpack_chunks(first, rest, w_gate_up, gain, chunk):
    owned = first.shape[1]
    per = CHUNKS * chunk

    def kernel(first_ref, rest_ref, w_ref, gain_ref, gate_up_ref, down_ref, out_ref):
        r = pl.program_id(0)
        total = jnp.zeros((owned, 1), F32)
        for j in range(CHUNKS):
            back_ref = rest_ref if j else first_ref
            at, to = 3 * chunk * max(j - 1, 0), slice(j * chunk, (j + 1) * chunk)
            for part in range(2):
                value = back_ref[0, :, at + part * chunk : at + (part + 1) * chunk].astype(F32)
                gate_up_ref[:, part, to] = value
                total = total + jnp.sum(value * w_ref[:, part, to].astype(F32), axis=1, keepdims=True)
            down_ref[:, to] = back_ref[0, :, at + 2 * chunk : at + 3 * chunk].astype(F32)
        total = total / gain_ref[...]

        @pl.when(r == 0)
        def _():
            out_ref[...] = total

        @pl.when(r > 0)
        def _():
            out_ref[...] += total

    outs = [
        shape((owned, 2, TEAM_SIZE * per), F32),
        shape((owned, TEAM_SIZE * per), F32),
        shape((owned, 1), F32),
    ]
    wide = pl.BlockSpec((owned, 2, per), lambda r: (0, 0, r))
    return run(
        kernel,
        (TEAM_SIZE,),
        [pl.BlockSpec((1,) + b.shape[1:], lambda r: (r, 0, 0)) for b in (first, rest)] + [wide, whole(gain)],
        [wide, pl.BlockSpec((owned, per), lambda r: (0, r)), whole(gain)],
        outs,
        [first, rest, w_gate_up, gain],
    )


def unpack_attention(back, w_qkv, gain):
    owned, columns = w_qkv.shape
    q_cols, kv_cols = QUERY_HEADS * HEAD_SIZE, KEY_VALUE_HEADS * HEAD_SIZE
    q_width = q_cols // TEAM_SIZE

    def kernel(back_ref, w_ref, gain_ref, qkv_ref, out_weight_ref, out_ref):
        total = jnp.zeros((owned, 1), F32)
        for r in range(TEAM_SIZE):
            spans = [(0, r * q_width, q_width)]
            for part in range(2):
                spans.append((q_width + part * HEAD_SIZE, q_cols + part * kv_cols + r * HEAD_SIZE, HEAD_SIZE))
            for at, to, n in spans:
                value = back_ref[r, :, at : at + n].astype(F32)
                qkv_ref[:, to : to + n] = value
                total = total + jnp.sum(value * w_ref[:, to : to + n].astype(F32), axis=1, keepdims=True)
            out_weight_ref[:, r * q_width : (r + 1) * q_width] = back_ref[
                r, :, q_width + 2 * HEAD_SIZE :
            ].astype(F32)
        out_ref[...] = total / gain_ref[...]

    outs = [shape((owned, columns), F32), shape((owned, q_cols), F32), shape((owned, 1), F32)]
    args = [back, w_qkv, gain]
    return run(kernel, (1,), [whole(a) for a in args], [whole(o) for o in outs], outs, args)


def either(step, steps, refs, body):
    per = steps // 2

    @pl.when(step < per)
    def _():
        body(*[r[0] for r in refs])

    @pl.when(step >= per)
    def _():
        body(*[r[1] for r in refs])


def half_specs(side, width, steps):
    halves, column = side
    per = steps // 2
    rows = halves[0].shape[0]
    return [
        pl.BlockSpec((rows // per, width), lambda i: (jnp.minimum(i, per - 1), column)),
        pl.BlockSpec((rows // per, width), lambda i: (jnp.maximum(i - per, 0), column)),
    ]


def turned(value, cosine, sine):
    return value * cosine + pltpu.roll(value, HEAD_SIZE // 2, 1) * sine


def project(x_side, blocks, g_attn, g_q, g_k, cosine, sine, q_width):
    count = len(blocks)
    tokens, width = 2 * x_side[0][0].shape[0], count * blocks[0].shape[0]
    columns = q_width + 2 * HEAD_SIZE
    steps = 4
    rows = tokens // steps

    def kernel(x0, x1, *refs):
        w_refs = refs[:count]
        g_attn_ref, g_q_ref, g_k_ref, cos_ref, sin_ref, normed_ref, raw_ref, qkv_ref = refs[count:]

        def body(x_ref):
            x = x_ref[...].astype(F32)
            normed_ref[...] = (x * inverse_rms(x) * g_attn_ref[...]).astype(BF16)

        either(pl.program_id(0), steps, [(x0, x1)], body)
        total = dot(normed_ref[...], joined([w[...] for w in w_refs]))
        raw_ref[...] = total[:, : q_width + HEAD_SIZE]
        cos, sin = cos_ref[...], sin_ref[...]
        for at in range(0, q_width + HEAD_SIZE, HEAD_SIZE):
            head = total[:, at : at + HEAD_SIZE]
            gain = g_q_ref[...] if at < q_width else g_k_ref[...]
            qkv_ref[:, at : at + HEAD_SIZE] = turned(head * inverse_rms(head) * gain, cos, sin).astype(BF16)
        qkv_ref[:, q_width + HEAD_SIZE :] = total[:, q_width + HEAD_SIZE :].astype(BF16)

    row = lambda n: pl.BlockSpec((rows, n), lambda i: (i, 0))
    outs = [
        shape((tokens, width), BF16),
        shape((tokens, q_width + HEAD_SIZE), F32),
        shape((tokens, columns), BF16),
    ]
    gains = [g_attn, g_q, g_k]
    return run(
        kernel,
        (steps,),
        half_specs(x_side, width, steps)
        + [pl.BlockSpec((w.shape[0], columns), lambda i: (0, 0)) for w in blocks]
        + [whole(g) for g in gains]
        + [row(HEAD_SIZE), row(HEAD_SIZE)],
        [row(o.shape[1]) for o in outs],
        outs,
        [*x_side[0], *blocks, *gains, cosine, sine],
        flops=2 * tokens * width * columns,
    )


def masked(q, k, allowed, scale):
    return jnp.where(allowed, dot_nt(q, k) * scale, -1e9)


def attention_specs(qkv, kv, kv_block, q_width, quarter, keys):
    parts = kv.shape[0]
    return [
        pl.BlockSpec((2, 1, quarter, q_width), lambda s: (0, s, 0, 0)),
        pl.BlockSpec((parts, 2, 1, quarter, 2 * HEAD_SIZE), lambda s: (0, 0, s, 0, kv_block)),
        pl.BlockSpec((1, 2 * quarter, 2), lambda s: (s, 0, 0)),
        pl.BlockSpec((1, 2, keys), lambda s: (s, 0, 0)),
    ]


def allowed_pairs(q_info, k_info):
    doc_q, index_q = q_info[:, 0:1], q_info[:, 1:2]
    doc_k, index_k = k_info[0:1, :], k_info[1:2, :]
    return (doc_q == doc_k) & (index_k <= index_q)


def attend(qkv, kv, kv_block, q_info, k_info, q_width):
    quarter = qkv.shape[2]
    keys = kv.shape[0] * 2 * quarter
    heads = q_width // HEAD_SIZE
    scale = HEAD_SIZE ** (-0.5)

    def kernel(q_ref, kv_ref, q_info_ref, k_info_ref, out_ref, lse_ref):
        allowed = allowed_pairs(q_info_ref[0], k_info_ref[0])
        pairs = kv_ref[...].reshape(keys, 2 * HEAD_SIZE)
        for h in range(heads):
            at = slice(h * HEAD_SIZE, (h + 1) * HEAD_SIZE)
            q = q_ref[:, 0, :, at].reshape(2 * quarter, HEAD_SIZE)
            scores = masked(q, pairs[:, :HEAD_SIZE], allowed, scale)
            peak = jnp.max(scores, axis=-1, keepdims=True)
            weights = jnp.exp(scores - peak)
            total = jnp.sum(weights, axis=-1, keepdims=True)
            probs = (weights * (1.0 / total)).astype(BF16)
            lse_ref[0, :, h : h + 1] = peak + jnp.log(total)
            attended = dot(probs, pairs[:, HEAD_SIZE:]).astype(BF16)
            out_ref[:, 0, :, at] = attended.reshape(2, quarter, HEAD_SIZE)

    outs = [shape((2, 2, quarter, q_width), BF16), shape((2, 2 * quarter, heads), F32)]
    return run(
        kernel,
        (2,),
        attention_specs(qkv, kv, kv_block, q_width, quarter, keys),
        [
            pl.BlockSpec((2, 1, quarter, q_width), lambda s: (0, s, 0, 0)),
            pl.BlockSpec((1, 2 * quarter, heads), lambda s: (s, 0, 0)),
        ],
        outs,
        [qkv, kv, q_info, k_info],
        flops=4 * 2 * heads * 2 * quarter * keys * HEAD_SIZE,
    )


def attend_back(qkv, kv, kv_block, q_info, k_info, q_width, lse, d_attended):
    quarter = qkv.shape[2]
    parts = kv.shape[0]
    keys = parts * 2 * quarter
    heads = q_width // HEAD_SIZE
    scale = HEAD_SIZE ** (-0.5)

    def kernel(q_ref, kv_ref, q_info_ref, k_info_ref, lse_ref, da_ref, dq_ref, dk_ref, dv_ref):
        allowed = allowed_pairs(q_info_ref[0], k_info_ref[0])
        pairs = kv_ref[...].reshape(keys, 2 * HEAD_SIZE)
        k, v = pairs[:, :HEAD_SIZE], pairs[:, HEAD_SIZE:]
        d_k = d_v = None
        for h in range(heads):
            at = slice(h * HEAD_SIZE, (h + 1) * HEAD_SIZE)
            q = q_ref[:, 0, :, at].reshape(2 * quarter, HEAD_SIZE)
            da = da_ref[:, 0, :, at].reshape(2 * quarter, HEAD_SIZE)
            probs = jnp.exp(masked(q, k, allowed, scale) - lse_ref[0, :, h : h + 1])
            d_probs = dot_nt(da, v)
            row_dot = jnp.sum(probs * d_probs, axis=-1, keepdims=True)
            d_raw = (probs * (d_probs - row_dot) * scale).astype(BF16)
            dq_ref[:, 0, :, at] = dot(d_raw, k).astype(BF16).reshape(2, quarter, HEAD_SIZE)
            k_term, v_term = dot_tn(d_raw, q), dot_tn(probs.astype(BF16), da)
            d_k = k_term if d_k is None else d_k + k_term
            d_v = v_term if d_v is None else d_v + v_term
        dk_ref[...] = d_k.astype(BF16).reshape(parts, 2, 1, quarter, HEAD_SIZE)
        dv_ref[...] = d_v.astype(BF16).reshape(parts, 2, 1, quarter, HEAD_SIZE)

    part = pl.BlockSpec((parts, 2, 1, quarter, HEAD_SIZE), lambda s: (0, 0, s, 0, 0))
    query = pl.BlockSpec((2, 1, quarter, q_width), lambda s: (0, s, 0, 0))
    part_shape = shape((parts, 2, 2, quarter, HEAD_SIZE), BF16)
    return run(
        kernel,
        (2,),
        attention_specs(qkv, kv, kv_block, q_width, quarter, keys)
        + [pl.BlockSpec((1, 2 * quarter, heads), lambda s: (s, 0, 0)), query],
        [query, part, part],
        [shape((2, 2, quarter, q_width), BF16), part_shape, part_shape],
        [qkv, kv, q_info, k_info, lse, d_attended],
        flops=10 * 2 * heads * 2 * quarter * keys * HEAD_SIZE,
    )


def project_back(raw, d_q, d_k, d_v, g_q, g_k, cosine, sine, q_width):
    tokens = raw.shape[0]
    steps = 4
    rows = tokens // steps

    def kernel(raw_ref, dq_ref, dk_ref, dv_ref, g_q_ref, g_k_ref, cos_ref, sin_ref, out_ref, gain_ref):
        cos, sin = cos_ref[...], sin_ref[...]
        gains = [jnp.zeros((1, HEAD_SIZE), F32), jnp.zeros((1, HEAD_SIZE), F32)]
        for at in range(0, q_width + HEAD_SIZE, HEAD_SIZE):
            is_key = int(at >= q_width)
            incoming = (dk_ref[...] if is_key else dq_ref[:, at : at + HEAD_SIZE]).astype(F32)
            back = turned(incoming, cos, -sin)
            head = raw_ref[:, at : at + HEAD_SIZE]
            inverse = inverse_rms(head)
            normed = head * inverse
            gains[is_key] = gains[is_key] + jnp.sum(back * normed, axis=0, keepdims=True)
            gain = g_k_ref[...] if is_key else g_q_ref[...]
            out_ref[:, at : at + HEAD_SIZE] = norm_input_gradient(normed, inverse, back * gain).astype(BF16)
        out_ref[:, q_width + HEAD_SIZE :] = dv_ref[...]

        @pl.when(pl.program_id(0) == 0)
        def _():
            gain_ref[...] = jnp.zeros_like(gain_ref)

        gain_ref[0:1, :] += gains[0]
        gain_ref[1:2, :] += gains[1]

    row = lambda n: pl.BlockSpec((rows, n), lambda i: (i, 0))
    outs = [shape((tokens, q_width + 2 * HEAD_SIZE), BF16), shape((8, HEAD_SIZE), F32)]
    args = [raw, d_q, d_k, d_v, g_q, g_k, cosine, sine]
    in_specs = [row(a.shape[1]) for a in args[:4]] + [whole(g_q), whole(g_k), row(HEAD_SIZE), row(HEAD_SIZE)]
    return run(kernel, (steps,), in_specs, [row(outs[0].shape[1]), whole(outs[1])], outs, args)


def back_rows(which, pairs, received=None, place=None):
    tokens = pairs[0][0].shape[0]
    half = tokens // 2
    steps = BACK_STEPS
    rows = half // steps
    block = half // 4
    count = len(pairs[0][1])
    per = pairs[0][1][0].shape[0]
    width = count * per
    left = [p[0] for p in pairs]
    blocks = [b for p in pairs for b in p[1]]

    def kernel(*refs):
        if place is not None:
            place_ref, refs = refs[0], refs[1:]
        left_refs, w_refs = refs[: len(left)], refs[len(left) : len(left) + len(blocks)]
        out_ref = refs[-1]
        for b in range(count):
            at = slice(b * per, (b + 1) * per)
            lefts = joined([l[...] for l in left_refs], 1)
            total = dot_nt(lefts, joined([w_refs[i * count + b][...] for i in range(len(left))], 1))
            if received is not None:
                total = total + refs[-2][:, at].astype(F32)
            total = total.astype(BF16)
            if place is None:
                out_ref[:, at] = total
                continue
            for i in range(rows // block):
                to = (pl.program_id(0) * (rows // block) + i) ^ place_ref[0]
                out_ref[to, :, at] = total[i * block : (i + 1) * block]

    out = shape((half, width), BF16)
    out_spec = pl.BlockSpec((rows, width), lambda i: (i, 0))
    in_specs = [pl.BlockSpec((rows, p[0].shape[1]), lambda i: (which * steps + i, 0)) for p in pairs]
    for _, group, column, n in pairs:
        in_specs += [pl.BlockSpec((per, n), lambda i, column=column: (0, column)) for _ in group]
    args = left + blocks
    if received is not None:
        in_specs.append(out_spec)
        args = args + [received]
    if place is not None:
        in_specs, args = [scalars()] + in_specs, [place] + args
        out = shape((4, block, width), BF16)
        out_spec = whole(out)
    flops = sum(2 * half * width * p[3] for p in pairs)
    return run(kernel, (steps,), in_specs, out_spec, out, args, flops=flops)


def feed_forward(nm, dy, blocks, chunk):
    count = len(blocks)
    per = blocks[0].shape[0]
    tokens, width = 2 * nm[0][0].shape[0], count * per
    steps = FORWARD_STEPS
    rows = tokens // steps

    def kernel(nm0, nm1, dy0, dy1, *refs):
        w_refs, (hidden_ref, d_ref) = refs[:count], refs[count:]

        def body(nm_ref, dy_ref):
            both = dot(nm_ref[...], joined([w[:, : 2 * chunk] for w in w_refs]))
            d_hidden = dot(dy_ref[...], joined([w[:, 2 * chunk : 3 * chunk] for w in w_refs]))
            gate, upward = both[:, :chunk], both[:, chunk:]
            sigma = 1.0 / (1.0 + jnp.exp(-gate))
            silu = gate * sigma
            hidden_ref[...] = (silu * upward).astype(BF16)
            d_ref[:, :chunk] = (d_hidden * upward * (sigma * (1.0 + gate * (1.0 - sigma)))).astype(BF16)
            d_ref[:, chunk:] = (d_hidden * silu).astype(BF16)

        either(pl.program_id(0), steps, [(nm0, nm1), (dy0, dy1)], body)

    row = lambda n: pl.BlockSpec((rows, n), lambda i: (i, 0))
    outs = [shape((tokens, chunk), BF16), shape((tokens, 2 * chunk), BF16)]
    w_specs = [pl.BlockSpec((per, 3 * chunk), lambda i: (0, 0)) for _ in blocks]
    return run(
        kernel,
        (steps,),
        half_specs(nm, width, steps) + half_specs(dy, width, steps) + w_specs,
        [row(chunk), row(2 * chunk)],
        outs,
        [*nm[0], *dy[0], *blocks],
        flops=2 * tokens * width * 3 * chunk,
    )


def weight_terms(layout, width, n, pairs, received=None):
    tile = width // layout.groups
    cuts = [p[1].shape[1] for p in pairs]
    columns = sum(cuts)
    tokens = pairs[0][1].shape[0]
    left = [(a, p[0][1]) for p in pairs for a in p[0][0]]

    def kernel(*refs):
        refs = list(refs)
        l_refs = [[refs.pop(0) for _ in p[0][0]] for p in pairs]
        d_refs = [refs.pop(0) for _ in pairs]
        in_refs = [refs.pop(0) for _ in (received or ())]
        column = 0
        for sources, d_ref, cut in zip(l_refs, d_refs, cuts):
            total = dot_tn(joined([source[...] for source in sources]), d_ref[...])
            span = slice(column, column + cut)
            column += cut
            for r in in_refs:
                total = total + r[:, span].astype(F32)
            if received is None:
                refs[0][:, span] = total.astype(BF16)
                continue
            for k, out_ref in enumerate(refs):

                @pl.when(pl.program_id(0) == k)
                def _(out_ref=out_ref, total=total, span=span):
                    out_ref[:, span] = total.astype(BF16)

    in_specs = [
        pl.BlockSpec((a.shape[0], tile), lambda k, column=column: (0, column * layout.groups + n * layout.zh + k))
        for a, column in left
    ]
    in_specs += [whole(p[1]) for p in pairs]
    args = [a for a, _ in left] + [p[1] for p in pairs]
    row = pl.BlockSpec((tile, columns), lambda k: (k, 0))
    if received is None:
        outs, out_specs = shape((layout.zh * tile, columns), BF16), row
    else:
        args += received
        in_specs += [row] * len(received)
        outs = [shape((tile, columns), BF16)] * layout.zh
        out_specs = [whole(o) for o in outs]
    return run(
        kernel, (layout.zh,), in_specs, out_specs, outs, args, flops=2 * tokens * layout.zh * tile * columns
    )


def scalars():
    return pl.BlockSpec(memory_space=pltpu.SMEM)


def assemble(own, x, z, both, place):
    rows, width = own.shape

    def kernel(place_ref, *refs):
        for i, ref in enumerate(refs[:4]):
            refs[4][place_ref[0] ^ i] = ref[...]

    out = shape((4, rows, width), BF16)
    args = [place, own, x, z, both]
    result = run(kernel, (1,), [scalars()] + [whole(a) for a in args[1:]], whole(out), out, args)
    return result.reshape(4 * rows, width)


def one_copy(value, width, column=0):
    if len(value.shape) == 2:
        return whole(value)
    return pl.BlockSpec((1, value.shape[1], width), lambda *_: (0, 0, column))


def rows_of(ref):
    return ref[...].reshape(ref.shape[-2:])


def middle_step(parts, x, gain):
    rows, width = x.shape[-2], gain.shape[1]

    def kernel(parts_ref, x_ref, gain_ref, middle_ref, nm_ref):
        middle = rows_of(x_ref).astype(F32)
        for i in range(4):
            middle = middle + parts_ref[i].astype(F32)
        middle_ref[...] = middle
        nm = (middle * inverse_rms(middle) * gain_ref[...]).astype(BF16)
        for i in range(4):
            nm_ref[i] = nm

    outs = [shape((rows, width), F32), shape((4, rows, width), BF16)]
    args = [parts, x, gain]
    return run(kernel, (1,), [whole(parts), one_copy(x, width), whole(gain)], [whole(o) for o in outs], outs, args)


def norm_back_step(parts, base, passed, gain, copies):
    rows, width = base.shape[-2], gain.shape[1]

    def kernel(parts_ref, base_ref, passed_ref, gain_ref, *out_refs):
        total = parts_ref[0].astype(F32)
        for i in range(1, parts.shape[0]):
            total = total + parts_ref[i].astype(F32)
        value = rows_of(base_ref).astype(F32)
        inverse = inverse_rms(value)
        result = rows_of(passed_ref).astype(F32) + norm_input_gradient(
            value * inverse, inverse, total * gain_ref[...]
        )
        rounded = result.astype(BF16)
        if copies == 1:
            out_refs[0][...] = rounded
            return
        out_refs[0][...] = result
        for i in range(copies):
            out_refs[1][i] = rounded

    outs = [shape((rows, width), F32), shape((copies, rows, width), BF16)]
    if copies == 1:
        outs = [shape((rows, width), BF16)]
    args = [parts, base, passed, gain]
    return run(kernel, (1,), [whole(parts), one_copy(base, width), one_copy(passed, width), whole(gain)], [whole(o) for o in outs], outs, args)


def plain_sum(base, *parts):
    def kernel(*refs):
        total = refs[0][...].astype(F32)
        for ref in refs[1:-1]:
            total = total + ref[...].astype(F32)
        refs[-1][...] = total.astype(BF16)

    out = shape(base.shape, BF16)
    args = [base, *parts]
    return run(kernel, (1,), [whole(a) for a in args], whole(out), out, args)


def attended_gradient(d_branch, blocks, column, n):
    count = len(blocks)
    per = blocks[0].shape[0]
    tokens, width = 2 * d_branch[0][0].shape[0], count * per
    steps = 4

    def kernel(d0, d1, *refs):
        w_refs, out_ref = refs[:count], refs[count]

        def body(d_ref):
            out_ref[...] = dot(d_ref[...], joined([w[...] for w in w_refs])).astype(BF16)

        either(pl.program_id(0), steps, [(d0, d1)], body)

    out = shape((tokens, n), BF16)
    return run(
        kernel,
        (steps,),
        half_specs(d_branch, width, steps) + [pl.BlockSpec((per, n), lambda i: (0, column)) for _ in blocks],
        pl.BlockSpec((tokens // steps, n), lambda i: (i, 0)),
        out,
        [*d_branch[0], *blocks],
        flops=2 * tokens * width * n,
    )


def layer(
    sizes,
    tokens,
    doc_ids,
    w_qkv_rows,
    w_out_rows,
    w_gate_up_rows,
    w_down_rows,
    attn_gain,
    q_gain,
    k_gain,
    mlp_gain,
    out_grad,
):
    layout = Layout(sizes)
    rows = tokens.shape[1]
    width = tokens.shape[2]
    owned = w_qkv_rows.shape[0]
    devices = width // owned
    q_width = QUERY_HEADS // TEAM_SIZE * HEAD_SIZE
    chunk = w_down_rows.shape[1] // TEAM_SIZE // CHUNKS
    small = q_gain.shape[0]
    places = layout.order()

    def arrived(value):
        return value.reshape(TEAM_SIZE * owned, -1)

    def gathered(near, far):
        columns = [near] + far
        return [columns[k][n] for n in range(layout.near) for k in range(layout.zh)]

    def with_near(block):
        return [block] + layout.near_blocks(block)

    mine = jnp.concatenate([attn_gain, mlp_gain, q_gain, k_gain, doc_ids.reshape(-1).astype(BF16)])[None]
    table = jnp.zeros((devices, mine.shape[1]), BF16)
    table = lax.dynamic_update_slice(table, mine, (device_index(sizes), 0))
    table = all_sum(table, sizes, ("c",))
    part_attn = arrived(exchange(pack_attention(w_qkv_rows, w_out_rows)))
    send_first, send_rest = pack_chunks(w_gate_up_rows, w_down_rows, chunk)
    x_own, dy_own = reorder([tokens[0], out_grad[0]], places, False)
    corner = (lax.axis_index("zl") * 2 + lax.axis_index("xl")).astype(jnp.int32).reshape(1)
    table, send_first, x_own = hold(table, send_first, x_own)
    table = all_sum(table, sizes, ("xl", "zl"))
    part_attn, x_own, send_first, table, dy_own = hold(part_attn, x_own, send_first, table, dy_own)

    attn_near, attn_far = with_near(part_attn), layout.far_blocks(part_attn)
    parts = [arrived(exchange(send_first))]
    x_parts = [x_own, other_x(x_own), other_z(x_own)]
    table = all_sum(table, sizes, ("y", "xh", "zh"))
    attn_near, attn_far, parts, table, x_parts, dy_own, send_rest = hold(
        attn_near, attn_far, parts, table, x_parts, dy_own, send_rest
    )

    near, far = {}, {}
    x_parts.append(other_x(x_parts[2]))
    w_attn = gathered(attn_near, [with_near(b) for b in attn_far])
    near[0], far[0] = with_near(parts[0]), layout.far_blocks(parts[0])
    rest = arrived(exchange(send_rest))
    parts += [rest[:, j * 3 * chunk : (j + 1) * 3 * chunk] for j in range(CHUNKS - 1)]
    dy_parts = [dy_own, other_x(dy_own), other_z(dy_own)]

    table = table.astype(F32)
    natural = jnp.stack([table[:, :owned].reshape(width), table[:, owned : 2 * owned].reshape(width)])
    count = places.shape[0]
    g_attn, g_mlp = jnp.split(
        jnp.take(natural.reshape(2, count, -1), places, axis=1).reshape(2, width), 2, axis=0
    )
    g_q = table[:, 2 * owned : 2 * owned + small].reshape(1, -1)
    g_k = table[:, 2 * owned + small : 2 * owned + 2 * small].reshape(1, -1)
    docs = table[:, 2 * owned + 2 * small :].astype(jnp.int32)
    docs = docs.reshape(sizes["zh"], 2, sizes["y"], sizes["xh"], 2, 2, rows)
    docs = lax.dynamic_slice(
        docs, (lax.axis_index("zh"), 0, lax.axis_index("y"), 0, 0, 0, 0), (1, 2, 1) + docs.shape[3:]
    )[0, :, 0]
    docs = jnp.moveaxis(jnp.roll(docs, -lax.axis_index("c"), axis=3), 3, 2)
    place = (
        jnp.arange(sizes["xh"])[:, None, None] * 4
        + jnp.arange(2)[None, None, :] * 2
        + (lax.axis_index("c") ^ jnp.arange(2))[None, :, None]
    )
    index = (place[..., None] * rows + jnp.arange(rows)).astype(jnp.int32)
    index = jnp.broadcast_to(index[None], docs.shape)
    k_info = jnp.stack([docs.reshape(2, -1), index.reshape(2, -1)], axis=1)
    q_info = lax.dynamic_slice(
        jnp.stack([docs, index], axis=-1), (0, lax.axis_index("xh"), 0, 0, 0, 0), (2, 1, 2, 2, rows, 2)
    ).reshape(2, -1, 2)
    doc_start = jnp.sum((k_info[:, 0, None, :] < q_info[:, :, 0, None]).astype(jnp.int32), axis=2)
    position = (q_info[:, :, 1] - doc_start).astype(F32)
    position = jnp.moveaxis(position.reshape(2, 2, 2 * rows), 1, 0).reshape(-1, 1)
    half_head = HEAD_SIZE // 2
    freqs = jnp.exp(jnp.arange(half_head).astype(F32) * (-math.log(THETA) / half_head))
    angle = position * freqs
    cosine, sine = jnp.cos(angle), jnp.sin(angle)
    cosine = jnp.concatenate([cosine, cosine], axis=1)
    sine = jnp.concatenate([-sine, sine], axis=1)
    x_half = assemble(*x_parts, corner)
    x_side = ([x_half, other_core(x_half)], 0)
    normed_in, raw, qkv = project(x_side, w_attn, g_attn, g_q, g_k, cosine, sine, q_width)
    qkv4 = qkv.reshape(2, 2, 2 * rows, -1)
    if sizes["xh"] == 1:
        kv, kv_block = qkv4[None], 1
    else:
        kv, kv_block = lax.all_gather(qkv4[..., q_width:], "xh", axis=0, tiled=False), 0
    attended, lse = attend(qkv4, kv, kv_block, q_info, k_info, q_width)
    attended = attended.reshape(-1, q_width)
    out_column = (q_width + 2 * HEAD_SIZE) // q_width
    out_pair = [(attended, w_attn, out_column, q_width)]
    branch_other = back_rows(1, out_pair)
    branch_other, dy_parts, near[0], far[0], parts = hold(branch_other, dy_parts, near[0], far[0], parts)

    near[1], far[1] = with_near(parts[1]), layout.far_blocks(parts[1])
    weights = [gathered(near[0], [with_near(b) for b in far[0]])]
    dy_parts.append(other_x(dy_parts[2]))
    branch = back_rows(0, out_pair, other_core(branch_other))
    branch = among_four(branch.reshape(4, rows, width))
    middle, nm_copies = middle_step(branch, x_own, g_mlp)
    nm_copies, weights[0], near[1], far[1], parts[2], dy_parts = hold(
        nm_copies, weights[0], near[1], far[1], parts[2], dy_parts
    )

    near[2], far[2] = with_near(parts[2]), layout.far_blocks(parts[2])
    weights.append(gathered(near[1], [with_near(b) for b in far[1]]))
    nm_half = spread(nm_copies)
    dy_half = assemble(*dy_parts, corner)
    dy_halves = [dy_half, other_core(dy_half)]
    nm_half, dy_halves, weights[1], near[2], far[2] = hold(nm_half, dy_halves, weights[1], near[2], far[2])
    dy = (dy_halves, 0)

    def near_send(*pairs):
        return [weight_terms(layout, width, n, pairs) for n in range(1, layout.near)]

    def to_near(terms):
        return [layout.to_near(t, n + 1) for n, t in enumerate(terms)]

    def own_terms(received, *pairs):
        return weight_terms(layout, width, 0, pairs, received=received)

    def to_far(sums):
        return [layout.to_far(sums[k], k) for k in range(1, layout.zh)]

    def far_total(own, received):
        total = own.astype(F32)
        for r in received:
            total = total + r.astype(F32)
        return total.astype(BF16).reshape(TEAM_SIZE, owned, -1)

    weights.append(gathered(near[2], [with_near(b) for b in far[2]]))
    nm = ([nm_half, other_core(nm_half)], 0)
    hidden, d_gate_up, mlp, going, arriving, sums, arrived_far = [], [], [], {}, {}, {}, {}

    def chunk_step(j):
        h, d = feed_forward(nm, dy, weights[j], chunk)
        hidden.append(h)
        d_gate_up.append(d)
        mlp.append([(nm, d), (dy, h)])

    chunk_step(0)
    chunk_step(1)
    going[0] = near_send(*mlp[0])
    weights[2], going[0], d_gate_up[1] = hold(weights[2], going[0], d_gate_up[1])

    arriving[0] = to_near(going[0])
    chunk_step(2)
    mid_pairs = [(d_gate_up[j], weights[j], 0, 2 * chunk) for j in range(CHUNKS)]
    out_pairs = [(hidden[j], weights[j], 2, chunk) for j in range(CHUNKS)]
    received = other_core(back_rows(1, mid_pairs))
    terms = back_rows(0, mid_pairs, received)
    terms, hidden, d_gate_up = hold(terms, hidden, d_gate_up)
    mlp = [[(nm, d), (dy, h)] for h, d in zip(hidden, d_gate_up)]
    out_pairs = [(hidden[j], weights[j], 2, chunk) for j in range(CHUNKS)]
    terms = among_four(terms.reshape(4, rows, width))
    going[1] = near_send(*mlp[1])
    sums[0] = own_terms(arriving[0], *mlp[0])
    d_middle, d_copies = norm_back_step(terms, middle, dy_own, g_mlp, 4)
    d_copies, going[1], sums[0], hidden, d_gate_up = hold(d_copies, going[1], sums[0], hidden, d_gate_up)
    mlp = [[(nm, d), (dy, h)] for h, d in zip(hidden, d_gate_up)]
    out_pairs = [(hidden[j], weights[j], 2, chunk) for j in range(CHUNKS)]

    arrived_far[0] = to_far(sums[0])
    arriving[1] = to_near(going[1])
    d_half = spread(d_copies)
    going[2] = near_send(*mlp[2])
    received = other_core(back_rows(1, out_pairs))
    out_total = back_rows(0, out_pairs, received, corner)
    sums[1] = own_terms(arriving[1], *mlp[1])
    d_half, sums[1], arrived_far[0], going[2], out_total = hold(
        d_half, sums[1], arrived_far[0], going[2], out_total
    )

    arrived_far[1] = to_far(sums[1])
    arriving[2] = to_near(going[2])
    out_both = other_x(out_total[3])
    d_branch = ([d_half, other_core(d_half)], 0)
    d_attended = attended_gradient(d_branch, w_attn, out_column, q_width)
    d_attended = d_attended.reshape(2, 2, 2 * rows, q_width)
    d_q, d_k, d_v = attend_back(qkv4, kv, kv_block, q_info, k_info, q_width, lse, d_attended)
    if sizes["xh"] > 1:
        d_k = lax.psum_scatter(d_k, "xh", scatter_dimension=0, tiled=True)
        d_v = lax.psum_scatter(d_v, "xh", scatter_dimension=0, tiled=True)
    d_projected, head_gains = project_back(
        raw,
        d_q.reshape(-1, q_width),
        d_k.reshape(-1, HEAD_SIZE),
        d_v.reshape(-1, HEAD_SIZE),
        g_q,
        g_k,
        cosine,
        sine,
        q_width,
    )
    in_pair = [(d_projected, w_attn, 0, q_width + 2 * HEAD_SIZE)]
    received = other_core(back_rows(1, in_pair))
    terms = back_rows(0, in_pair, received, corner)
    attention = [(([normed_in], 0), d_projected), (d_branch, attended)]
    going[3] = near_send(*attention)
    terms, arriving[2] = hold(terms, arriving[2])
    sums[2] = own_terms(arriving[2], *mlp[2])
    out_z = plain_sum(out_total[2], out_both)
    terms, sums[2], arrived_far[1], out_total, out_z, going[3] = hold(
        terms, sums[2], arrived_far[1], out_total, out_z, going[3]
    )

    arriving[3] = to_near(going[3])
    arrived_far[2] = to_far(sums[2])
    in_both = other_x(terms[3])
    output = plain_sum(middle, out_total[0], other_x(out_total[1]), other_z(out_z))
    sums[3] = own_terms(arriving[3], *attention)
    head_gains = all_sum(head_gains, sizes, ("c", "xl"))
    in_z = plain_sum(terms[2], in_both)
    back_first = exchange(far_total(sums[0][0], arrived_far[0]))
    terms, in_z, sums[3], arrived_far[2], head_gains, output, back_first = hold(
        terms, in_z, sums[3], arrived_far[2], head_gains, output, back_first
    )

    arrived_far[3] = to_far(sums[3])
    back = jnp.concatenate([far_total(sums[j][0], arrived_far[j]) for j in range(1, CHUNKS)], axis=2)
    back = exchange(back)
    terms = jnp.stack([terms[0], other_x(terms[1]), other_z(in_z)])
    (token_grad,) = norm_back_step(terms, x_own, d_middle, g_attn, 1)
    token_grad, output = reorder([token_grad, output], places, True)
    head_gains = all_sum(head_gains, sizes, ("zl", "y", "xh", "zh"))
    back, arrived_far[3], head_gains, token_grad = hold(back, arrived_far[3], head_gains, token_grad)

    last = exchange(far_total(sums[3][0], arrived_far[3]))
    grad_gate_up, grad_down, grad_mlp_gain = unpack_chunks(
        back_first, back, w_gate_up_rows, mlp_gain.astype(F32).reshape(owned, 1), chunk
    )
    grad_qkv, grad_out, grad_attn_gain = unpack_attention(
        last, w_qkv_rows, attn_gain.astype(F32).reshape(owned, 1)
    )
    at = device_index(sizes) * small
    grad_q_gain = lax.dynamic_slice(head_gains[0], (at,), (small,))
    grad_k_gain = lax.dynamic_slice(head_gains[1], (at,), (small,))
    return (
        output[None],
        token_grad[None],
        grad_qkv,
        grad_out,
        grad_gate_up,
        grad_down,
        grad_attn_gain.reshape(owned),
        grad_q_gain,
        grad_k_gain,
        grad_mlp_gain.reshape(owned),
    )


def solution(mesh):
    dp, seq = mesh.shape["dp"], mesh.shape["seq"]
    fine = Mesh(mesh.devices.reshape(dp // 4, 2, 2, seq // 4, 2, 2), AXES)
    sizes = dict(fine.shape)
    dp_axes, seq_axes = ("zh", "zl", "y"), ("xh", "xl", "c")
    token, weight, vector = P(dp_axes, seq_axes, None), P(AXES, None), P(AXES)
    wide = P(AXES, None, None)

    def shards(*args):
        return layer(sizes, *args)

    return jax.shard_map(
        shards,
        mesh=fine,
        in_specs=(token, P(dp_axes, seq_axes), weight, weight, wide, weight, vector, vector, vector, vector, token),
        out_specs=(token, token, weight, weight, wide, weight, vector, vector, vector, vector),
        check_vma=False,
    )
```

```python
import math

import jax
import jax.numpy as jnp
from jax import lax
from jax.experimental import pallas as pl
from jax.experimental.pallas import tpu as pltpu
from jax.sharding import Mesh, PartitionSpec as P

QUERY_HEADS = 16
KEY_VALUE_HEADS = 8
HEAD_SIZE = 128
EPS = 1e-06
THETA = 1000000.0

F32 = jnp.float32
BF16 = jnp.bfloat16
SWAP = [(0, 1), (1, 0)]
TEAM = ("zl", "xl", "c")
TEAM_SIZE = 8
AXES = ("zh", "zl", "y", "xh", "xl", "c")
CHUNKS = 3
VMEM_LIMIT = 32 << 20
WEIGHT = 100
FORWARD_STEPS = 4
BACK_STEPS = 2


def hold(*values):
    return lax.optimization_barrier(values)


class Layout:
    def __init__(self, sizes):
        self.zh, self.y, self.xh = sizes["zh"], sizes["y"], sizes["xh"]
        self.near = self.y * self.xh
        self.groups = self.zh * self.near

    def order(self):
        zh, y, xh = (lax.axis_index(name) for name in ("zh", "y", "xh"))
        places = []
        for j in range(self.y):
            for i in range(self.xh):
                for k in range(self.zh):
                    for low in range(2):
                        at = ((zh + k) % self.zh * 2 + low) * self.y + (y + j) % self.y
                        places.append(at * self.xh + (xh + i) % self.xh)
        return jnp.stack(places).astype(jnp.int32)

    def far_blocks(self, block):
        return [
            lax.ppermute(block, "zh", [((i + k) % self.zh, i) for i in range(self.zh)]) for k in range(1, self.zh)
        ]

    def shifted(self, n):
        j, i = n // self.xh, n % self.xh
        return [
            (a * self.xh + b, (a + j) % self.y * self.xh + (b + i) % self.xh)
            for a in range(self.y)
            for b in range(self.xh)
        ]

    def near_blocks(self, block):
        return [
            lax.ppermute(block, ("y", "xh"), [(b, a) for a, b in self.shifted(n)]) for n in range(1, self.near)
        ]

    def to_near(self, value, n):
        return lax.ppermute(value, ("y", "xh"), self.shifted(n))

    def to_far(self, value, k):
        return lax.ppermute(value, "zh", [(i, (i + k) % self.zh) for i in range(self.zh)])


def among_four(value):
    return lax.all_to_all(value, ("zl", "xl"), 0, 0, tiled=True)


def spread(copies):
    return among_four(copies).reshape(-1, copies.shape[-1])


def other_core(value):
    return lax.ppermute(value, "c", SWAP)


def other_x(value):
    return lax.ppermute(value, "xl", SWAP)


def other_z(value):
    return lax.ppermute(value, "zl", SWAP)


def exchange(value):
    return lax.all_to_all(value, TEAM, 0, 0, tiled=True)


def all_sum(value, sizes, axes):
    for axis in axes:
        total = value
        for k in range(1, sizes[axis]):
            total = total + lax.ppermute(value, axis, [((i + k) % sizes[axis], i) for i in range(sizes[axis])])
        value = total
    return value


def device_index(sizes):
    index = 0
    for axis in AXES:
        index = index * sizes[axis] + lax.axis_index(axis)
    return index


def dot(left, right):
    return lax.dot_general(left, right, (((1,), (0,)), ((), ())), preferred_element_type=F32)


def dot_nt(left, right):
    return lax.dot_general(left, right, (((1,), (1,)), ((), ())), preferred_element_type=F32)


def dot_tn(left, right):
    return lax.dot_general(left, right, (((0,), (0,)), ((), ())), preferred_element_type=F32)


def joined(values, axis=0):
    return values[0] if len(values) == 1 else jnp.concatenate(values, axis=axis)


def shape(dims, dtype):
    return jax.ShapeDtypeStruct(tuple(dims), dtype)


def in_hbm(args):
    return [
        pltpu.with_memory_space_constraint(a, pltpu.HBM) if math.prod(a.shape) >= 1 << 16 else a for a in args
    ]


def run(kernel, grid, in_specs, out_specs, out_shape, args, flops=0):
    outs = jax.tree.leaves(out_shape)
    size = sum(math.prod(a.shape) * a.dtype.itemsize for a in list(args) + outs)
    return pl.pallas_call(
        kernel,
        grid=grid,
        in_specs=in_specs,
        out_specs=out_specs,
        out_shape=out_shape,
        compiler_params=pltpu.CompilerParams(
            vmem_limit_bytes=VMEM_LIMIT, dimension_semantics=("arbitrary",) * len(grid)
        ),
        cost_estimate=pl.CostEstimate(
            flops=WEIGHT * int(flops), bytes_accessed=WEIGHT * int(size), transcendentals=0
        ),
    )(*args)


def whole(array):
    return pl.BlockSpec(array.shape, lambda *_, n=len(array.shape): (0,) * n)


def inverse_rms(value):
    return lax.rsqrt(jnp.mean(value * value, axis=-1, keepdims=True) + EPS)


def norm_input_gradient(normed, inverse, e):
    return inverse * (e - normed * jnp.mean(e * normed, axis=-1, keepdims=True))


def reorder(values, places, inverse, copies=0):
    count = places.shape[0]
    width = values[0].shape[-1]
    cut = width // count
    if cut % 128:
        at = jnp.argsort(places) if inverse else places
        moved = [jnp.take(v.reshape(v.shape[:-1] + (count, cut)), at, axis=-2).reshape(v.shape) for v in values]
        if copies:
            moved = [jnp.broadcast_to(v[None], (copies,) + v.shape) for v in moved]
        return moved
    outs = [shape(((copies,) if copies else ()) + v.shape, v.dtype) for v in values]

    def kernel(places_ref, *refs):
        for source, target in zip(refs[: len(values)], refs[len(values) :]):
            for i in range(count):
                moving = pl.ds(pl.multiple_of(places_ref[i] * cut, 128), cut)
                still = pl.ds(i * cut, cut)
                if copies:
                    value = source[:, moving]
                    for copy in range(copies):
                        target[copy, :, still] = value
                else:
                    target[:, moving if inverse else still] = source[:, still if inverse else moving]

    size = sum(math.prod(a.shape) * a.dtype.itemsize for a in list(values) + outs)
    return pl.pallas_call(
        kernel,
        grid_spec=pltpu.PrefetchScalarGridSpec(
            num_scalar_prefetch=1,
            grid=(1,),
            in_specs=[whole(v) for v in values],
            out_specs=[whole(o) for o in outs],
        ),
        out_shape=outs,
        compiler_params=pltpu.CompilerParams(vmem_limit_bytes=VMEM_LIMIT),
        cost_estimate=pl.CostEstimate(flops=0, bytes_accessed=WEIGHT * size, transcendentals=0),
    )(places, *values)


def pack_attention(w_qkv, w_out):
    owned, columns = w_qkv.shape
    q_cols, kv_cols = QUERY_HEADS * HEAD_SIZE, KEY_VALUE_HEADS * HEAD_SIZE
    q_width = q_cols // TEAM_SIZE

    def kernel(w_ref, w_out_ref, out_ref):
        for r in range(TEAM_SIZE):
            out_ref[r, :, :q_width] = w_ref[:, r * q_width : (r + 1) * q_width]
            for part in range(2):
                at = q_cols + part * kv_cols + r * HEAD_SIZE
                to = q_width + part * HEAD_SIZE
                out_ref[r, :, to : to + HEAD_SIZE] = w_ref[:, at : at + HEAD_SIZE]
            out_ref[r, :, columns // TEAM_SIZE :] = w_out_ref[:, r * q_width : (r + 1) * q_width]

    out = shape((TEAM_SIZE, owned, columns // TEAM_SIZE + q_width), BF16)
    return run(kernel, (1,), [whole(w_qkv), whole(w_out)], whole(out), out, in_hbm([w_qkv, w_out]))


def pack_chunks(w_gate_up, w_down, chunk):
    owned = w_down.shape[0]
    per = w_down.shape[1] // TEAM_SIZE

    def kernel(gate_up_ref, down_ref, *targets):
        for j in range(CHUNKS):
            target = targets[min(j, 1)]
            to = 3 * chunk * max(j - 1, 0)
            for r in range(TEAM_SIZE):
                at = slice(r * per + j * chunk, r * per + (j + 1) * chunk)
                target[r, :, to : to + chunk] = gate_up_ref[:, 0, at]
                target[r, :, to + chunk : to + 2 * chunk] = gate_up_ref[:, 1, at]
                target[r, :, to + 2 * chunk : to + 3 * chunk] = down_ref[:, at]

    outs = [shape((TEAM_SIZE, owned, 3 * chunk * n), BF16) for n in (1, CHUNKS - 1)]
    args = [w_gate_up, w_down]
    return run(kernel, (1,), [whole(a) for a in args], [whole(o) for o in outs], outs, args)


def unpack_chunks(first, rest, w_gate_up, gain, chunk):
    owned = first.shape[1]
    per = CHUNKS * chunk

    def kernel(first_ref, rest_ref, w_ref, gain_ref, gate_up_ref, down_ref, out_ref):
        r = pl.program_id(0)
        total = jnp.zeros((owned, 1), F32)
        for j in range(CHUNKS):
            back_ref = rest_ref if j == CHUNKS - 1 else first_ref
            at, to = 3 * chunk * (j % (CHUNKS - 1)), slice(j * chunk, (j + 1) * chunk)
            for part in range(2):
                value = back_ref[0, :, at + part * chunk : at + (part + 1) * chunk].astype(F32)
                gate_up_ref[:, part, to] = value
                total = total + jnp.sum(value * w_ref[:, part, to].astype(F32), axis=1, keepdims=True)
            down_ref[:, to] = back_ref[0, :, at + 2 * chunk : at + 3 * chunk].astype(F32)
        total = total / gain_ref[...]

        @pl.when(r == 0)
        def _():
            out_ref[...] = total

        @pl.when(r > 0)
        def _():
            out_ref[...] += total

    outs = [
        shape((owned, 2, TEAM_SIZE * per), F32),
        shape((owned, TEAM_SIZE * per), F32),
        shape((owned, 1), F32),
    ]
    wide = pl.BlockSpec((owned, 2, per), lambda r: (0, 0, r))
    return run(
        kernel,
        (TEAM_SIZE,),
        [pl.BlockSpec((1,) + b.shape[1:], lambda r: (r, 0, 0)) for b in (first, rest)] + [wide, whole(gain)],
        [wide, pl.BlockSpec((owned, per), lambda r: (0, r)), whole(gain)],
        outs,
        in_hbm([first, rest, w_gate_up, gain]),
    )


def unpack_attention(back, w_qkv, gain):
    owned, columns = w_qkv.shape
    q_cols, kv_cols = QUERY_HEADS * HEAD_SIZE, KEY_VALUE_HEADS * HEAD_SIZE
    q_width = q_cols // TEAM_SIZE

    def kernel(back_ref, w_ref, gain_ref, qkv_ref, out_weight_ref, out_ref):
        total = jnp.zeros((owned, 1), F32)
        for r in range(TEAM_SIZE):
            spans = [(0, r * q_width, q_width)]
            for part in range(2):
                spans.append((q_width + part * HEAD_SIZE, q_cols + part * kv_cols + r * HEAD_SIZE, HEAD_SIZE))
            for at, to, n in spans:
                value = back_ref[r, :, at : at + n].astype(F32)
                qkv_ref[:, to : to + n] = value
                total = total + jnp.sum(value * w_ref[:, to : to + n].astype(F32), axis=1, keepdims=True)
            out_weight_ref[:, r * q_width : (r + 1) * q_width] = back_ref[
                r, :, q_width + 2 * HEAD_SIZE :
            ].astype(F32)
        out_ref[...] = total / gain_ref[...]

    outs = [shape((owned, columns), F32), shape((owned, q_cols), F32), shape((owned, 1), F32)]
    args = [back, w_qkv, gain]
    return run(kernel, (1,), [whole(a) for a in args], [whole(o) for o in outs], outs, args)


def either(step, steps, refs, body):
    per = steps // 2

    @pl.when(step < per)
    def _():
        body(*[r[0] for r in refs])

    @pl.when(step >= per)
    def _():
        body(*[r[1] for r in refs])


def half_specs(side, width, steps):
    halves, column = side
    per = steps // 2
    rows = halves[0].shape[0]
    return [
        pl.BlockSpec((rows // per, width), lambda i: (jnp.minimum(i, per - 1), column)),
        pl.BlockSpec((rows // per, width), lambda i: (jnp.maximum(i - per, 0), column)),
    ]


def turned(value, cosine, sine):
    return value * cosine + pltpu.roll(value, HEAD_SIZE // 2, 1) * sine


def project(x_side, blocks, g_attn, g_q, g_k, cosine, sine, q_width):
    count = len(blocks)
    tokens, width = 2 * x_side[0][0].shape[0], count * blocks[0].shape[0]
    columns = q_width + 2 * HEAD_SIZE
    steps = 4
    rows = tokens // steps

    def kernel(x0, x1, *refs):
        w_refs = refs[:count]
        g_attn_ref, g_q_ref, g_k_ref, cos_ref, sin_ref, normed_ref, raw_ref, qkv_ref = refs[count:]

        def body(x_ref):
            x = x_ref[...].astype(F32)
            normed_ref[...] = (x * inverse_rms(x) * g_attn_ref[...]).astype(BF16)

        either(pl.program_id(0), steps, [(x0, x1)], body)
        total = dot(normed_ref[...], joined([w[...] for w in w_refs]))
        raw_ref[...] = total[:, : q_width + HEAD_SIZE]
        cos, sin = cos_ref[...], sin_ref[...]
        for at in range(0, q_width + HEAD_SIZE, HEAD_SIZE):
            head = total[:, at : at + HEAD_SIZE]
            gain = g_q_ref[...] if at < q_width else g_k_ref[...]
            qkv_ref[:, at : at + HEAD_SIZE] = turned(head * inverse_rms(head) * gain, cos, sin).astype(BF16)
        qkv_ref[:, q_width + HEAD_SIZE :] = total[:, q_width + HEAD_SIZE :].astype(BF16)

    row = lambda n: pl.BlockSpec((rows, n), lambda i: (i, 0))
    outs = [
        shape((tokens, width), BF16),
        shape((tokens, q_width + HEAD_SIZE), F32),
        shape((tokens, columns), BF16),
    ]
    gains = [g_attn, g_q, g_k]
    return run(
        kernel,
        (steps,),
        half_specs(x_side, width, steps)
        + [pl.BlockSpec((w.shape[0], columns), lambda i: (0, 0)) for w in blocks]
        + [whole(g) for g in gains]
        + [row(HEAD_SIZE), row(HEAD_SIZE)],
        [row(o.shape[1]) for o in outs],
        outs,
        [*x_side[0], *blocks, *gains, cosine, sine],
        flops=2 * tokens * width * columns,
    )


def masked(q, k, allowed, scale):
    return jnp.where(allowed, dot_nt(q, k) * scale, -1e9)


def attention_specs(qkv, kv, kv_block, q_width, quarter, keys):
    parts = kv.shape[0]
    return [
        pl.BlockSpec((2, 1, quarter, q_width), lambda s: (0, s, 0, 0)),
        pl.BlockSpec((parts, 2, 1, quarter, 2 * HEAD_SIZE), lambda s: (0, 0, s, 0, kv_block)),
        pl.BlockSpec((1, 2 * quarter, 2), lambda s: (s, 0, 0)),
        pl.BlockSpec((1, 2, keys), lambda s: (s, 0, 0)),
    ]


def allowed_pairs(q_info, k_info):
    doc_q, index_q = q_info[:, 0:1], q_info[:, 1:2]
    doc_k, index_k = k_info[0:1, :], k_info[1:2, :]
    return (doc_q == doc_k) & (index_k <= index_q)


def attend(qkv, kv, kv_block, q_info, k_info, q_width):
    quarter = qkv.shape[2]
    keys = kv.shape[0] * 2 * quarter
    heads = q_width // HEAD_SIZE
    scale = HEAD_SIZE ** (-0.5)

    def kernel(q_ref, kv_ref, q_info_ref, k_info_ref, out_ref, lse_ref):
        allowed = allowed_pairs(q_info_ref[0], k_info_ref[0])
        pairs = kv_ref[...].reshape(keys, 2 * HEAD_SIZE)
        for h in range(heads):
            at = slice(h * HEAD_SIZE, (h + 1) * HEAD_SIZE)
            q = q_ref[:, 0, :, at].reshape(2 * quarter, HEAD_SIZE)
            scores = masked(q, pairs[:, :HEAD_SIZE], allowed, scale)
            peak = jnp.max(scores, axis=-1, keepdims=True)
            weights = jnp.exp(scores - peak)
            total = jnp.sum(weights, axis=-1, keepdims=True)
            probs = (weights * (1.0 / total)).astype(BF16)
            lse_ref[0, :, h : h + 1] = peak + jnp.log(total)
            attended = dot(probs, pairs[:, HEAD_SIZE:]).astype(BF16)
            out_ref[:, 0, :, at] = attended.reshape(2, quarter, HEAD_SIZE)

    outs = [shape((2, 2, quarter, q_width), BF16), shape((2, 2 * quarter, heads), F32)]
    return run(
        kernel,
        (2,),
        attention_specs(qkv, kv, kv_block, q_width, quarter, keys),
        [
            pl.BlockSpec((2, 1, quarter, q_width), lambda s: (0, s, 0, 0)),
            pl.BlockSpec((1, 2 * quarter, heads), lambda s: (s, 0, 0)),
        ],
        outs,
        [qkv, kv, q_info, k_info],
        flops=4 * 2 * heads * 2 * quarter * keys * HEAD_SIZE,
    )


def attend_back(qkv, kv, kv_block, q_info, k_info, q_width, lse, d_attended):
    quarter = qkv.shape[2]
    parts = kv.shape[0]
    keys = parts * 2 * quarter
    heads = q_width // HEAD_SIZE
    scale = HEAD_SIZE ** (-0.5)

    def kernel(q_ref, kv_ref, q_info_ref, k_info_ref, lse_ref, da_ref, dq_ref, dk_ref, dv_ref):
        allowed = allowed_pairs(q_info_ref[0], k_info_ref[0])
        pairs = kv_ref[...].reshape(keys, 2 * HEAD_SIZE)
        k, v = pairs[:, :HEAD_SIZE], pairs[:, HEAD_SIZE:]
        d_k = d_v = None
        for h in range(heads):
            at = slice(h * HEAD_SIZE, (h + 1) * HEAD_SIZE)
            q = q_ref[:, 0, :, at].reshape(2 * quarter, HEAD_SIZE)
            da = da_ref[:, 0, :, at].reshape(2 * quarter, HEAD_SIZE)
            probs = jnp.exp(masked(q, k, allowed, scale) - lse_ref[0, :, h : h + 1])
            d_probs = dot_nt(da, v)
            row_dot = jnp.sum(probs * d_probs, axis=-1, keepdims=True)
            d_raw = (probs * (d_probs - row_dot) * scale).astype(BF16)
            dq_ref[:, 0, :, at] = dot(d_raw, k).astype(BF16).reshape(2, quarter, HEAD_SIZE)
            k_term, v_term = dot_tn(d_raw, q), dot_tn(probs.astype(BF16), da)
            d_k = k_term if d_k is None else d_k + k_term
            d_v = v_term if d_v is None else d_v + v_term
        dk_ref[...] = d_k.astype(BF16).reshape(parts, 2, 1, quarter, HEAD_SIZE)
        dv_ref[...] = d_v.astype(BF16).reshape(parts, 2, 1, quarter, HEAD_SIZE)

    part = pl.BlockSpec((parts, 2, 1, quarter, HEAD_SIZE), lambda s: (0, 0, s, 0, 0))
    query = pl.BlockSpec((2, 1, quarter, q_width), lambda s: (0, s, 0, 0))
    part_shape = shape((parts, 2, 2, quarter, HEAD_SIZE), BF16)
    return run(
        kernel,
        (2,),
        attention_specs(qkv, kv, kv_block, q_width, quarter, keys)
        + [pl.BlockSpec((1, 2 * quarter, heads), lambda s: (s, 0, 0)), query],
        [query, part, part],
        [shape((2, 2, quarter, q_width), BF16), part_shape, part_shape],
        [qkv, kv, q_info, k_info, lse, d_attended],
        flops=10 * 2 * heads * 2 * quarter * keys * HEAD_SIZE,
    )


def project_back(raw, d_q, d_k, d_v, g_q, g_k, cosine, sine, q_width):
    tokens = raw.shape[0]
    steps = 4
    rows = tokens // steps

    def kernel(raw_ref, dq_ref, dk_ref, dv_ref, g_q_ref, g_k_ref, cos_ref, sin_ref, out_ref, gain_ref):
        cos, sin = cos_ref[...], sin_ref[...]
        gains = [jnp.zeros((1, HEAD_SIZE), F32), jnp.zeros((1, HEAD_SIZE), F32)]
        for at in range(0, q_width + HEAD_SIZE, HEAD_SIZE):
            is_key = int(at >= q_width)
            incoming = (dk_ref[...] if is_key else dq_ref[:, at : at + HEAD_SIZE]).astype(F32)
            back = turned(incoming, cos, -sin)
            head = raw_ref[:, at : at + HEAD_SIZE]
            inverse = inverse_rms(head)
            normed = head * inverse
            gains[is_key] = gains[is_key] + jnp.sum(back * normed, axis=0, keepdims=True)
            gain = g_k_ref[...] if is_key else g_q_ref[...]
            out_ref[:, at : at + HEAD_SIZE] = norm_input_gradient(normed, inverse, back * gain).astype(BF16)
        out_ref[:, q_width + HEAD_SIZE :] = dv_ref[...]

        @pl.when(pl.program_id(0) == 0)
        def _():
            gain_ref[...] = jnp.zeros_like(gain_ref)

        gain_ref[0:1, :] += gains[0]
        gain_ref[1:2, :] += gains[1]

    row = lambda n: pl.BlockSpec((rows, n), lambda i: (i, 0))
    outs = [shape((tokens, q_width + 2 * HEAD_SIZE), BF16), shape((8, HEAD_SIZE), F32)]
    args = [raw, d_q, d_k, d_v, g_q, g_k, cosine, sine]
    in_specs = [row(a.shape[1]) for a in args[:4]] + [whole(g_q), whole(g_k), row(HEAD_SIZE), row(HEAD_SIZE)]
    return run(kernel, (steps,), in_specs, [row(outs[0].shape[1]), whole(outs[1])], outs, args)


def back_rows(which, pairs, received=None, place=None):
    tokens = pairs[0][0].shape[0]
    half = tokens // 2
    steps = BACK_STEPS
    rows = half // steps
    block = half // 4
    count = len(pairs[0][1])
    per = pairs[0][1][0].shape[0]
    width = count * per
    left = [p[0] for p in pairs]
    blocks = [b for p in pairs for b in p[1]]

    def kernel(*refs):
        if place is not None:
            place_ref, refs = refs[0], refs[1:]
        left_refs, w_refs = refs[: len(left)], refs[len(left) : len(left) + len(blocks)]
        out_ref = refs[-1]
        for b in range(count):
            at = slice(b * per, (b + 1) * per)
            lefts = joined([l[...] for l in left_refs], 1)
            total = dot_nt(lefts, joined([w_refs[i * count + b][...] for i in range(len(left))], 1))
            if received is not None:
                total = total + refs[-2][:, at].astype(F32)
            total = total.astype(BF16)
            if place is None:
                out_ref[:, at] = total
                continue
            for i in range(rows // block):
                to = (pl.program_id(0) * (rows // block) + i) ^ place_ref[0]
                out_ref[to, :, at] = total[i * block : (i + 1) * block]

    out = shape((half, width), BF16)
    out_spec = pl.BlockSpec((rows, width), lambda i: (i, 0))
    in_specs = [pl.BlockSpec((rows, p[0].shape[1]), lambda i: (which * steps + i, 0)) for p in pairs]
    for _, group, column, n in pairs:
        in_specs += [pl.BlockSpec((per, n), lambda i, column=column: (0, column)) for _ in group]
    args = left + blocks
    if received is not None:
        in_specs.append(out_spec)
        args = args + [received]
    if place is not None:
        in_specs, args = [scalars()] + in_specs, [place] + args
        out = shape((4, block, width), BF16)
        out_spec = whole(out)
    flops = sum(2 * half * width * p[3] for p in pairs)
    return run(kernel, (steps,), in_specs, out_spec, out, args, flops=flops)


def feed_forward(nm, dy, blocks, chunk):
    count = len(blocks)
    per = blocks[0].shape[0]
    tokens, width = 2 * nm[0][0].shape[0], count * per
    steps = FORWARD_STEPS
    rows = tokens // steps

    def kernel(nm0, nm1, dy0, dy1, *refs):
        w_refs, (hidden_ref, d_ref) = refs[:count], refs[count:]

        def body(nm_ref, dy_ref):
            both = dot(nm_ref[...], joined([w[:, : 2 * chunk] for w in w_refs]))
            d_hidden = dot(dy_ref[...], joined([w[:, 2 * chunk : 3 * chunk] for w in w_refs]))
            gate, upward = both[:, :chunk], both[:, chunk:]
            sigma = 1.0 / (1.0 + jnp.exp(-gate))
            silu = gate * sigma
            hidden_ref[...] = (silu * upward).astype(BF16)
            d_ref[:, :chunk] = (d_hidden * upward * (sigma * (1.0 + gate * (1.0 - sigma)))).astype(BF16)
            d_ref[:, chunk:] = (d_hidden * silu).astype(BF16)

        either(pl.program_id(0), steps, [(nm0, nm1), (dy0, dy1)], body)

    row = lambda n: pl.BlockSpec((rows, n), lambda i: (i, 0))
    outs = [shape((tokens, chunk), BF16), shape((tokens, 2 * chunk), BF16)]
    w_specs = [pl.BlockSpec((per, 3 * chunk), lambda i: (0, 0)) for _ in blocks]
    return run(
        kernel,
        (steps,),
        half_specs(nm, width, steps) + half_specs(dy, width, steps) + w_specs,
        [row(chunk), row(2 * chunk)],
        outs,
        in_hbm([*nm[0], *dy[0], *blocks]),
        flops=2 * tokens * width * 3 * chunk,
    )


def weight_terms(layout, width, n, pairs, received=None):
    tile = width // layout.groups
    cuts = [p[1].shape[1] for p in pairs]
    columns = sum(cuts)
    tokens = pairs[0][1].shape[0]
    left = [(a, p[0][1]) for p in pairs for a in p[0][0]]

    def kernel(*refs):
        refs = list(refs)
        l_refs = [[refs.pop(0) for _ in p[0][0]] for p in pairs]
        d_refs = [refs.pop(0) for _ in pairs]
        in_refs = [refs.pop(0) for _ in (received or ())]
        column = 0
        for sources, d_ref, cut in zip(l_refs, d_refs, cuts):
            total = dot_tn(joined([source[...] for source in sources]), d_ref[...])
            span = slice(column, column + cut)
            column += cut
            for r in in_refs:
                total = total + r[:, span].astype(F32)
            if received is None:
                refs[0][:, span] = total.astype(BF16)
                continue
            for k, out_ref in enumerate(refs):

                @pl.when(pl.program_id(0) == k)
                def _(out_ref=out_ref, total=total, span=span):
                    out_ref[:, span] = total.astype(BF16)

    in_specs = [
        pl.BlockSpec((a.shape[0], tile), lambda k, column=column: (0, column * layout.groups + n * layout.zh + k))
        for a, column in left
    ]
    in_specs += [whole(p[1]) for p in pairs]
    args = [a for a, _ in left] + [p[1] for p in pairs]
    row = pl.BlockSpec((tile, columns), lambda k: (k, 0))
    if received is None:
        outs, out_specs = shape((layout.zh * tile, columns), BF16), row
    else:
        args += received
        in_specs += [row] * len(received)
        outs = [shape((tile, columns), BF16)] * layout.zh
        out_specs = [whole(o) for o in outs]
    return run(
        kernel, (layout.zh,), in_specs, out_specs, outs, args, flops=2 * tokens * layout.zh * tile * columns
    )


def scalars():
    return pl.BlockSpec(memory_space=pltpu.SMEM)


def assemble(own, x, z, both, place):
    rows, width = own.shape

    def kernel(place_ref, *refs):
        for i, ref in enumerate(refs[:4]):
            refs[4][place_ref[0] ^ i] = ref[...]

    out = shape((4, rows, width), BF16)
    args = [place, own, x, z, both]
    result = run(kernel, (1,), [scalars()] + [whole(a) for a in args[1:]], whole(out), out, in_hbm(args))
    return result.reshape(4 * rows, width)


def one_copy(value, width, column=0):
    if len(value.shape) == 2:
        return whole(value)
    return pl.BlockSpec((1, value.shape[1], width), lambda *_: (0, 0, column))


def rows_of(ref):
    return ref[...].reshape(ref.shape[-2:])


def middle_step(parts, x, gain):
    rows, width = x.shape[-2], gain.shape[1]

    def kernel(parts_ref, x_ref, gain_ref, middle_ref, nm_ref):
        middle = rows_of(x_ref).astype(F32)
        for i in range(4):
            middle = middle + parts_ref[i].astype(F32)
        middle_ref[...] = middle
        nm = (middle * inverse_rms(middle) * gain_ref[...]).astype(BF16)
        for i in range(4):
            nm_ref[i] = nm

    outs = [shape((rows, width), F32), shape((4, rows, width), BF16)]
    args = [parts, x, gain]
    return run(kernel, (1,), [whole(parts), one_copy(x, width), whole(gain)], [whole(o) for o in outs], outs, args)


def norm_back_step(parts, base, passed, gain, copies):
    rows, width = base.shape[-2], gain.shape[1]

    def kernel(parts_ref, base_ref, passed_ref, gain_ref, *out_refs):
        total = parts_ref[0].astype(F32)
        for i in range(1, parts.shape[0]):
            total = total + parts_ref[i].astype(F32)
        value = rows_of(base_ref).astype(F32)
        inverse = inverse_rms(value)
        result = rows_of(passed_ref).astype(F32) + norm_input_gradient(
            value * inverse, inverse, total * gain_ref[...]
        )
        rounded = result.astype(BF16)
        if copies == 1:
            out_refs[0][...] = rounded
            return
        out_refs[0][...] = result
        for i in range(copies):
            out_refs[1][i] = rounded

    outs = [shape((rows, width), F32), shape((copies, rows, width), BF16)]
    if copies == 1:
        outs = [shape((rows, width), BF16)]
    args = [parts, base, passed, gain]
    return run(kernel, (1,), [whole(parts), one_copy(base, width), one_copy(passed, width), whole(gain)], [whole(o) for o in outs], outs, args)


def plain_sum(base, *parts):
    def kernel(*refs):
        total = refs[0][...].astype(F32)
        for ref in refs[1:-1]:
            total = total + ref[...].astype(F32)
        refs[-1][...] = total.astype(BF16)

    out = shape(base.shape, BF16)
    args = [base, *parts]
    return run(kernel, (1,), [whole(a) for a in args], whole(out), out, args)


def attended_gradient(d_branch, blocks, column, n):
    count = len(blocks)
    per = blocks[0].shape[0]
    tokens, width = 2 * d_branch[0][0].shape[0], count * per
    steps = 4

    def kernel(d0, d1, *refs):
        w_refs, out_ref = refs[:count], refs[count]

        def body(d_ref):
            out_ref[...] = dot(d_ref[...], joined([w[...] for w in w_refs])).astype(BF16)

        either(pl.program_id(0), steps, [(d0, d1)], body)

    out = shape((tokens, n), BF16)
    return run(
        kernel,
        (steps,),
        half_specs(d_branch, width, steps) + [pl.BlockSpec((per, n), lambda i: (0, column)) for _ in blocks],
        pl.BlockSpec((tokens // steps, n), lambda i: (i, 0)),
        out,
        [*d_branch[0], *blocks],
        flops=2 * tokens * width * n,
    )


def layer(
    sizes,
    tokens,
    doc_ids,
    w_qkv_rows,
    w_out_rows,
    w_gate_up_rows,
    w_down_rows,
    attn_gain,
    q_gain,
    k_gain,
    mlp_gain,
    out_grad,
):
    layout = Layout(sizes)
    rows = tokens.shape[1]
    width = tokens.shape[2]
    owned = w_qkv_rows.shape[0]
    devices = width // owned
    q_width = QUERY_HEADS // TEAM_SIZE * HEAD_SIZE
    chunk = w_down_rows.shape[1] // TEAM_SIZE // CHUNKS
    small = q_gain.shape[0]
    places = layout.order()

    def arrived(value):
        return value.reshape(TEAM_SIZE * owned, -1)

    def gathered(near, far):
        columns = [near] + far
        return [columns[k][n] for n in range(layout.near) for k in range(layout.zh)]

    def with_near(block):
        return [block] + layout.near_blocks(block)

    mine = jnp.concatenate([attn_gain, mlp_gain, q_gain, k_gain, doc_ids.reshape(-1).astype(BF16)])[None]
    table = jnp.zeros((devices, mine.shape[1]), BF16)
    table = lax.dynamic_update_slice(table, mine, (device_index(sizes), 0))
    table = all_sum(table, sizes, ("c",))
    part_attn = arrived(exchange(pack_attention(w_qkv_rows, w_out_rows)))
    send_first, send_rest = pack_chunks(w_gate_up_rows, w_down_rows, chunk)
    x_own, dy_own = reorder([tokens[0], out_grad[0]], places, False)
    corner = (lax.axis_index("zl") * 2 + lax.axis_index("xl")).astype(jnp.int32).reshape(1)
    table, send_first, x_own = hold(table, send_first, x_own)
    table = all_sum(table, sizes, ("xl", "zl"))
    part_attn, x_own, send_first, table, dy_own = hold(part_attn, x_own, send_first, table, dy_own)

    attn_near, attn_far = with_near(part_attn), layout.far_blocks(part_attn)
    parts = [arrived(exchange(send_first))]
    x_parts = [x_own, other_x(x_own), other_z(x_own)]
    table = all_sum(table, sizes, ("y", "xh", "zh"))
    attn_near, attn_far, parts, table, x_parts, dy_own, send_rest = hold(
        attn_near, attn_far, parts, table, x_parts, dy_own, send_rest
    )

    near, far = {}, {}
    x_parts.append(other_x(x_parts[2]))
    w_attn = gathered(attn_near, [with_near(b) for b in attn_far])
    near[0], far[0] = with_near(parts[0]), layout.far_blocks(parts[0])
    rest = arrived(exchange(send_rest))
    parts += [rest[:, j * 3 * chunk : (j + 1) * 3 * chunk] for j in range(CHUNKS - 1)]
    dy_parts = [dy_own, other_x(dy_own), other_z(dy_own)]

    table = table.astype(F32)
    natural = jnp.stack([table[:, :owned].reshape(width), table[:, owned : 2 * owned].reshape(width)])
    count = places.shape[0]
    g_attn, g_mlp = jnp.split(
        jnp.take(natural.reshape(2, count, -1), places, axis=1).reshape(2, width), 2, axis=0
    )
    g_q = table[:, 2 * owned : 2 * owned + small].reshape(1, -1)
    g_k = table[:, 2 * owned + small : 2 * owned + 2 * small].reshape(1, -1)
    docs = table[:, 2 * owned + 2 * small :].astype(jnp.int32)
    docs = docs.reshape(sizes["zh"], 2, sizes["y"], sizes["xh"], 2, 2, rows)
    docs = lax.dynamic_slice(
        docs, (lax.axis_index("zh"), 0, lax.axis_index("y"), 0, 0, 0, 0), (1, 2, 1) + docs.shape[3:]
    )[0, :, 0]
    docs = jnp.moveaxis(jnp.roll(docs, -lax.axis_index("c"), axis=3), 3, 2)
    place = (
        jnp.arange(sizes["xh"])[:, None, None] * 4
        + jnp.arange(2)[None, None, :] * 2
        + (lax.axis_index("c") ^ jnp.arange(2))[None, :, None]
    )
    index = (place[..., None] * rows + jnp.arange(rows)).astype(jnp.int32)
    index = jnp.broadcast_to(index[None], docs.shape)
    k_info = jnp.stack([docs.reshape(2, -1), index.reshape(2, -1)], axis=1)
    q_info = lax.dynamic_slice(
        jnp.stack([docs, index], axis=-1), (0, lax.axis_index("xh"), 0, 0, 0, 0), (2, 1, 2, 2, rows, 2)
    ).reshape(2, -1, 2)
    doc_start = jnp.sum((k_info[:, 0, None, :] < q_info[:, :, 0, None]).astype(jnp.int32), axis=2)
    position = (q_info[:, :, 1] - doc_start).astype(F32)
    position = jnp.moveaxis(position.reshape(2, 2, 2 * rows), 1, 0).reshape(-1, 1)
    half_head = HEAD_SIZE // 2
    freqs = jnp.exp(jnp.arange(half_head).astype(F32) * (-math.log(THETA) / half_head))
    angle = position * freqs
    cosine, sine = jnp.cos(angle), jnp.sin(angle)
    cosine = jnp.concatenate([cosine, cosine], axis=1)
    sine = jnp.concatenate([-sine, sine], axis=1)
    w_attn, x_parts = hold(w_attn, x_parts)
    x_half = assemble(*x_parts, corner)
    x_side = ([x_half, other_core(x_half)], 0)
    normed_in, raw, qkv = project(x_side, w_attn, g_attn, g_q, g_k, cosine, sine, q_width)
    qkv4 = qkv.reshape(2, 2, 2 * rows, -1)
    if sizes["xh"] == 1:
        kv, kv_block = qkv4[None], 1
    else:
        kv, kv_block = lax.all_gather(qkv4[..., q_width:], "xh", axis=0, tiled=False), 0
    attended, lse = attend(qkv4, kv, kv_block, q_info, k_info, q_width)
    attended = attended.reshape(-1, q_width)
    out_column = (q_width + 2 * HEAD_SIZE) // q_width
    out_pair = [(attended, w_attn, out_column, q_width)]
    branch_other = back_rows(1, out_pair)
    branch_other, dy_parts, near[0], far[0], parts = hold(branch_other, dy_parts, near[0], far[0], parts)

    near[1], far[1] = with_near(parts[1]), layout.far_blocks(parts[1])
    weights = [gathered(near[0], [with_near(b) for b in far[0]])]
    dy_parts.append(other_x(dy_parts[2]))
    branch = back_rows(0, out_pair, other_core(branch_other))
    branch = among_four(branch.reshape(4, rows, width))
    middle, nm_copies = middle_step(branch, x_own, g_mlp)
    nm_copies, weights[0], near[1], far[1], parts[2], dy_parts = hold(
        nm_copies, weights[0], near[1], far[1], parts[2], dy_parts
    )

    near[2], far[2] = with_near(parts[2]), layout.far_blocks(parts[2])
    weights.append(gathered(near[1], [with_near(b) for b in far[1]]))
    nm_half = spread(nm_copies)
    dy_half = assemble(*dy_parts, corner)
    dy_halves = [dy_half, other_core(dy_half)]
    nm_half, dy_halves, weights[1], near[2], far[2] = hold(nm_half, dy_halves, weights[1], near[2], far[2])
    dy = (dy_halves, 0)

    def near_send(*pairs):
        return [weight_terms(layout, width, n, pairs) for n in range(1, layout.near)]

    def to_near(terms):
        return [layout.to_near(t, n + 1) for n, t in enumerate(terms)]

    def own_terms(received, *pairs):
        return weight_terms(layout, width, 0, pairs, received=received)

    def to_far(sums):
        return [layout.to_far(sums[k], k) for k in range(1, layout.zh)]

    def far_total(own, received):
        total = own.astype(F32)
        for r in received:
            total = total + r.astype(F32)
        return total.astype(BF16).reshape(TEAM_SIZE, owned, -1)

    weights.append(gathered(near[2], [with_near(b) for b in far[2]]))
    nm = ([nm_half, other_core(nm_half)], 0)
    hidden, d_gate_up, mlp, going, arriving, sums, arrived_far = [], [], [], {}, {}, {}, {}

    def chunk_step(j):
        h, d = feed_forward(nm, dy, weights[j], chunk)
        hidden.append(h)
        d_gate_up.append(d)
        mlp.append([(nm, d), (dy, h)])

    chunk_step(0)
    chunk_step(1)
    going[0] = near_send(*mlp[0])
    weights[2], going[0], d_gate_up[1] = hold(weights[2], going[0], d_gate_up[1])

    arriving[0] = to_near(going[0])
    chunk_step(2)
    mid_pairs = [(d_gate_up[j], weights[j], 0, 2 * chunk) for j in range(CHUNKS)]
    out_pairs = [(hidden[j], weights[j], 2, chunk) for j in range(CHUNKS)]
    received = other_core(back_rows(1, mid_pairs))
    terms = back_rows(0, mid_pairs, received)
    terms, hidden, d_gate_up = hold(terms, hidden, d_gate_up)
    mlp = [[(nm, d), (dy, h)] for h, d in zip(hidden, d_gate_up)]
    out_pairs = [(hidden[j], weights[j], 2, chunk) for j in range(CHUNKS)]
    terms = among_four(terms.reshape(4, rows, width))
    going[1] = near_send(*mlp[1])
    sums[0] = own_terms(arriving[0], *mlp[0])
    d_middle, d_copies = norm_back_step(terms, middle, dy_own, g_mlp, 4)
    d_copies, going[1], sums[0], hidden, d_gate_up = hold(d_copies, going[1], sums[0], hidden, d_gate_up)
    mlp = [[(nm, d), (dy, h)] for h, d in zip(hidden, d_gate_up)]
    out_pairs = [(hidden[j], weights[j], 2, chunk) for j in range(CHUNKS)]

    arrived_far[0] = to_far(sums[0])
    arriving[1] = to_near(going[1])
    d_half = spread(d_copies)
    going[2] = near_send(*mlp[2])
    sums[1] = own_terms(arriving[1], *mlp[1])
    d_half, sums[1], arrived_far[0], going[2] = hold(d_half, sums[1], arrived_far[0], going[2])

    arrived_far[1] = to_far(sums[1])
    arriving[2] = to_near(going[2])
    d_branch = ([d_half, other_core(d_half)], 0)
    d_attended = attended_gradient(d_branch, w_attn, out_column, q_width)
    d_attended = d_attended.reshape(2, 2, 2 * rows, q_width)
    d_q, d_k, d_v = attend_back(qkv4, kv, kv_block, q_info, k_info, q_width, lse, d_attended)
    if sizes["xh"] > 1:
        d_k = lax.psum_scatter(d_k, "xh", scatter_dimension=0, tiled=True)
        d_v = lax.psum_scatter(d_v, "xh", scatter_dimension=0, tiled=True)
    d_projected, head_gains = project_back(
        raw,
        d_q.reshape(-1, q_width),
        d_k.reshape(-1, HEAD_SIZE),
        d_v.reshape(-1, HEAD_SIZE),
        g_q,
        g_k,
        cosine,
        sine,
        q_width,
    )
    in_pair = [(d_projected, w_attn, 0, q_width + 2 * HEAD_SIZE)]
    received = other_core(back_rows(1, in_pair))
    terms = back_rows(0, in_pair, received, corner)
    attention = [(([normed_in], 0), d_projected), (d_branch, attended)]
    going[3] = near_send(*attention)
    terms, arriving[2] = hold(terms, arriving[2])
    sums[2] = own_terms(arriving[2], *mlp[2])
    head_gains = all_sum(head_gains, sizes, ("c",))
    terms, sums[2], arrived_far[1], going[3], head_gains, hidden = hold(
        terms, sums[2], arrived_far[1], going[3], head_gains, hidden
    )
    out_pairs = [(hidden[j], weights[j], 2, chunk) for j in range(CHUNKS)]

    arriving[3] = to_near(going[3])
    arrived_far[2] = to_far(sums[2])
    in_both = other_x(terms[3])
    received = other_core(back_rows(1, out_pairs))
    out_total = back_rows(0, out_pairs, received, corner)
    out_both = other_x(out_total[3])
    sums[3] = own_terms(arriving[3], *attention)
    head_gains = all_sum(head_gains, sizes, ("xl",))
    in_z = plain_sum(terms[2], in_both)
    back_first = [far_total(sums[j][0], arrived_far[j]) for j in range(CHUNKS - 1)]
    back_first = exchange(jnp.concatenate(back_first, axis=2))
    terms, in_z, sums[3], arrived_far[2], head_gains, out_total, out_both, back_first = hold(
        terms, in_z, sums[3], arrived_far[2], head_gains, out_total, out_both, back_first
    )

    arrived_far[3] = to_far(sums[3])
    back = exchange(far_total(sums[CHUNKS - 1][0], arrived_far[CHUNKS - 1]))
    out_z = plain_sum(out_total[2], out_both)
    output = plain_sum(middle, out_total[0], other_x(out_total[1]), other_z(out_z))
    terms = jnp.stack([terms[0], other_x(terms[1]), other_z(in_z)])
    (token_grad,) = norm_back_step(terms, x_own, d_middle, g_attn, 1)
    token_grad, output = reorder([token_grad, output], places, True)
    head_gains = all_sum(head_gains, sizes, ("zl",))
    back, arrived_far[3], head_gains, token_grad, output = hold(
        back, arrived_far[3], head_gains, token_grad, output
    )

    last = exchange(far_total(sums[3][0], arrived_far[3]))
    head_gains = all_sum(head_gains, sizes, ("y", "xh", "zh"))
    grad_gate_up, grad_down, grad_mlp_gain = unpack_chunks(
        back_first, back, w_gate_up_rows, mlp_gain.astype(F32).reshape(owned, 1), chunk
    )
    grad_qkv, grad_out, grad_attn_gain = unpack_attention(
        last, w_qkv_rows, attn_gain.astype(F32).reshape(owned, 1)
    )
    at = device_index(sizes) * small
    grad_q_gain = lax.dynamic_slice(head_gains[0], (at,), (small,))
    grad_k_gain = lax.dynamic_slice(head_gains[1], (at,), (small,))
    return (
        output[None],
        token_grad[None],
        grad_qkv,
        grad_out,
        grad_gate_up,
        grad_down,
        grad_attn_gain.reshape(owned),
        grad_q_gain,
        grad_k_gain,
        grad_mlp_gain.reshape(owned),
    )


def solution(mesh):
    dp, seq = mesh.shape["dp"], mesh.shape["seq"]
    fine = Mesh(mesh.devices.reshape(dp // 4, 2, 2, seq // 4, 2, 2), AXES)
    sizes = dict(fine.shape)
    dp_axes, seq_axes = ("zh", "zl", "y"), ("xh", "xl", "c")
    token, weight, vector = P(dp_axes, seq_axes, None), P(AXES, None), P(AXES)
    wide = P(AXES, None, None)

    def shards(*args):
        return layer(sizes, *args)

    return jax.shard_map(
        shards,
        mesh=fine,
        in_specs=(token, P(dp_axes, seq_axes), weight, weight, wide, weight, vector, vector, vector, vector, token),
        out_specs=(token, token, weight, weight, wide, weight, vector, vector, vector, vector),
        check_vma=False,
    )
```

```python
import math

import jax
import jax.numpy as jnp
from jax import lax
from jax.experimental import pallas as pl
from jax.experimental.pallas import tpu as pltpu
from jax.sharding import Mesh, PartitionSpec as P

QUERY_HEADS = 16
KEY_VALUE_HEADS = 8
HEAD_SIZE = 128
EPS = 1e-06
THETA = 1000000.0

F32 = jnp.float32
BF16 = jnp.bfloat16
SWAP = [(0, 1), (1, 0)]
TEAM = ("zl", "xl", "c")
TEAM_SIZE = 8
AXES = ("zh", "zl", "y", "xh", "xl", "c")
CHUNKS = 3
VMEM_LIMIT = 32 << 20
WEIGHT = 100
FORWARD_STEPS = 4
BACK_STEPS = 2


def hold(*values):
    return lax.optimization_barrier(values)


class Layout:
    def __init__(self, sizes):
        self.zh, self.y, self.xh = sizes["zh"], sizes["y"], sizes["xh"]
        self.near = self.y * self.xh
        self.groups = self.zh * self.near

    def order(self):
        zh, y, xh = (lax.axis_index(name) for name in ("zh", "y", "xh"))
        places = []
        for j in range(self.y):
            for i in range(self.xh):
                for k in range(self.zh):
                    for low in range(2):
                        at = ((zh + k) % self.zh * 2 + low) * self.y + (y + j) % self.y
                        places.append(at * self.xh + (xh + i) % self.xh)
        return jnp.stack(places).astype(jnp.int32)

    def far_blocks(self, block):
        return [
            lax.ppermute(block, "zh", [((i + k) % self.zh, i) for i in range(self.zh)]) for k in range(1, self.zh)
        ]

    def shifted(self, n):
        j, i = n // self.xh, n % self.xh
        return [
            (a * self.xh + b, (a + j) % self.y * self.xh + (b + i) % self.xh)
            for a in range(self.y)
            for b in range(self.xh)
        ]

    def near_blocks(self, block):
        return [
            lax.ppermute(block, ("y", "xh"), [(b, a) for a, b in self.shifted(n)]) for n in range(1, self.near)
        ]

    def to_near(self, value, n):
        return lax.ppermute(value, ("y", "xh"), self.shifted(n))

    def to_far(self, value, k):
        return lax.ppermute(value, "zh", [(i, (i + k) % self.zh) for i in range(self.zh)])


def among_four(value):
    return lax.all_to_all(value, ("zl", "xl"), 0, 0, tiled=True)


def spread(copies):
    return among_four(copies).reshape(-1, copies.shape[-1])


def other_core(value):
    return lax.ppermute(value, "c", SWAP)


def other_x(value):
    return lax.ppermute(value, "xl", SWAP)


def other_z(value):
    return lax.ppermute(value, "zl", SWAP)


def exchange(value):
    return lax.all_to_all(value, TEAM, 0, 0, tiled=True)


def all_sum(value, sizes, axes):
    for axis in axes:
        total = value
        for k in range(1, sizes[axis]):
            total = total + lax.ppermute(value, axis, [((i + k) % sizes[axis], i) for i in range(sizes[axis])])
        value = total
    return value


def device_index(sizes):
    index = 0
    for axis in AXES:
        index = index * sizes[axis] + lax.axis_index(axis)
    return index


def dot(left, right):
    return lax.dot_general(left, right, (((1,), (0,)), ((), ())), preferred_element_type=F32)


def dot_nt(left, right):
    return lax.dot_general(left, right, (((1,), (1,)), ((), ())), preferred_element_type=F32)


def dot_tn(left, right):
    return lax.dot_general(left, right, (((0,), (0,)), ((), ())), preferred_element_type=F32)


def joined(values, axis=0):
    return values[0] if len(values) == 1 else jnp.concatenate(values, axis=axis)


def shape(dims, dtype):
    return jax.ShapeDtypeStruct(tuple(dims), dtype)


def in_hbm(args):
    return [
        pltpu.with_memory_space_constraint(a, pltpu.HBM) if math.prod(a.shape) >= 1 << 16 else a for a in args
    ]


def run(kernel, grid, in_specs, out_specs, out_shape, args, flops=0):
    outs = jax.tree.leaves(out_shape)
    size = sum(math.prod(a.shape) * a.dtype.itemsize for a in list(args) + outs)
    return pl.pallas_call(
        kernel,
        grid=grid,
        in_specs=in_specs,
        out_specs=out_specs,
        out_shape=out_shape,
        compiler_params=pltpu.CompilerParams(
            vmem_limit_bytes=VMEM_LIMIT, dimension_semantics=("arbitrary",) * len(grid)
        ),
        cost_estimate=pl.CostEstimate(
            flops=WEIGHT * int(flops), bytes_accessed=WEIGHT * int(size), transcendentals=0
        ),
    )(*args)


def whole(array):
    return pl.BlockSpec(array.shape, lambda *_, n=len(array.shape): (0,) * n)


def inverse_rms(value):
    return lax.rsqrt(jnp.mean(value * value, axis=-1, keepdims=True) + EPS)


def norm_input_gradient(normed, inverse, e):
    return inverse * (e - normed * jnp.mean(e * normed, axis=-1, keepdims=True))


def reorder(values, places, inverse, copies=0):
    count = places.shape[0]
    width = values[0].shape[-1]
    cut = width // count
    if cut % 128:
        at = jnp.argsort(places) if inverse else places
        moved = [jnp.take(v.reshape(v.shape[:-1] + (count, cut)), at, axis=-2).reshape(v.shape) for v in values]
        if copies:
            moved = [jnp.broadcast_to(v[None], (copies,) + v.shape) for v in moved]
        return moved
    outs = [shape(((copies,) if copies else ()) + v.shape, v.dtype) for v in values]

    def kernel(places_ref, *refs):
        for source, target in zip(refs[: len(values)], refs[len(values) :]):
            for i in range(count):
                moving = pl.ds(pl.multiple_of(places_ref[i] * cut, 128), cut)
                still = pl.ds(i * cut, cut)
                if copies:
                    value = source[:, moving]
                    for copy in range(copies):
                        target[copy, :, still] = value
                else:
                    target[:, moving if inverse else still] = source[:, still if inverse else moving]

    size = sum(math.prod(a.shape) * a.dtype.itemsize for a in list(values) + outs)
    return pl.pallas_call(
        kernel,
        grid_spec=pltpu.PrefetchScalarGridSpec(
            num_scalar_prefetch=1,
            grid=(1,),
            in_specs=[whole(v) for v in values],
            out_specs=[whole(o) for o in outs],
        ),
        out_shape=outs,
        compiler_params=pltpu.CompilerParams(vmem_limit_bytes=VMEM_LIMIT),
        cost_estimate=pl.CostEstimate(flops=0, bytes_accessed=WEIGHT * size, transcendentals=0),
    )(places, *values)


def pack_attention(w_qkv, w_out):
    owned, columns = w_qkv.shape
    q_cols, kv_cols = QUERY_HEADS * HEAD_SIZE, KEY_VALUE_HEADS * HEAD_SIZE
    q_width = q_cols // TEAM_SIZE

    def kernel(w_ref, w_out_ref, out_ref):
        for r in range(TEAM_SIZE):
            out_ref[r, :, :q_width] = w_ref[:, r * q_width : (r + 1) * q_width]
            for part in range(2):
                at = q_cols + part * kv_cols + r * HEAD_SIZE
                to = q_width + part * HEAD_SIZE
                out_ref[r, :, to : to + HEAD_SIZE] = w_ref[:, at : at + HEAD_SIZE]
            out_ref[r, :, columns // TEAM_SIZE :] = w_out_ref[:, r * q_width : (r + 1) * q_width]

    out = shape((TEAM_SIZE, owned, columns // TEAM_SIZE + q_width), BF16)
    return run(kernel, (1,), [whole(w_qkv), whole(w_out)], whole(out), out, in_hbm([w_qkv, w_out]))


def pack_chunks(w_gate_up, w_down, chunk):
    owned = w_down.shape[0]
    per = w_down.shape[1] // TEAM_SIZE

    def kernel(gate_up_ref, down_ref, *targets):
        for j in range(CHUNKS):
            target = targets[min(j, 1)]
            to = 3 * chunk * max(j - 1, 0)
            for r in range(TEAM_SIZE):
                at = slice(r * per + j * chunk, r * per + (j + 1) * chunk)
                target[r, :, to : to + chunk] = gate_up_ref[:, 0, at]
                target[r, :, to + chunk : to + 2 * chunk] = gate_up_ref[:, 1, at]
                target[r, :, to + 2 * chunk : to + 3 * chunk] = down_ref[:, at]

    outs = [shape((TEAM_SIZE, owned, 3 * chunk * n), BF16) for n in (1, CHUNKS - 1)]
    args = [w_gate_up, w_down]
    return run(kernel, (1,), [whole(a) for a in args], [whole(o) for o in outs], outs, args)


def unpack_chunks(first, rest, w_gate_up, gain, chunk):
    owned = first.shape[1]
    per = CHUNKS * chunk

    def kernel(first_ref, rest_ref, w_ref, gain_ref, gate_up_ref, down_ref, out_ref):
        r = pl.program_id(0)
        total = jnp.zeros((owned, 1), F32)
        for j in range(CHUNKS):
            back_ref = rest_ref if j == CHUNKS - 1 else first_ref
            at, to = 3 * chunk * (j % (CHUNKS - 1)), slice(j * chunk, (j + 1) * chunk)
            for part in range(2):
                value = back_ref[0, :, at + part * chunk : at + (part + 1) * chunk].astype(F32)
                gate_up_ref[:, part, to] = value
                total = total + jnp.sum(value * w_ref[:, part, to].astype(F32), axis=1, keepdims=True)
            down_ref[:, to] = back_ref[0, :, at + 2 * chunk : at + 3 * chunk].astype(F32)
        total = total / gain_ref[...]

        @pl.when(r == 0)
        def _():
            out_ref[...] = total

        @pl.when(r > 0)
        def _():
            out_ref[...] += total

    outs = [
        shape((owned, 2, TEAM_SIZE * per), F32),
        shape((owned, TEAM_SIZE * per), F32),
        shape((owned, 1), F32),
    ]
    wide = pl.BlockSpec((owned, 2, per), lambda r: (0, 0, r))
    return run(
        kernel,
        (TEAM_SIZE,),
        [pl.BlockSpec((1,) + b.shape[1:], lambda r: (r, 0, 0)) for b in (first, rest)] + [wide, whole(gain)],
        [wide, pl.BlockSpec((owned, per), lambda r: (0, r)), whole(gain)],
        outs,
        in_hbm([first, rest, w_gate_up, gain]),
    )


def unpack_attention(back, w_qkv, gain):
    owned, columns = w_qkv.shape
    q_cols, kv_cols = QUERY_HEADS * HEAD_SIZE, KEY_VALUE_HEADS * HEAD_SIZE
    q_width = q_cols // TEAM_SIZE

    def kernel(back_ref, w_ref, gain_ref, qkv_ref, out_weight_ref, out_ref):
        total = jnp.zeros((owned, 1), F32)
        for r in range(TEAM_SIZE):
            spans = [(0, r * q_width, q_width)]
            for part in range(2):
                spans.append((q_width + part * HEAD_SIZE, q_cols + part * kv_cols + r * HEAD_SIZE, HEAD_SIZE))
            for at, to, n in spans:
                value = back_ref[r, :, at : at + n].astype(F32)
                qkv_ref[:, to : to + n] = value
                total = total + jnp.sum(value * w_ref[:, to : to + n].astype(F32), axis=1, keepdims=True)
            out_weight_ref[:, r * q_width : (r + 1) * q_width] = back_ref[
                r, :, q_width + 2 * HEAD_SIZE :
            ].astype(F32)
        out_ref[...] = total / gain_ref[...]

    outs = [shape((owned, columns), F32), shape((owned, q_cols), F32), shape((owned, 1), F32)]
    args = [back, w_qkv, gain]
    return run(kernel, (1,), [whole(a) for a in args], [whole(o) for o in outs], outs, args)


def either(step, steps, refs, body):
    per = steps // 2

    @pl.when(step < per)
    def _():
        body(*[r[0] for r in refs])

    @pl.when(step >= per)
    def _():
        body(*[r[1] for r in refs])


def half_specs(side, width, steps):
    halves, column = side
    per = steps // 2
    rows = halves[0].shape[0]
    return [
        pl.BlockSpec((rows // per, width), lambda i: (jnp.minimum(i, per - 1), column)),
        pl.BlockSpec((rows // per, width), lambda i: (jnp.maximum(i - per, 0), column)),
    ]


def turned(value, cosine, sine):
    return value * cosine + pltpu.roll(value, HEAD_SIZE // 2, 1) * sine


def project(x_side, blocks, g_attn, g_q, g_k, cosine, sine, q_width):
    count = len(blocks)
    tokens, width = 2 * x_side[0][0].shape[0], count * blocks[0].shape[0]
    columns = q_width + 2 * HEAD_SIZE
    steps = 4
    rows = tokens // steps

    def kernel(x0, x1, *refs):
        w_refs = refs[:count]
        g_attn_ref, g_q_ref, g_k_ref, cos_ref, sin_ref, normed_ref, raw_ref, qkv_ref = refs[count:]

        def body(x_ref):
            x = x_ref[...].astype(F32)
            normed_ref[...] = (x * inverse_rms(x) * g_attn_ref[...]).astype(BF16)

        either(pl.program_id(0), steps, [(x0, x1)], body)
        total = dot(normed_ref[...], joined([w[...] for w in w_refs]))
        raw_ref[...] = total[:, : q_width + HEAD_SIZE]
        cos, sin = cos_ref[...], sin_ref[...]
        for at in range(0, q_width + HEAD_SIZE, HEAD_SIZE):
            head = total[:, at : at + HEAD_SIZE]
            gain = g_q_ref[...] if at < q_width else g_k_ref[...]
            qkv_ref[:, at : at + HEAD_SIZE] = turned(head * inverse_rms(head) * gain, cos, sin).astype(BF16)
        qkv_ref[:, q_width + HEAD_SIZE :] = total[:, q_width + HEAD_SIZE :].astype(BF16)

    row = lambda n: pl.BlockSpec((rows, n), lambda i: (i, 0))
    outs = [
        shape((tokens, width), BF16),
        shape((tokens, q_width + HEAD_SIZE), F32),
        shape((tokens, columns), BF16),
    ]
    gains = [g_attn, g_q, g_k]
    return run(
        kernel,
        (steps,),
        half_specs(x_side, width, steps)
        + [pl.BlockSpec((w.shape[0], columns), lambda i: (0, 0)) for w in blocks]
        + [whole(g) for g in gains]
        + [row(HEAD_SIZE), row(HEAD_SIZE)],
        [row(o.shape[1]) for o in outs],
        outs,
        [*x_side[0], *blocks, *gains, cosine, sine],
        flops=2 * tokens * width * columns,
    )


def masked(q, k, allowed, scale):
    return jnp.where(allowed, dot_nt(q, k) * scale, -1e9)


def attention_specs(qkv, kv, kv_block, q_width, quarter, keys):
    parts = kv.shape[0]
    return [
        pl.BlockSpec((2, 1, quarter, q_width), lambda s: (0, s, 0, 0)),
        pl.BlockSpec((parts, 2, 1, quarter, 2 * HEAD_SIZE), lambda s: (0, 0, s, 0, kv_block)),
        pl.BlockSpec((1, 2 * quarter, 2), lambda s: (s, 0, 0)),
        pl.BlockSpec((1, 2, keys), lambda s: (s, 0, 0)),
    ]


def allowed_pairs(q_info, k_info):
    doc_q, index_q = q_info[:, 0:1], q_info[:, 1:2]
    doc_k, index_k = k_info[0:1, :], k_info[1:2, :]
    return (doc_q == doc_k) & (index_k <= index_q)


def attend(qkv, kv, kv_block, q_info, k_info, q_width):
    quarter = qkv.shape[2]
    keys = kv.shape[0] * 2 * quarter
    heads = q_width // HEAD_SIZE
    scale = HEAD_SIZE ** (-0.5)

    def kernel(q_ref, kv_ref, q_info_ref, k_info_ref, out_ref, lse_ref):
        allowed = allowed_pairs(q_info_ref[0], k_info_ref[0])
        pairs = kv_ref[...].reshape(keys, 2 * HEAD_SIZE)
        for h in range(heads):
            at = slice(h * HEAD_SIZE, (h + 1) * HEAD_SIZE)
            q = q_ref[:, 0, :, at].reshape(2 * quarter, HEAD_SIZE)
            scores = masked(q, pairs[:, :HEAD_SIZE], allowed, scale)
            peak = jnp.max(scores, axis=-1, keepdims=True)
            weights = jnp.exp(scores - peak)
            total = jnp.sum(weights, axis=-1, keepdims=True)
            probs = (weights * (1.0 / total)).astype(BF16)
            lse_ref[0, :, h : h + 1] = peak + jnp.log(total)
            attended = dot(probs, pairs[:, HEAD_SIZE:]).astype(BF16)
            out_ref[:, 0, :, at] = attended.reshape(2, quarter, HEAD_SIZE)

    outs = [shape((2, 2, quarter, q_width), BF16), shape((2, 2 * quarter, heads), F32)]
    return run(
        kernel,
        (2,),
        attention_specs(qkv, kv, kv_block, q_width, quarter, keys),
        [
            pl.BlockSpec((2, 1, quarter, q_width), lambda s: (0, s, 0, 0)),
            pl.BlockSpec((1, 2 * quarter, heads), lambda s: (s, 0, 0)),
        ],
        outs,
        [qkv, kv, q_info, k_info],
        flops=4 * 2 * heads * 2 * quarter * keys * HEAD_SIZE,
    )


def attend_back(qkv, kv, kv_block, q_info, k_info, q_width, lse, d_attended):
    quarter = qkv.shape[2]
    parts = kv.shape[0]
    keys = parts * 2 * quarter
    heads = q_width // HEAD_SIZE
    scale = HEAD_SIZE ** (-0.5)

    def kernel(q_ref, kv_ref, q_info_ref, k_info_ref, lse_ref, da_ref, dq_ref, dk_ref, dv_ref):
        allowed = allowed_pairs(q_info_ref[0], k_info_ref[0])
        pairs = kv_ref[...].reshape(keys, 2 * HEAD_SIZE)
        k, v = pairs[:, :HEAD_SIZE], pairs[:, HEAD_SIZE:]
        d_k = d_v = None
        for h in range(heads):
            at = slice(h * HEAD_SIZE, (h + 1) * HEAD_SIZE)
            q = q_ref[:, 0, :, at].reshape(2 * quarter, HEAD_SIZE)
            da = da_ref[:, 0, :, at].reshape(2 * quarter, HEAD_SIZE)
            probs = jnp.exp(masked(q, k, allowed, scale) - lse_ref[0, :, h : h + 1])
            d_probs = dot_nt(da, v)
            row_dot = jnp.sum(probs * d_probs, axis=-1, keepdims=True)
            d_raw = (probs * (d_probs - row_dot) * scale).astype(BF16)
            dq_ref[:, 0, :, at] = dot(d_raw, k).astype(BF16).reshape(2, quarter, HEAD_SIZE)
            k_term, v_term = dot_tn(d_raw, q), dot_tn(probs.astype(BF16), da)
            d_k = k_term if d_k is None else d_k + k_term
            d_v = v_term if d_v is None else d_v + v_term
        dk_ref[...] = d_k.astype(BF16).reshape(parts, 2, 1, quarter, HEAD_SIZE)
        dv_ref[...] = d_v.astype(BF16).reshape(parts, 2, 1, quarter, HEAD_SIZE)

    part = pl.BlockSpec((parts, 2, 1, quarter, HEAD_SIZE), lambda s: (0, 0, s, 0, 0))
    query = pl.BlockSpec((2, 1, quarter, q_width), lambda s: (0, s, 0, 0))
    part_shape = shape((parts, 2, 2, quarter, HEAD_SIZE), BF16)
    return run(
        kernel,
        (2,),
        attention_specs(qkv, kv, kv_block, q_width, quarter, keys)
        + [pl.BlockSpec((1, 2 * quarter, heads), lambda s: (s, 0, 0)), query],
        [query, part, part],
        [shape((2, 2, quarter, q_width), BF16), part_shape, part_shape],
        [qkv, kv, q_info, k_info, lse, d_attended],
        flops=10 * 2 * heads * 2 * quarter * keys * HEAD_SIZE,
    )


def project_back(raw, d_q, d_k, d_v, g_q, g_k, cosine, sine, q_width):
    tokens = raw.shape[0]
    steps = 4
    rows = tokens // steps

    def kernel(raw_ref, dq_ref, dk_ref, dv_ref, g_q_ref, g_k_ref, cos_ref, sin_ref, out_ref, gain_ref):
        cos, sin = cos_ref[...], sin_ref[...]
        gains = [jnp.zeros((1, HEAD_SIZE), F32), jnp.zeros((1, HEAD_SIZE), F32)]
        for at in range(0, q_width + HEAD_SIZE, HEAD_SIZE):
            is_key = int(at >= q_width)
            incoming = (dk_ref[...] if is_key else dq_ref[:, at : at + HEAD_SIZE]).astype(F32)
            back = turned(incoming, cos, -sin)
            head = raw_ref[:, at : at + HEAD_SIZE]
            inverse = inverse_rms(head)
            normed = head * inverse
            gains[is_key] = gains[is_key] + jnp.sum(back * normed, axis=0, keepdims=True)
            gain = g_k_ref[...] if is_key else g_q_ref[...]
            out_ref[:, at : at + HEAD_SIZE] = norm_input_gradient(normed, inverse, back * gain).astype(BF16)
        out_ref[:, q_width + HEAD_SIZE :] = dv_ref[...]

        @pl.when(pl.program_id(0) == 0)
        def _():
            gain_ref[...] = jnp.zeros_like(gain_ref)

        gain_ref[0:1, :] += gains[0]
        gain_ref[1:2, :] += gains[1]

    row = lambda n: pl.BlockSpec((rows, n), lambda i: (i, 0))
    outs = [shape((tokens, q_width + 2 * HEAD_SIZE), BF16), shape((8, HEAD_SIZE), F32)]
    args = [raw, d_q, d_k, d_v, g_q, g_k, cosine, sine]
    in_specs = [row(a.shape[1]) for a in args[:4]] + [whole(g_q), whole(g_k), row(HEAD_SIZE), row(HEAD_SIZE)]
    return run(kernel, (steps,), in_specs, [row(outs[0].shape[1]), whole(outs[1])], outs, args)


def back_rows(which, pairs, received=None, place=None):
    tokens = pairs[0][0].shape[0]
    half = tokens // 2
    steps = BACK_STEPS
    rows = half // steps
    block = half // 4
    count = len(pairs[0][1])
    per = pairs[0][1][0].shape[0]
    width = count * per
    left = [p[0] for p in pairs]
    blocks = [b for p in pairs for b in p[1]]

    def kernel(*refs):
        if place is not None:
            place_ref, refs = refs[0], refs[1:]
        left_refs, w_refs = refs[: len(left)], refs[len(left) : len(left) + len(blocks)]
        out_ref = refs[-1]
        for b in range(count):
            at = slice(b * per, (b + 1) * per)
            lefts = joined([l[...] for l in left_refs], 1)
            total = dot_nt(lefts, joined([w_refs[i * count + b][...] for i in range(len(left))], 1))
            if received is not None:
                total = total + refs[-2][:, at].astype(F32)
            total = total.astype(BF16)
            if place is None:
                out_ref[:, at] = total
                continue
            for i in range(rows // block):
                to = (pl.program_id(0) * (rows // block) + i) ^ place_ref[0]
                out_ref[to, :, at] = total[i * block : (i + 1) * block]

    out = shape((half, width), BF16)
    out_spec = pl.BlockSpec((rows, width), lambda i: (i, 0))
    in_specs = [pl.BlockSpec((rows, p[0].shape[1]), lambda i: (which * steps + i, 0)) for p in pairs]
    for _, group, column, n in pairs:
        in_specs += [pl.BlockSpec((per, n), lambda i, column=column: (0, column)) for _ in group]
    args = left + blocks
    if received is not None:
        in_specs.append(out_spec)
        args = args + [received]
    if place is not None:
        in_specs, args = [scalars()] + in_specs, [place] + args
        out = shape((4, block, width), BF16)
        out_spec = whole(out)
    flops = sum(2 * half * width * p[3] for p in pairs)
    return run(kernel, (steps,), in_specs, out_spec, out, args, flops=flops)


def feed_forward(nm, dy, groups, chunk):
    count = len(groups[0])
    per = groups[0][0].shape[0]
    blocks = [w for group in groups for w in group]
    tokens, width = 2 * nm[0][0].shape[0], count * per
    steps = FORWARD_STEPS
    rows = tokens // steps

    def kernel(nm0, nm1, dy0, dy1, *refs):
        all_refs, out_refs = refs[: len(blocks)], refs[len(blocks) :]

        def body(nm_ref, dy_ref):
            for g in range(len(groups)):
                w_refs = all_refs[g * count : (g + 1) * count]
                hidden_ref, d_ref = out_refs[2 * g : 2 * g + 2]
                both = dot(nm_ref[...], joined([w[:, : 2 * chunk] for w in w_refs]))
                d_hidden = dot(dy_ref[...], joined([w[:, 2 * chunk : 3 * chunk] for w in w_refs]))
                gate, upward = both[:, :chunk], both[:, chunk:]
                sigma = 1.0 / (1.0 + jnp.exp(-gate))
                silu = gate * sigma
                hidden_ref[...] = (silu * upward).astype(BF16)
                d_ref[:, :chunk] = (d_hidden * upward * (sigma * (1.0 + gate * (1.0 - sigma)))).astype(BF16)
                d_ref[:, chunk:] = (d_hidden * silu).astype(BF16)

        either(pl.program_id(0), steps, [(nm0, nm1), (dy0, dy1)], body)

    row = lambda n: pl.BlockSpec((rows, n), lambda i: (i, 0))
    outs = [shape((tokens, chunk), BF16), shape((tokens, 2 * chunk), BF16)] * len(groups)
    w_specs = [pl.BlockSpec((per, 3 * chunk), lambda i: (0, 0)) for _ in blocks]
    return run(
        kernel,
        (steps,),
        half_specs(nm, width, steps) + half_specs(dy, width, steps) + w_specs,
        [row(chunk), row(2 * chunk)] * len(groups),
        outs,
        in_hbm([*nm[0], *dy[0], *blocks]),
        flops=2 * tokens * width * 3 * chunk * len(groups),
    )


def weight_terms(layout, width, n, pairs, received=None):
    tile = width // layout.groups
    cuts = [p[1].shape[1] for p in pairs]
    columns = sum(cuts)
    tokens = pairs[0][1].shape[0]
    left = [(a, p[0][1]) for p in pairs for a in p[0][0]]

    def kernel(*refs):
        refs = list(refs)
        l_refs = [[refs.pop(0) for _ in p[0][0]] for p in pairs]
        d_refs = [refs.pop(0) for _ in pairs]
        in_refs = [refs.pop(0) for _ in (received or ())]
        column = 0
        for sources, d_ref, cut in zip(l_refs, d_refs, cuts):
            total = dot_tn(joined([source[...] for source in sources]), d_ref[...])
            span = slice(column, column + cut)
            column += cut
            for r in in_refs:
                total = total + r[:, span].astype(F32)
            if received is None:
                refs[0][:, span] = total.astype(BF16)
                continue
            for k, out_ref in enumerate(refs):

                @pl.when(pl.program_id(0) == k)
                def _(out_ref=out_ref, total=total, span=span):
                    out_ref[:, span] = total.astype(BF16)

    in_specs = [
        pl.BlockSpec((a.shape[0], tile), lambda k, column=column: (0, column * layout.groups + n * layout.zh + k))
        for a, column in left
    ]
    in_specs += [whole(p[1]) for p in pairs]
    args = [a for a, _ in left] + [p[1] for p in pairs]
    row = pl.BlockSpec((tile, columns), lambda k: (k, 0))
    if received is None:
        outs, out_specs = shape((layout.zh * tile, columns), BF16), row
    else:
        args += received
        in_specs += [row] * len(received)
        outs = [shape((tile, columns), BF16)] * layout.zh
        out_specs = [whole(o) for o in outs]
    return run(
        kernel, (layout.zh,), in_specs, out_specs, outs, args, flops=2 * tokens * layout.zh * tile * columns
    )


def scalars():
    return pl.BlockSpec(memory_space=pltpu.SMEM)


def assemble(own, x, z, both, place):
    rows, width = own.shape

    def kernel(place_ref, *refs):
        for i, ref in enumerate(refs[:4]):
            refs[4][place_ref[0] ^ i] = ref[...]

    out = shape((4, rows, width), BF16)
    args = [place, own, x, z, both]
    result = run(kernel, (1,), [scalars()] + [whole(a) for a in args[1:]], whole(out), out, in_hbm(args))
    return result.reshape(4 * rows, width)


def one_copy(value, width, column=0):
    if len(value.shape) == 2:
        return whole(value)
    return pl.BlockSpec((1, value.shape[1], width), lambda *_: (0, 0, column))


def rows_of(ref):
    return ref[...].reshape(ref.shape[-2:])


def middle_step(parts, x, gain):
    rows, width = x.shape[-2], gain.shape[1]

    def kernel(parts_ref, x_ref, gain_ref, middle_ref, nm_ref):
        middle = rows_of(x_ref).astype(F32)
        for i in range(4):
            middle = middle + parts_ref[i].astype(F32)
        middle_ref[...] = middle
        nm = (middle * inverse_rms(middle) * gain_ref[...]).astype(BF16)
        for i in range(4):
            nm_ref[i] = nm

    outs = [shape((rows, width), F32), shape((4, rows, width), BF16)]
    args = [parts, x, gain]
    return run(kernel, (1,), [whole(parts), one_copy(x, width), whole(gain)], [whole(o) for o in outs], outs, args)


def norm_back_step(parts, base, passed, gain, copies):
    rows, width = base.shape[-2], gain.shape[1]

    def kernel(parts_ref, base_ref, passed_ref, gain_ref, *out_refs):
        total = parts_ref[0].astype(F32)
        for i in range(1, parts.shape[0]):
            total = total + parts_ref[i].astype(F32)
        value = rows_of(base_ref).astype(F32)
        inverse = inverse_rms(value)
        result = rows_of(passed_ref).astype(F32) + norm_input_gradient(
            value * inverse, inverse, total * gain_ref[...]
        )
        rounded = result.astype(BF16)
        if copies == 1:
            out_refs[0][...] = rounded
            return
        out_refs[0][...] = result
        for i in range(copies):
            out_refs[1][i] = rounded

    outs = [shape((rows, width), F32), shape((copies, rows, width), BF16)]
    if copies == 1:
        outs = [shape((rows, width), BF16)]
    args = [parts, base, passed, gain]
    return run(kernel, (1,), [whole(parts), one_copy(base, width), one_copy(passed, width), whole(gain)], [whole(o) for o in outs], outs, args)


def plain_sum(base, *parts):
    def kernel(*refs):
        total = refs[0][...].astype(F32)
        for ref in refs[1:-1]:
            total = total + ref[...].astype(F32)
        refs[-1][...] = total.astype(BF16)

    out = shape(base.shape, BF16)
    args = [base, *parts]
    return run(kernel, (1,), [whole(a) for a in args], whole(out), out, args)


def attended_gradient(d_branch, blocks, column, n):
    count = len(blocks)
    per = blocks[0].shape[0]
    tokens, width = 2 * d_branch[0][0].shape[0], count * per
    steps = 4

    def kernel(d0, d1, *refs):
        w_refs, out_ref = refs[:count], refs[count]

        def body(d_ref):
            out_ref[...] = dot(d_ref[...], joined([w[...] for w in w_refs])).astype(BF16)

        either(pl.program_id(0), steps, [(d0, d1)], body)

    out = shape((tokens, n), BF16)
    return run(
        kernel,
        (steps,),
        half_specs(d_branch, width, steps) + [pl.BlockSpec((per, n), lambda i: (0, column)) for _ in blocks],
        pl.BlockSpec((tokens // steps, n), lambda i: (i, 0)),
        out,
        [*d_branch[0], *blocks],
        flops=2 * tokens * width * n,
    )


def layer(
    sizes,
    tokens,
    doc_ids,
    w_qkv_rows,
    w_out_rows,
    w_gate_up_rows,
    w_down_rows,
    attn_gain,
    q_gain,
    k_gain,
    mlp_gain,
    out_grad,
):
    layout = Layout(sizes)
    rows = tokens.shape[1]
    width = tokens.shape[2]
    owned = w_qkv_rows.shape[0]
    devices = width // owned
    q_width = QUERY_HEADS // TEAM_SIZE * HEAD_SIZE
    chunk = w_down_rows.shape[1] // TEAM_SIZE // CHUNKS
    small = q_gain.shape[0]
    places = layout.order()

    def arrived(value):
        return value.reshape(TEAM_SIZE * owned, -1)

    def gathered(near, far):
        columns = [near] + far
        return [columns[k][n] for n in range(layout.near) for k in range(layout.zh)]

    def with_near(block):
        return [block] + layout.near_blocks(block)

    mine = jnp.concatenate([attn_gain, mlp_gain, q_gain, k_gain, doc_ids.reshape(-1).astype(BF16)])[None]
    table = jnp.zeros((devices, mine.shape[1]), BF16)
    table = lax.dynamic_update_slice(table, mine, (device_index(sizes), 0))
    table = all_sum(table, sizes, ("c",))
    part_attn = arrived(exchange(pack_attention(w_qkv_rows, w_out_rows)))
    send_first, send_rest = pack_chunks(w_gate_up_rows, w_down_rows, chunk)
    x_own, dy_own = reorder([tokens[0], out_grad[0]], places, False)
    corner = (lax.axis_index("zl") * 2 + lax.axis_index("xl")).astype(jnp.int32).reshape(1)
    table, send_first, x_own = hold(table, send_first, x_own)
    table = all_sum(table, sizes, ("xl", "zl"))
    part_attn, x_own, send_first, table, dy_own = hold(part_attn, x_own, send_first, table, dy_own)

    attn_near, attn_far = with_near(part_attn), layout.far_blocks(part_attn)
    parts = [arrived(exchange(send_first))]
    x_parts = [x_own, other_x(x_own), other_z(x_own)]
    table = all_sum(table, sizes, ("y", "xh", "zh"))
    attn_near, attn_far, parts, table, x_parts, dy_own, send_rest = hold(
        attn_near, attn_far, parts, table, x_parts, dy_own, send_rest
    )

    near, far = {}, {}
    x_parts.append(other_x(x_parts[2]))
    w_attn = gathered(attn_near, [with_near(b) for b in attn_far])
    far[0] = layout.far_blocks(parts[0])
    dy_z = other_z(dy_own)

    table = table.astype(F32)
    natural = jnp.stack([table[:, :owned].reshape(width), table[:, owned : 2 * owned].reshape(width)])
    count = places.shape[0]
    g_attn, g_mlp = jnp.split(
        jnp.take(natural.reshape(2, count, -1), places, axis=1).reshape(2, width), 2, axis=0
    )
    g_q = table[:, 2 * owned : 2 * owned + small].reshape(1, -1)
    g_k = table[:, 2 * owned + small : 2 * owned + 2 * small].reshape(1, -1)
    docs = table[:, 2 * owned + 2 * small :].astype(jnp.int32)
    docs = docs.reshape(sizes["zh"], 2, sizes["y"], sizes["xh"], 2, 2, rows)
    docs = lax.dynamic_slice(
        docs, (lax.axis_index("zh"), 0, lax.axis_index("y"), 0, 0, 0, 0), (1, 2, 1) + docs.shape[3:]
    )[0, :, 0]
    docs = jnp.moveaxis(jnp.roll(docs, -lax.axis_index("c"), axis=3), 3, 2)
    place = (
        jnp.arange(sizes["xh"])[:, None, None] * 4
        + jnp.arange(2)[None, None, :] * 2
        + (lax.axis_index("c") ^ jnp.arange(2))[None, :, None]
    )
    index = (place[..., None] * rows + jnp.arange(rows)).astype(jnp.int32)
    index = jnp.broadcast_to(index[None], docs.shape)
    k_info = jnp.stack([docs.reshape(2, -1), index.reshape(2, -1)], axis=1)
    q_info = lax.dynamic_slice(
        jnp.stack([docs, index], axis=-1), (0, lax.axis_index("xh"), 0, 0, 0, 0), (2, 1, 2, 2, rows, 2)
    ).reshape(2, -1, 2)
    doc_start = jnp.sum((k_info[:, 0, None, :] < q_info[:, :, 0, None]).astype(jnp.int32), axis=2)
    position = (q_info[:, :, 1] - doc_start).astype(F32)
    position = jnp.moveaxis(position.reshape(2, 2, 2 * rows), 1, 0).reshape(-1, 1)
    half_head = HEAD_SIZE // 2
    freqs = jnp.exp(jnp.arange(half_head).astype(F32) * (-math.log(THETA) / half_head))
    angle = position * freqs
    cosine, sine = jnp.cos(angle), jnp.sin(angle)
    cosine = jnp.concatenate([cosine, cosine], axis=1)
    sine = jnp.concatenate([-sine, sine], axis=1)
    w_attn, x_parts = hold(w_attn, x_parts)
    x_half = assemble(*x_parts, corner)
    x_half, send_rest, dy_late, late = hold(x_half, send_rest, dy_own, parts[0])
    near[0] = with_near(late)
    rest = arrived(exchange(send_rest))
    parts += [rest[:, j * 3 * chunk : (j + 1) * 3 * chunk] for j in range(CHUNKS - 1)]
    dy_parts = [dy_own, dy_own, dy_z]
    x_side = ([x_half, other_core(x_half)], 0)
    normed_in, raw, qkv = project(x_side, w_attn, g_attn, g_q, g_k, cosine, sine, q_width)
    qkv4 = qkv.reshape(2, 2, 2 * rows, -1)
    if sizes["xh"] == 1:
        kv, kv_block = qkv4[None], 1
    else:
        kv, kv_block = lax.all_gather(qkv4[..., q_width:], "xh", axis=0, tiled=False), 0
    attended, lse = attend(qkv4, kv, kv_block, q_info, k_info, q_width)
    attended = attended.reshape(-1, q_width)
    out_column = (q_width + 2 * HEAD_SIZE) // q_width
    out_pair = [(attended, w_attn, out_column, q_width)]
    branch_other = back_rows(1, out_pair)
    branch_other, dy_parts, near[0], far[0], parts = hold(branch_other, dy_parts, near[0], far[0], parts)

    near[1], far[1] = with_near(parts[1]), layout.far_blocks(parts[1])
    weights = [gathered(near[0], [with_near(b) for b in far[0]])]
    dy_parts = [dy_parts[0], other_x(dy_parts[0]), dy_parts[2], other_x(dy_parts[2])]
    branch = back_rows(0, out_pair, other_core(branch_other))
    branch = among_four(branch.reshape(4, rows, width))
    middle, nm_copies = middle_step(branch, x_own, g_mlp)
    nm_copies, weights[0], near[1], far[1], parts[2], dy_parts = hold(
        nm_copies, weights[0], near[1], far[1], parts[2], dy_parts
    )

    near[2], far[2] = with_near(parts[2]), layout.far_blocks(parts[2])
    weights.append(gathered(near[1], [with_near(b) for b in far[1]]))
    nm_half = spread(nm_copies)
    dy_half = assemble(*dy_parts, corner)
    dy_halves = [dy_half, other_core(dy_half)]
    nm_half, dy_halves, weights[1], near[2], far[2] = hold(nm_half, dy_halves, weights[1], near[2], far[2])
    dy = (dy_halves, 0)

    def near_send(*pairs):
        return [weight_terms(layout, width, n, pairs) for n in range(1, layout.near)]

    def to_near(terms):
        return [layout.to_near(t, n + 1) for n, t in enumerate(terms)]

    def own_terms(received, *pairs):
        return weight_terms(layout, width, 0, pairs, received=received)

    def to_far(sums):
        return [layout.to_far(sums[k], k) for k in range(1, layout.zh)]

    def far_total(own, received):
        total = own.astype(F32)
        for r in received:
            total = total + r.astype(F32)
        return total.astype(BF16).reshape(TEAM_SIZE, owned, -1)

    weights.append(gathered(near[2], [with_near(b) for b in far[2]]))
    nm = ([nm_half, other_core(nm_half)], 0)
    hidden, d_gate_up, mlp, going, arriving, sums, arrived_far = [], [], [], {}, {}, {}, {}

    def chunk_steps(*chunks):
        results = feed_forward(nm, dy, [weights[j] for j in chunks], chunk)
        for h, d in zip(results[::2], results[1::2]):
            hidden.append(h)
            d_gate_up.append(d)
            mlp.append([(nm, d), (dy, h)])

    chunk_steps(0, 1)
    going[0] = near_send(*mlp[0])
    weights[2], going[0], d_gate_up[1] = hold(weights[2], going[0], d_gate_up[1])

    arriving[0] = to_near(going[0])
    chunk_steps(2)
    mid_pairs = [(d_gate_up[j], weights[j], 0, 2 * chunk) for j in range(CHUNKS)]
    out_pairs = [(hidden[j], weights[j], 2, chunk) for j in range(CHUNKS)]
    received = other_core(back_rows(1, mid_pairs))
    terms = back_rows(0, mid_pairs, received)
    terms, hidden, d_gate_up = hold(terms, hidden, d_gate_up)
    mlp = [[(nm, d), (dy, h)] for h, d in zip(hidden, d_gate_up)]
    out_pairs = [(hidden[j], weights[j], 2, chunk) for j in range(CHUNKS)]
    terms = among_four(terms.reshape(4, rows, width))
    going[1] = near_send(*mlp[1])
    sums[0] = own_terms(arriving[0], *mlp[0])
    d_middle, d_copies = norm_back_step(terms, middle, dy_own, g_mlp, 4)
    d_copies, going[1], sums[0], hidden, d_gate_up = hold(d_copies, going[1], sums[0], hidden, d_gate_up)
    mlp = [[(nm, d), (dy, h)] for h, d in zip(hidden, d_gate_up)]
    out_pairs = [(hidden[j], weights[j], 2, chunk) for j in range(CHUNKS)]

    arrived_far[0] = to_far(sums[0])
    arriving[1] = to_near(going[1])
    d_half = spread(d_copies)
    going[2] = near_send(*mlp[2])
    sums[1] = own_terms(arriving[1], *mlp[1])
    d_half, sums[1], arrived_far[0], going[2] = hold(d_half, sums[1], arrived_far[0], going[2])

    arrived_far[1] = to_far(sums[1])
    arriving[2] = to_near(going[2])
    d_branch = ([d_half, other_core(d_half)], 0)
    d_attended = attended_gradient(d_branch, w_attn, out_column, q_width)
    d_attended = d_attended.reshape(2, 2, 2 * rows, q_width)
    d_q, d_k, d_v = attend_back(qkv4, kv, kv_block, q_info, k_info, q_width, lse, d_attended)
    if sizes["xh"] > 1:
        d_k = lax.psum_scatter(d_k, "xh", scatter_dimension=0, tiled=True)
        d_v = lax.psum_scatter(d_v, "xh", scatter_dimension=0, tiled=True)
    d_projected, head_gains = project_back(
        raw,
        d_q.reshape(-1, q_width),
        d_k.reshape(-1, HEAD_SIZE),
        d_v.reshape(-1, HEAD_SIZE),
        g_q,
        g_k,
        cosine,
        sine,
        q_width,
    )
    in_pair = [(d_projected, w_attn, 0, q_width + 2 * HEAD_SIZE)]
    received = other_core(back_rows(1, in_pair))
    terms = back_rows(0, in_pair, received, corner)
    attention = [(([normed_in], 0), d_projected), (d_branch, attended)]
    going[3] = near_send(*attention)
    terms, arriving[2] = hold(terms, arriving[2])
    sums[2] = own_terms(arriving[2], *mlp[2])
    head_gains = all_sum(head_gains, sizes, ("c",))
    terms, sums[2], arrived_far[1], going[3], head_gains, hidden = hold(
        terms, sums[2], arrived_far[1], going[3], head_gains, hidden
    )
    out_pairs = [(hidden[j], weights[j], 2, chunk) for j in range(CHUNKS)]

    arriving[3] = to_near(going[3])
    arrived_far[2] = to_far(sums[2])
    in_both = other_x(terms[3])
    received = other_core(back_rows(1, out_pairs))
    out_total = back_rows(0, out_pairs, received, corner)
    out_both = other_x(out_total[3])
    sums[3] = own_terms(arriving[3], *attention)
    head_gains = all_sum(head_gains, sizes, ("xl",))
    in_z = plain_sum(terms[2], in_both)
    back_first = [far_total(sums[j][0], arrived_far[j]) for j in range(CHUNKS - 1)]
    back_first = exchange(jnp.concatenate(back_first, axis=2))
    terms, in_z, sums[3], arrived_far[2], head_gains, out_total, out_both, back_first = hold(
        terms, in_z, sums[3], arrived_far[2], head_gains, out_total, out_both, back_first
    )

    arrived_far[3] = to_far(sums[3])
    back = exchange(far_total(sums[CHUNKS - 1][0], arrived_far[CHUNKS - 1]))
    out_z = plain_sum(out_total[2], out_both)
    output = plain_sum(middle, out_total[0], other_x(out_total[1]), other_z(out_z))
    terms = jnp.stack([terms[0], other_x(terms[1]), other_z(in_z)])
    (token_grad,) = norm_back_step(terms, x_own, d_middle, g_attn, 1)
    token_grad, output = reorder([token_grad, output], places, True)
    head_gains = all_sum(head_gains, sizes, ("zl",))
    back, arrived_far[3], head_gains, token_grad, output = hold(
        back, arrived_far[3], head_gains, token_grad, output
    )

    last = exchange(far_total(sums[3][0], arrived_far[3]))
    head_gains = all_sum(head_gains, sizes, ("y", "xh", "zh"))
    grad_gate_up, grad_down, grad_mlp_gain = unpack_chunks(
        back_first, back, w_gate_up_rows, mlp_gain.astype(F32).reshape(owned, 1), chunk
    )
    grad_qkv, grad_out, grad_attn_gain = unpack_attention(
        last, w_qkv_rows, attn_gain.astype(F32).reshape(owned, 1)
    )
    at = device_index(sizes) * small
    grad_q_gain = lax.dynamic_slice(head_gains[0], (at,), (small,))
    grad_k_gain = lax.dynamic_slice(head_gains[1], (at,), (small,))
    return (
        output[None],
        token_grad[None],
        grad_qkv,
        grad_out,
        grad_gate_up,
        grad_down,
        grad_attn_gain.reshape(owned),
        grad_q_gain,
        grad_k_gain,
        grad_mlp_gain.reshape(owned),
    )


def solution(mesh):
    dp, seq = mesh.shape["dp"], mesh.shape["seq"]
    fine = Mesh(mesh.devices.reshape(dp // 4, 2, 2, seq // 4, 2, 2), AXES)
    sizes = dict(fine.shape)
    dp_axes, seq_axes = ("zh", "zl", "y"), ("xh", "xl", "c")
    token, weight, vector = P(dp_axes, seq_axes, None), P(AXES, None), P(AXES)
    wide = P(AXES, None, None)

    def shards(*args):
        return layer(sizes, *args)

    return jax.shard_map(
        shards,
        mesh=fine,
        in_specs=(token, P(dp_axes, seq_axes), weight, weight, wide, weight, vector, vector, vector, vector, token),
        out_specs=(token, token, weight, weight, wide, weight, vector, vector, vector, vector),
        check_vma=False,
    )
```

```python
import math

import jax
import jax.numpy as jnp
from jax import lax
from jax.experimental import pallas as pl
from jax.experimental.pallas import tpu as pltpu
from jax.sharding import Mesh, PartitionSpec as P

QUERY_HEADS = 16
KEY_VALUE_HEADS = 8
HEAD_SIZE = 128
EPS = 1e-06
THETA = 1000000.0

F32 = jnp.float32
BF16 = jnp.bfloat16
SWAP = [(0, 1), (1, 0)]
TEAM = ("zl", "xl", "c")
TEAM_SIZE = 8
AXES = ("zh", "zl", "y", "xh", "xl", "c")
CHUNKS = 3
VMEM_LIMIT = 32 << 20
WEIGHT = 100
FORWARD_STEPS = 4
BACK_STEPS = 1


def hold(*values):
    return lax.optimization_barrier(values)


class Layout:
    def __init__(self, sizes):
        self.zh, self.y, self.xh = sizes["zh"], sizes["y"], sizes["xh"]
        self.near = self.y * self.xh
        self.groups = self.zh * self.near

    def order(self):
        zh, y, xh = (lax.axis_index(name) for name in ("zh", "y", "xh"))
        places = []
        for j in range(self.y):
            for i in range(self.xh):
                for k in range(self.zh):
                    for low in range(2):
                        at = ((zh + k) % self.zh * 2 + low) * self.y + (y + j) % self.y
                        places.append(at * self.xh + (xh + i) % self.xh)
        return jnp.stack(places).astype(jnp.int32)

    def far_blocks(self, block):
        return [
            lax.ppermute(block, "zh", [((i + k) % self.zh, i) for i in range(self.zh)]) for k in range(1, self.zh)
        ]

    def shifted(self, n):
        j, i = n // self.xh, n % self.xh
        return [
            (a * self.xh + b, (a + j) % self.y * self.xh + (b + i) % self.xh)
            for a in range(self.y)
            for b in range(self.xh)
        ]

    def near_blocks(self, block):
        return [
            lax.ppermute(block, ("y", "xh"), [(b, a) for a, b in self.shifted(n)]) for n in range(1, self.near)
        ]

    def to_near(self, value, n):
        return lax.ppermute(value, ("y", "xh"), self.shifted(n))

    def to_far(self, value, k):
        return lax.ppermute(value, "zh", [(i, (i + k) % self.zh) for i in range(self.zh)])


def among_four(value):
    return lax.all_to_all(value, ("zl", "xl"), 0, 0, tiled=True)


def spread(copies):
    return among_four(copies).reshape(-1, copies.shape[-1])


def other_core(value):
    return lax.ppermute(value, "c", SWAP)


def other_x(value):
    return lax.ppermute(value, "xl", SWAP)


def other_z(value):
    return lax.ppermute(value, "zl", SWAP)


def exchange(value):
    return lax.all_to_all(value, TEAM, 0, 0, tiled=True)


def all_sum(value, sizes, axes):
    for axis in axes:
        total = value
        for k in range(1, sizes[axis]):
            total = total + lax.ppermute(value, axis, [((i + k) % sizes[axis], i) for i in range(sizes[axis])])
        value = total
    return value


def device_index(sizes):
    index = 0
    for axis in AXES:
        index = index * sizes[axis] + lax.axis_index(axis)
    return index


def dot(left, right):
    return lax.dot_general(left, right, (((1,), (0,)), ((), ())), preferred_element_type=F32)


def dot_nt(left, right):
    return lax.dot_general(left, right, (((1,), (1,)), ((), ())), preferred_element_type=F32)


def dot_tn(left, right):
    return lax.dot_general(left, right, (((0,), (0,)), ((), ())), preferred_element_type=F32)


def joined(values, axis=0):
    return values[0] if len(values) == 1 else jnp.concatenate(values, axis=axis)


def shape(dims, dtype):
    return jax.ShapeDtypeStruct(tuple(dims), dtype)


def in_hbm(args):
    return [
        pltpu.with_memory_space_constraint(a, pltpu.HBM) if math.prod(a.shape) >= 1 << 16 else a for a in args
    ]


def run(kernel, grid, in_specs, out_specs, out_shape, args, flops=0):
    outs = jax.tree.leaves(out_shape)
    size = sum(math.prod(a.shape) * a.dtype.itemsize for a in list(args) + outs)
    return pl.pallas_call(
        kernel,
        grid=grid,
        in_specs=in_specs,
        out_specs=out_specs,
        out_shape=out_shape,
        compiler_params=pltpu.CompilerParams(
            vmem_limit_bytes=VMEM_LIMIT, dimension_semantics=("arbitrary",) * len(grid)
        ),
        cost_estimate=pl.CostEstimate(
            flops=WEIGHT * int(flops), bytes_accessed=WEIGHT * int(size), transcendentals=0
        ),
    )(*args)


def whole(array):
    return pl.BlockSpec(array.shape, lambda *_, n=len(array.shape): (0,) * n)


def inverse_rms(value):
    return lax.rsqrt(jnp.mean(value * value, axis=-1, keepdims=True) + EPS)


def norm_input_gradient(normed, inverse, e):
    return inverse * (e - normed * jnp.mean(e * normed, axis=-1, keepdims=True))


def reorder(values, places, inverse, copies=0):
    count = places.shape[0]
    width = values[0].shape[-1]
    cut = width // count
    if cut % 128:
        at = jnp.argsort(places) if inverse else places
        moved = [jnp.take(v.reshape(v.shape[:-1] + (count, cut)), at, axis=-2).reshape(v.shape) for v in values]
        if copies:
            moved = [jnp.broadcast_to(v[None], (copies,) + v.shape) for v in moved]
        return moved
    outs = [shape(((copies,) if copies else ()) + v.shape, v.dtype) for v in values]

    def kernel(places_ref, *refs):
        for source, target in zip(refs[: len(values)], refs[len(values) :]):
            for i in range(count):
                moving = pl.ds(pl.multiple_of(places_ref[i] * cut, 128), cut)
                still = pl.ds(i * cut, cut)
                if copies:
                    value = source[:, moving]
                    for copy in range(copies):
                        target[copy, :, still] = value
                else:
                    target[:, moving if inverse else still] = source[:, still if inverse else moving]

    size = sum(math.prod(a.shape) * a.dtype.itemsize for a in list(values) + outs)
    return pl.pallas_call(
        kernel,
        grid_spec=pltpu.PrefetchScalarGridSpec(
            num_scalar_prefetch=1,
            grid=(1,),
            in_specs=[whole(v) for v in values],
            out_specs=[whole(o) for o in outs],
        ),
        out_shape=outs,
        compiler_params=pltpu.CompilerParams(vmem_limit_bytes=VMEM_LIMIT),
        cost_estimate=pl.CostEstimate(flops=0, bytes_accessed=WEIGHT * size, transcendentals=0),
    )(places, *values)


def pack_attention(w_qkv, w_out):
    owned, columns = w_qkv.shape
    q_cols, kv_cols = QUERY_HEADS * HEAD_SIZE, KEY_VALUE_HEADS * HEAD_SIZE
    q_width = q_cols // TEAM_SIZE

    def kernel(w_ref, w_out_ref, out_ref):
        for r in range(TEAM_SIZE):
            out_ref[r, :, :q_width] = w_ref[:, r * q_width : (r + 1) * q_width]
            for part in range(2):
                at = q_cols + part * kv_cols + r * HEAD_SIZE
                to = q_width + part * HEAD_SIZE
                out_ref[r, :, to : to + HEAD_SIZE] = w_ref[:, at : at + HEAD_SIZE]
            out_ref[r, :, columns // TEAM_SIZE :] = w_out_ref[:, r * q_width : (r + 1) * q_width]

    out = shape((TEAM_SIZE, owned, columns // TEAM_SIZE + q_width), BF16)
    return run(kernel, (1,), [whole(w_qkv), whole(w_out)], whole(out), out, in_hbm([w_qkv, w_out]))


def pack_chunks(w_gate_up, w_down, chunk):
    owned = w_down.shape[0]
    per = w_down.shape[1] // TEAM_SIZE

    def kernel(gate_up_ref, down_ref, *targets):
        for j in range(CHUNKS):
            target = targets[min(j, 1)]
            to = 3 * chunk * max(j - 1, 0)
            for r in range(TEAM_SIZE):
                at = slice(r * per + j * chunk, r * per + (j + 1) * chunk)
                target[r, :, to : to + chunk] = gate_up_ref[:, 0, at]
                target[r, :, to + chunk : to + 2 * chunk] = gate_up_ref[:, 1, at]
                target[r, :, to + 2 * chunk : to + 3 * chunk] = down_ref[:, at]

    outs = [shape((TEAM_SIZE, owned, 3 * chunk * n), BF16) for n in (1, CHUNKS - 1)]
    args = [w_gate_up, w_down]
    return run(kernel, (1,), [whole(a) for a in args], [whole(o) for o in outs], outs, args)


def unpack_chunks(first, rest, w_gate_up, gain, chunk):
    owned = first.shape[1]
    per = CHUNKS * chunk

    def kernel(first_ref, rest_ref, w_ref, gain_ref, gate_up_ref, down_ref, out_ref):
        r = pl.program_id(0)
        total = jnp.zeros((owned, 1), F32)
        for j in range(CHUNKS):
            back_ref = rest_ref if j == CHUNKS - 1 else first_ref
            at, to = 3 * chunk * (j % (CHUNKS - 1)), slice(j * chunk, (j + 1) * chunk)
            for part in range(2):
                value = back_ref[0, :, at + part * chunk : at + (part + 1) * chunk].astype(F32)
                gate_up_ref[:, part, to] = value
                total = total + jnp.sum(value * w_ref[:, part, to].astype(F32), axis=1, keepdims=True)
            down_ref[:, to] = back_ref[0, :, at + 2 * chunk : at + 3 * chunk].astype(F32)
        total = total / gain_ref[...]

        @pl.when(r == 0)
        def _():
            out_ref[...] = total

        @pl.when(r > 0)
        def _():
            out_ref[...] += total

    outs = [
        shape((owned, 2, TEAM_SIZE * per), F32),
        shape((owned, TEAM_SIZE * per), F32),
        shape((owned, 1), F32),
    ]
    wide = pl.BlockSpec((owned, 2, per), lambda r: (0, 0, r))
    return run(
        kernel,
        (TEAM_SIZE,),
        [pl.BlockSpec((1,) + b.shape[1:], lambda r: (r, 0, 0)) for b in (first, rest)] + [wide, whole(gain)],
        [wide, pl.BlockSpec((owned, per), lambda r: (0, r)), whole(gain)],
        outs,
        in_hbm([first, rest, w_gate_up, gain]),
    )


def unpack_attention(back, w_qkv, gain):
    owned, columns = w_qkv.shape
    q_cols, kv_cols = QUERY_HEADS * HEAD_SIZE, KEY_VALUE_HEADS * HEAD_SIZE
    q_width = q_cols // TEAM_SIZE

    def kernel(back_ref, w_ref, gain_ref, qkv_ref, out_weight_ref, out_ref):
        total = jnp.zeros((owned, 1), F32)
        for r in range(TEAM_SIZE):
            spans = [(0, r * q_width, q_width)]
            for part in range(2):
                spans.append((q_width + part * HEAD_SIZE, q_cols + part * kv_cols + r * HEAD_SIZE, HEAD_SIZE))
            for at, to, n in spans:
                value = back_ref[r, :, at : at + n].astype(F32)
                qkv_ref[:, to : to + n] = value
                total = total + jnp.sum(value * w_ref[:, to : to + n].astype(F32), axis=1, keepdims=True)
            out_weight_ref[:, r * q_width : (r + 1) * q_width] = back_ref[
                r, :, q_width + 2 * HEAD_SIZE :
            ].astype(F32)
        out_ref[...] = total / gain_ref[...]

    outs = [shape((owned, columns), F32), shape((owned, q_cols), F32), shape((owned, 1), F32)]
    args = [back, w_qkv, gain]
    return run(kernel, (1,), [whole(a) for a in args], [whole(o) for o in outs], outs, args)


def either(step, steps, refs, body):
    per = steps // 2

    @pl.when(step < per)
    def _():
        body(*[r[0] for r in refs])

    @pl.when(step >= per)
    def _():
        body(*[r[1] for r in refs])


def half_specs(side, width, steps):
    halves, column = side
    per = steps // 2
    rows = halves[0].shape[0]
    return [
        pl.BlockSpec((rows // per, width), lambda i: (jnp.minimum(i, per - 1), column)),
        pl.BlockSpec((rows // per, width), lambda i: (jnp.maximum(i - per, 0), column)),
    ]


def turned(value, cosine, sine):
    return value * cosine + pltpu.roll(value, HEAD_SIZE // 2, 1) * sine


def project(x_side, blocks, g_attn, g_q, g_k, cosine, sine, q_width):
    count = len(blocks)
    tokens, width = 2 * x_side[0][0].shape[0], count * blocks[0].shape[0]
    columns = q_width + 2 * HEAD_SIZE
    steps = 4
    rows = tokens // steps

    def kernel(x0, x1, *refs):
        w_refs = refs[:count]
        g_attn_ref, g_q_ref, g_k_ref, cos_ref, sin_ref, normed_ref, raw_ref, qkv_ref = refs[count:]

        def body(x_ref):
            x = x_ref[...].astype(F32)
            normed_ref[...] = (x * inverse_rms(x) * g_attn_ref[...]).astype(BF16)

        either(pl.program_id(0), steps, [(x0, x1)], body)
        total = dot(normed_ref[...], joined([w[...] for w in w_refs]))
        raw_ref[...] = total[:, : q_width + HEAD_SIZE]
        cos, sin = cos_ref[...], sin_ref[...]
        for at in range(0, q_width + HEAD_SIZE, HEAD_SIZE):
            head = total[:, at : at + HEAD_SIZE]
            gain = g_q_ref[...] if at < q_width else g_k_ref[...]
            qkv_ref[:, at : at + HEAD_SIZE] = turned(head * inverse_rms(head) * gain, cos, sin).astype(BF16)
        qkv_ref[:, q_width + HEAD_SIZE :] = total[:, q_width + HEAD_SIZE :].astype(BF16)

    row = lambda n: pl.BlockSpec((rows, n), lambda i: (i, 0))
    outs = [
        shape((tokens, width), BF16),
        shape((tokens, q_width + HEAD_SIZE), F32),
        shape((tokens, columns), BF16),
    ]
    gains = [g_attn, g_q, g_k]
    return run(
        kernel,
        (steps,),
        half_specs(x_side, width, steps)
        + [pl.BlockSpec((w.shape[0], columns), lambda i: (0, 0)) for w in blocks]
        + [whole(g) for g in gains]
        + [row(HEAD_SIZE), row(HEAD_SIZE)],
        [row(o.shape[1]) for o in outs],
        outs,
        [*x_side[0], *blocks, *gains, cosine, sine],
        flops=2 * tokens * width * columns,
    )


def masked(q, k, allowed, scale):
    return jnp.where(allowed, dot_nt(q, k) * scale, -1e9)


def attention_specs(qkv, kv, kv_block, q_width, quarter, keys):
    parts = kv.shape[0]
    return [
        pl.BlockSpec((2, 1, quarter, q_width), lambda s: (0, s, 0, 0)),
        pl.BlockSpec((parts, 2, 1, quarter, 2 * HEAD_SIZE), lambda s: (0, 0, s, 0, kv_block)),
        pl.BlockSpec((1, 2 * quarter, 2), lambda s: (s, 0, 0)),
        pl.BlockSpec((1, 2, keys), lambda s: (s, 0, 0)),
    ]


def allowed_pairs(q_info, k_info):
    doc_q, index_q = q_info[:, 0:1], q_info[:, 1:2]
    doc_k, index_k = k_info[0:1, :], k_info[1:2, :]
    return (doc_q == doc_k) & (index_k <= index_q)


def attend(qkv, kv, kv_block, q_info, k_info, q_width):
    quarter = qkv.shape[2]
    keys = kv.shape[0] * 2 * quarter
    heads = q_width // HEAD_SIZE
    scale = HEAD_SIZE ** (-0.5)

    def kernel(q_ref, kv_ref, q_info_ref, k_info_ref, out_ref, lse_ref):
        allowed = allowed_pairs(q_info_ref[0], k_info_ref[0])
        pairs = kv_ref[...].reshape(keys, 2 * HEAD_SIZE)
        for h in range(heads):
            at = slice(h * HEAD_SIZE, (h + 1) * HEAD_SIZE)
            q = q_ref[:, 0, :, at].reshape(2 * quarter, HEAD_SIZE)
            scores = masked(q, pairs[:, :HEAD_SIZE], allowed, scale)
            peak = jnp.max(scores, axis=-1, keepdims=True)
            weights = jnp.exp(scores - peak)
            total = jnp.sum(weights, axis=-1, keepdims=True)
            probs = (weights * (1.0 / total)).astype(BF16)
            lse_ref[0, :, h : h + 1] = peak + jnp.log(total)
            attended = dot(probs, pairs[:, HEAD_SIZE:]).astype(BF16)
            out_ref[:, 0, :, at] = attended.reshape(2, quarter, HEAD_SIZE)

    outs = [shape((2, 2, quarter, q_width), BF16), shape((2, 2 * quarter, heads), F32)]
    return run(
        kernel,
        (2,),
        attention_specs(qkv, kv, kv_block, q_width, quarter, keys),
        [
            pl.BlockSpec((2, 1, quarter, q_width), lambda s: (0, s, 0, 0)),
            pl.BlockSpec((1, 2 * quarter, heads), lambda s: (s, 0, 0)),
        ],
        outs,
        [qkv, kv, q_info, k_info],
        flops=4 * 2 * heads * 2 * quarter * keys * HEAD_SIZE,
    )


def attend_back(qkv, kv, kv_block, q_info, k_info, q_width, lse, d_attended):
    quarter = qkv.shape[2]
    parts = kv.shape[0]
    keys = parts * 2 * quarter
    heads = q_width // HEAD_SIZE
    scale = HEAD_SIZE ** (-0.5)

    def kernel(q_ref, kv_ref, q_info_ref, k_info_ref, lse_ref, da_ref, dq_ref, dk_ref, dv_ref):
        allowed = allowed_pairs(q_info_ref[0], k_info_ref[0])
        pairs = kv_ref[...].reshape(keys, 2 * HEAD_SIZE)
        k, v = pairs[:, :HEAD_SIZE], pairs[:, HEAD_SIZE:]
        d_k = d_v = None
        for h in range(heads):
            at = slice(h * HEAD_SIZE, (h + 1) * HEAD_SIZE)
            q = q_ref[:, 0, :, at].reshape(2 * quarter, HEAD_SIZE)
            da = da_ref[:, 0, :, at].reshape(2 * quarter, HEAD_SIZE)
            probs = jnp.exp(masked(q, k, allowed, scale) - lse_ref[0, :, h : h + 1])
            d_probs = dot_nt(da, v)
            row_dot = jnp.sum(probs * d_probs, axis=-1, keepdims=True)
            d_raw = (probs * (d_probs - row_dot) * scale).astype(BF16)
            dq_ref[:, 0, :, at] = dot(d_raw, k).astype(BF16).reshape(2, quarter, HEAD_SIZE)
            k_term, v_term = dot_tn(d_raw, q), dot_tn(probs.astype(BF16), da)
            d_k = k_term if d_k is None else d_k + k_term
            d_v = v_term if d_v is None else d_v + v_term
        dk_ref[...] = d_k.astype(BF16).reshape(parts, 2, 1, quarter, HEAD_SIZE)
        dv_ref[...] = d_v.astype(BF16).reshape(parts, 2, 1, quarter, HEAD_SIZE)

    part = pl.BlockSpec((parts, 2, 1, quarter, HEAD_SIZE), lambda s: (0, 0, s, 0, 0))
    query = pl.BlockSpec((2, 1, quarter, q_width), lambda s: (0, s, 0, 0))
    part_shape = shape((parts, 2, 2, quarter, HEAD_SIZE), BF16)
    return run(
        kernel,
        (2,),
        attention_specs(qkv, kv, kv_block, q_width, quarter, keys)
        + [pl.BlockSpec((1, 2 * quarter, heads), lambda s: (s, 0, 0)), query],
        [query, part, part],
        [shape((2, 2, quarter, q_width), BF16), part_shape, part_shape],
        [qkv, kv, q_info, k_info, lse, d_attended],
        flops=10 * 2 * heads * 2 * quarter * keys * HEAD_SIZE,
    )


def project_back(raw, d_q, d_k, d_v, g_q, g_k, cosine, sine, q_width):
    tokens = raw.shape[0]
    steps = 4
    rows = tokens // steps

    def kernel(raw_ref, dq_ref, dk_ref, dv_ref, g_q_ref, g_k_ref, cos_ref, sin_ref, out_ref, gain_ref):
        cos, sin = cos_ref[...], sin_ref[...]
        gains = [jnp.zeros((1, HEAD_SIZE), F32), jnp.zeros((1, HEAD_SIZE), F32)]
        for at in range(0, q_width + HEAD_SIZE, HEAD_SIZE):
            is_key = int(at >= q_width)
            incoming = (dk_ref[...] if is_key else dq_ref[:, at : at + HEAD_SIZE]).astype(F32)
            back = turned(incoming, cos, -sin)
            head = raw_ref[:, at : at + HEAD_SIZE]
            inverse = inverse_rms(head)
            normed = head * inverse
            gains[is_key] = gains[is_key] + jnp.sum(back * normed, axis=0, keepdims=True)
            gain = g_k_ref[...] if is_key else g_q_ref[...]
            out_ref[:, at : at + HEAD_SIZE] = norm_input_gradient(normed, inverse, back * gain).astype(BF16)
        out_ref[:, q_width + HEAD_SIZE :] = dv_ref[...]

        @pl.when(pl.program_id(0) == 0)
        def _():
            gain_ref[...] = jnp.zeros_like(gain_ref)

        gain_ref[0:1, :] += gains[0]
        gain_ref[1:2, :] += gains[1]

    row = lambda n: pl.BlockSpec((rows, n), lambda i: (i, 0))
    outs = [shape((tokens, q_width + 2 * HEAD_SIZE), BF16), shape((8, HEAD_SIZE), F32)]
    args = [raw, d_q, d_k, d_v, g_q, g_k, cosine, sine]
    in_specs = [row(a.shape[1]) for a in args[:4]] + [whole(g_q), whole(g_k), row(HEAD_SIZE), row(HEAD_SIZE)]
    return run(kernel, (steps,), in_specs, [row(outs[0].shape[1]), whole(outs[1])], outs, args)


def back_rows(which, pairs, received=None, place=None):
    tokens = pairs[0][0].shape[0]
    half = tokens // 2
    steps = BACK_STEPS
    rows = half // steps
    block = half // 4
    count = len(pairs[0][1])
    per = pairs[0][1][0].shape[0]
    width = count * per
    left = [p[0] for p in pairs]
    blocks = [b for p in pairs for b in p[1]]

    def kernel(*refs):
        if place is not None:
            place_ref, refs = refs[0], refs[1:]
        left_refs, w_refs = refs[: len(left)], refs[len(left) : len(left) + len(blocks)]
        out_ref = refs[-1]
        for b in range(count):
            at = slice(b * per, (b + 1) * per)
            lefts = joined([l[...] for l in left_refs], 1)
            total = dot_nt(lefts, joined([w_refs[i * count + b][...] for i in range(len(left))], 1))
            if received is not None:
                total = total + refs[-2][:, at].astype(F32)
            total = total.astype(BF16)
            if place is None:
                out_ref[:, at] = total
                continue
            for i in range(rows // block):
                to = (pl.program_id(0) * (rows // block) + i) ^ place_ref[0]
                out_ref[to, :, at] = total[i * block : (i + 1) * block]

    out = shape((half, width), BF16)
    out_spec = pl.BlockSpec((rows, width), lambda i: (i, 0))
    in_specs = [pl.BlockSpec((rows, p[0].shape[1]), lambda i: (which * steps + i, 0)) for p in pairs]
    for _, group, column, n in pairs:
        in_specs += [pl.BlockSpec((per, n), lambda i, column=column: (0, column)) for _ in group]
    args = left + blocks
    if received is not None:
        in_specs.append(out_spec)
        args = args + [received]
    if place is not None:
        in_specs, args = [scalars()] + in_specs, [place] + args
        out = shape((4, block, width), BF16)
        out_spec = whole(out)
    flops = sum(2 * half * width * p[3] for p in pairs)
    return run(kernel, (steps,), in_specs, out_spec, out, args, flops=flops)


def feed_forward(nm, dy, groups, chunk):
    count = len(groups[0])
    per = groups[0][0].shape[0]
    blocks = [w for group in groups for w in group]
    tokens, width = 2 * nm[0][0].shape[0], count * per
    steps = FORWARD_STEPS
    rows = tokens // steps

    def kernel(nm0, nm1, dy0, dy1, *refs):
        all_refs, out_refs = refs[: len(blocks)], refs[len(blocks) :]

        def body(nm_ref, dy_ref):
            for g in range(len(groups)):
                w_refs = all_refs[g * count : (g + 1) * count]
                hidden_ref, d_ref = out_refs[2 * g : 2 * g + 2]
                both = dot(nm_ref[...], joined([w[:, : 2 * chunk] for w in w_refs]))
                d_hidden = dot(dy_ref[...], joined([w[:, 2 * chunk : 3 * chunk] for w in w_refs]))
                gate, upward = both[:, :chunk], both[:, chunk:]
                sigma = 1.0 / (1.0 + jnp.exp(-gate))
                silu = gate * sigma
                hidden_ref[...] = (silu * upward).astype(BF16)
                d_ref[:, :chunk] = (d_hidden * upward * (sigma * (1.0 + gate * (1.0 - sigma)))).astype(BF16)
                d_ref[:, chunk:] = (d_hidden * silu).astype(BF16)

        either(pl.program_id(0), steps, [(nm0, nm1), (dy0, dy1)], body)

    row = lambda n: pl.BlockSpec((rows, n), lambda i: (i, 0))
    outs = [shape((tokens, chunk), BF16), shape((tokens, 2 * chunk), BF16)] * len(groups)
    w_specs = [pl.BlockSpec((per, 3 * chunk), lambda i: (0, 0)) for _ in blocks]
    return run(
        kernel,
        (steps,),
        half_specs(nm, width, steps) + half_specs(dy, width, steps) + w_specs,
        [row(chunk), row(2 * chunk)] * len(groups),
        outs,
        in_hbm([*nm[0], *dy[0], *blocks]),
        flops=2 * tokens * width * 3 * chunk * len(groups),
    )


def weight_terms(layout, width, n, pairs, received=None):
    tile = width // layout.groups
    cuts = [p[1].shape[1] for p in pairs]
    columns = sum(cuts)
    tokens = pairs[0][1].shape[0]
    left = [(a, p[0][1]) for p in pairs for a in p[0][0]]

    def kernel(*refs):
        refs = list(refs)
        l_refs = [[refs.pop(0) for _ in p[0][0]] for p in pairs]
        d_refs = [refs.pop(0) for _ in pairs]
        in_refs = [refs.pop(0) for _ in (received or ())]
        column = 0
        for sources, d_ref, cut in zip(l_refs, d_refs, cuts):
            total = dot_tn(joined([source[...] for source in sources]), d_ref[...])
            span = slice(column, column + cut)
            column += cut
            for r in in_refs:
                total = total + r[:, span].astype(F32)
            if received is None:
                refs[0][:, span] = total.astype(BF16)
                continue
            for k, out_ref in enumerate(refs):

                @pl.when(pl.program_id(0) == k)
                def _(out_ref=out_ref, total=total, span=span):
                    out_ref[:, span] = total.astype(BF16)

    in_specs = [
        pl.BlockSpec((a.shape[0], tile), lambda k, column=column: (0, column * layout.groups + n * layout.zh + k))
        for a, column in left
    ]
    in_specs += [whole(p[1]) for p in pairs]
    args = [a for a, _ in left] + [p[1] for p in pairs]
    row = pl.BlockSpec((tile, columns), lambda k: (k, 0))
    if received is None:
        outs, out_specs = shape((layout.zh * tile, columns), BF16), row
    else:
        args += received
        in_specs += [row] * len(received)
        outs = [shape((tile, columns), BF16)] * layout.zh
        out_specs = [whole(o) for o in outs]
    return run(
        kernel, (layout.zh,), in_specs, out_specs, outs, args, flops=2 * tokens * layout.zh * tile * columns
    )


def scalars():
    return pl.BlockSpec(memory_space=pltpu.SMEM)


def assemble(own, x, z, both, place):
    rows, width = own.shape

    def kernel(place_ref, *refs):
        for i, ref in enumerate(refs[:4]):
            refs[4][place_ref[0] ^ i] = ref[...]

    out = shape((4, rows, width), BF16)
    args = [place, own, x, z, both]
    result = run(kernel, (1,), [scalars()] + [whole(a) for a in args[1:]], whole(out), out, in_hbm(args))
    return result.reshape(4 * rows, width)


def one_copy(value, width, column=0):
    if len(value.shape) == 2:
        return whole(value)
    return pl.BlockSpec((1, value.shape[1], width), lambda *_: (0, 0, column))


def rows_of(ref):
    return ref[...].reshape(ref.shape[-2:])


def middle_step(parts, x, gain):
    rows, width = x.shape[-2], gain.shape[1]

    def kernel(parts_ref, x_ref, gain_ref, middle_ref, nm_ref):
        middle = rows_of(x_ref).astype(F32)
        for i in range(4):
            middle = middle + parts_ref[i].astype(F32)
        middle_ref[...] = middle
        nm = (middle * inverse_rms(middle) * gain_ref[...]).astype(BF16)
        for i in range(4):
            nm_ref[i] = nm

    outs = [shape((rows, width), F32), shape((4, rows, width), BF16)]
    args = [parts, x, gain]
    return run(kernel, (1,), [whole(parts), one_copy(x, width), whole(gain)], [whole(o) for o in outs], outs, args)


def norm_back_step(parts, base, passed, gain, copies):
    rows, width = base.shape[-2], gain.shape[1]

    def kernel(parts_ref, base_ref, passed_ref, gain_ref, *out_refs):
        total = parts_ref[0].astype(F32)
        for i in range(1, parts.shape[0]):
            total = total + parts_ref[i].astype(F32)
        value = rows_of(base_ref).astype(F32)
        inverse = inverse_rms(value)
        result = rows_of(passed_ref).astype(F32) + norm_input_gradient(
            value * inverse, inverse, total * gain_ref[...]
        )
        rounded = result.astype(BF16)
        if copies == 1:
            out_refs[0][...] = rounded
            return
        out_refs[0][...] = result
        for i in range(copies):
            out_refs[1][i] = rounded

    outs = [shape((rows, width), F32), shape((copies, rows, width), BF16)]
    if copies == 1:
        outs = [shape((rows, width), BF16)]
    args = [parts, base, passed, gain]
    return run(kernel, (1,), [whole(parts), one_copy(base, width), one_copy(passed, width), whole(gain)], [whole(o) for o in outs], outs, args)


def plain_sum(base, *parts):
    def kernel(*refs):
        total = refs[0][...].astype(F32)
        for ref in refs[1:-1]:
            total = total + ref[...].astype(F32)
        refs[-1][...] = total.astype(BF16)

    out = shape(base.shape, BF16)
    args = [base, *parts]
    return run(kernel, (1,), [whole(a) for a in args], whole(out), out, args)


def attended_gradient(d_branch, blocks, column, n):
    count = len(blocks)
    per = blocks[0].shape[0]
    tokens, width = 2 * d_branch[0][0].shape[0], count * per
    steps = 4

    def kernel(d0, d1, *refs):
        w_refs, out_ref = refs[:count], refs[count]

        def body(d_ref):
            out_ref[...] = dot(d_ref[...], joined([w[...] for w in w_refs])).astype(BF16)

        either(pl.program_id(0), steps, [(d0, d1)], body)

    out = shape((tokens, n), BF16)
    return run(
        kernel,
        (steps,),
        half_specs(d_branch, width, steps) + [pl.BlockSpec((per, n), lambda i: (0, column)) for _ in blocks],
        pl.BlockSpec((tokens // steps, n), lambda i: (i, 0)),
        out,
        [*d_branch[0], *blocks],
        flops=2 * tokens * width * n,
    )


def layer(
    sizes,
    tokens,
    doc_ids,
    w_qkv_rows,
    w_out_rows,
    w_gate_up_rows,
    w_down_rows,
    attn_gain,
    q_gain,
    k_gain,
    mlp_gain,
    out_grad,
):
    layout = Layout(sizes)
    rows = tokens.shape[1]
    width = tokens.shape[2]
    owned = w_qkv_rows.shape[0]
    devices = width // owned
    q_width = QUERY_HEADS // TEAM_SIZE * HEAD_SIZE
    chunk = w_down_rows.shape[1] // TEAM_SIZE // CHUNKS
    small = q_gain.shape[0]
    places = layout.order()

    def arrived(value):
        return value.reshape(TEAM_SIZE * owned, -1)

    def gathered(near, far):
        columns = [near] + far
        return [columns[k][n] for n in range(layout.near) for k in range(layout.zh)]

    def with_near(block):
        return [block] + layout.near_blocks(block)

    mine = jnp.concatenate([attn_gain, mlp_gain, q_gain, k_gain, doc_ids.reshape(-1).astype(BF16)])[None]
    table = jnp.zeros((devices, mine.shape[1]), BF16)
    table = lax.dynamic_update_slice(table, mine, (device_index(sizes), 0))
    table = all_sum(table, sizes, ("c",))
    part_attn = arrived(exchange(pack_attention(w_qkv_rows, w_out_rows)))
    send_first, send_rest = pack_chunks(w_gate_up_rows, w_down_rows, chunk)
    x_own, dy_own = reorder([tokens[0], out_grad[0]], places, False)
    corner = (lax.axis_index("zl") * 2 + lax.axis_index("xl")).astype(jnp.int32).reshape(1)
    table, send_first, x_own = hold(table, send_first, x_own)
    table = all_sum(table, sizes, ("xl", "zl"))
    part_attn, x_own, send_first, table, dy_own = hold(part_attn, x_own, send_first, table, dy_own)

    attn_near, attn_far = with_near(part_attn), layout.far_blocks(part_attn)
    parts = [arrived(exchange(send_first))]
    x_parts = [x_own, other_x(x_own), other_z(x_own)]
    table = all_sum(table, sizes, ("y", "xh", "zh"))
    attn_near, attn_far, parts, table, x_parts, dy_own, send_rest = hold(
        attn_near, attn_far, parts, table, x_parts, dy_own, send_rest
    )

    near, far = {}, {}
    x_parts.append(other_x(x_parts[2]))
    w_attn = gathered(attn_near, [with_near(b) for b in attn_far])
    far[0] = layout.far_blocks(parts[0])
    dy_z = other_z(dy_own)

    table = table.astype(F32)
    natural = jnp.stack([table[:, :owned].reshape(width), table[:, owned : 2 * owned].reshape(width)])
    count = places.shape[0]
    g_attn, g_mlp = jnp.split(
        jnp.take(natural.reshape(2, count, -1), places, axis=1).reshape(2, width), 2, axis=0
    )
    g_q = table[:, 2 * owned : 2 * owned + small].reshape(1, -1)
    g_k = table[:, 2 * owned + small : 2 * owned + 2 * small].reshape(1, -1)
    docs = table[:, 2 * owned + 2 * small :].astype(jnp.int32)
    docs = docs.reshape(sizes["zh"], 2, sizes["y"], sizes["xh"], 2, 2, rows)
    docs = lax.dynamic_slice(
        docs, (lax.axis_index("zh"), 0, lax.axis_index("y"), 0, 0, 0, 0), (1, 2, 1) + docs.shape[3:]
    )[0, :, 0]
    docs = jnp.moveaxis(jnp.roll(docs, -lax.axis_index("c"), axis=3), 3, 2)
    place = (
        jnp.arange(sizes["xh"])[:, None, None] * 4
        + jnp.arange(2)[None, None, :] * 2
        + (lax.axis_index("c") ^ jnp.arange(2))[None, :, None]
    )
    index = (place[..., None] * rows + jnp.arange(rows)).astype(jnp.int32)
    index = jnp.broadcast_to(index[None], docs.shape)
    k_info = jnp.stack([docs.reshape(2, -1), index.reshape(2, -1)], axis=1)
    q_info = lax.dynamic_slice(
        jnp.stack([docs, index], axis=-1), (0, lax.axis_index("xh"), 0, 0, 0, 0), (2, 1, 2, 2, rows, 2)
    ).reshape(2, -1, 2)
    doc_start = jnp.sum((k_info[:, 0, None, :] < q_info[:, :, 0, None]).astype(jnp.int32), axis=2)
    position = (q_info[:, :, 1] - doc_start).astype(F32)
    position = jnp.moveaxis(position.reshape(2, 2, 2 * rows), 1, 0).reshape(-1, 1)
    half_head = HEAD_SIZE // 2
    freqs = jnp.exp(jnp.arange(half_head).astype(F32) * (-math.log(THETA) / half_head))
    angle = position * freqs
    cosine, sine = jnp.cos(angle), jnp.sin(angle)
    cosine = jnp.concatenate([cosine, cosine], axis=1)
    sine = jnp.concatenate([-sine, sine], axis=1)
    w_attn, x_parts = hold(w_attn, x_parts)
    x_half = assemble(*x_parts, corner)
    x_half, send_rest, dy_late, late = hold(x_half, send_rest, dy_own, parts[0])
    near[0] = with_near(late)
    rest = arrived(exchange(send_rest))
    parts += [rest[:, j * 3 * chunk : (j + 1) * 3 * chunk] for j in range(CHUNKS - 1)]
    dy_parts = [dy_own, dy_own, dy_z]
    x_side = ([x_half, other_core(x_half)], 0)
    normed_in, raw, qkv = project(x_side, w_attn, g_attn, g_q, g_k, cosine, sine, q_width)
    qkv4 = qkv.reshape(2, 2, 2 * rows, -1)
    if sizes["xh"] == 1:
        kv, kv_block = qkv4[None], 1
    else:
        kv, kv_block = lax.all_gather(qkv4[..., q_width:], "xh", axis=0, tiled=False), 0
    attended, lse = attend(qkv4, kv, kv_block, q_info, k_info, q_width)
    attended = attended.reshape(-1, q_width)
    out_column = (q_width + 2 * HEAD_SIZE) // q_width
    out_pair = [(attended, w_attn, out_column, q_width)]
    branch_other = back_rows(1, out_pair)
    branch_other, dy_parts, near[0], far[0], parts = hold(branch_other, dy_parts, near[0], far[0], parts)

    near[1], far[1] = with_near(parts[1]), layout.far_blocks(parts[1])
    weights = [gathered(near[0], [with_near(b) for b in far[0]])]
    dy_parts = [dy_parts[0], other_x(dy_parts[0]), dy_parts[2], other_x(dy_parts[2])]
    branch = back_rows(0, out_pair, other_core(branch_other))
    branch = among_four(branch.reshape(4, rows, width))
    middle, nm_copies = middle_step(branch, x_own, g_mlp)
    nm_copies, weights[0], near[1], far[1], parts[2], dy_parts = hold(
        nm_copies, weights[0], near[1], far[1], parts[2], dy_parts
    )

    near[2], far[2] = with_near(parts[2]), layout.far_blocks(parts[2])
    weights.append(gathered(near[1], [with_near(b) for b in far[1]]))
    nm_half = spread(nm_copies)
    dy_half = assemble(*dy_parts, corner)
    dy_halves = [dy_half, other_core(dy_half)]
    nm_half, dy_halves, weights[1], near[2], far[2] = hold(nm_half, dy_halves, weights[1], near[2], far[2])
    dy = (dy_halves, 0)

    def near_send(*pairs):
        return [weight_terms(layout, width, n, pairs) for n in range(1, layout.near)]

    def to_near(terms):
        return [layout.to_near(t, n + 1) for n, t in enumerate(terms)]

    def own_terms(received, *pairs):
        return weight_terms(layout, width, 0, pairs, received=received)

    def to_far(sums):
        return [layout.to_far(sums[k], k) for k in range(1, layout.zh)]

    def far_total(own, received):
        total = own.astype(F32)
        for r in received:
            total = total + r.astype(F32)
        return total.astype(BF16).reshape(TEAM_SIZE, owned, -1)

    weights.append(gathered(near[2], [with_near(b) for b in far[2]]))
    nm = ([nm_half, other_core(nm_half)], 0)
    hidden, d_gate_up, mlp, going, arriving, sums, arrived_far = [], [], [], {}, {}, {}, {}

    def chunk_steps(*chunks):
        results = feed_forward(nm, dy, [weights[j] for j in chunks], chunk)
        for h, d in zip(results[::2], results[1::2]):
            hidden.append(h)
            d_gate_up.append(d)
            mlp.append([(nm, d), (dy, h)])

    chunk_steps(0, 1)
    going[0] = near_send(*mlp[0])
    weights[2], going[0], d_gate_up[1] = hold(weights[2], going[0], d_gate_up[1])

    arriving[0] = to_near(going[0])
    chunk_steps(2)
    mid_pairs = [(d_gate_up[j], weights[j], 0, 2 * chunk) for j in range(CHUNKS)]
    out_pairs = [(hidden[j], weights[j], 2, chunk) for j in range(CHUNKS)]
    received = other_core(back_rows(1, mid_pairs))
    terms = back_rows(0, mid_pairs, received)
    terms, hidden, d_gate_up = hold(terms, hidden, d_gate_up)
    mlp = [[(nm, d), (dy, h)] for h, d in zip(hidden, d_gate_up)]
    out_pairs = [(hidden[j], weights[j], 2, chunk) for j in range(CHUNKS)]
    terms = among_four(terms.reshape(4, rows, width))
    going[1] = near_send(*mlp[1])
    sums[0] = own_terms(arriving[0], *mlp[0])
    d_middle, d_copies = norm_back_step(terms, middle, dy_own, g_mlp, 4)
    d_copies, going[1], sums[0], hidden, d_gate_up = hold(d_copies, going[1], sums[0], hidden, d_gate_up)
    mlp = [[(nm, d), (dy, h)] for h, d in zip(hidden, d_gate_up)]
    out_pairs = [(hidden[j], weights[j], 2, chunk) for j in range(CHUNKS)]

    arrived_far[0] = to_far(sums[0])
    arriving[1] = to_near(going[1])
    d_half = spread(d_copies)
    going[2] = near_send(*mlp[2])
    sums[1] = own_terms(arriving[1], *mlp[1])
    d_half, sums[1], arrived_far[0], going[2] = hold(d_half, sums[1], arrived_far[0], going[2])

    arrived_far[1] = to_far(sums[1])
    arriving[2] = to_near(going[2])
    d_branch = ([d_half, other_core(d_half)], 0)
    d_attended = attended_gradient(d_branch, w_attn, out_column, q_width)
    d_attended = d_attended.reshape(2, 2, 2 * rows, q_width)
    d_q, d_k, d_v = attend_back(qkv4, kv, kv_block, q_info, k_info, q_width, lse, d_attended)
    if sizes["xh"] > 1:
        d_k = lax.psum_scatter(d_k, "xh", scatter_dimension=0, tiled=True)
        d_v = lax.psum_scatter(d_v, "xh", scatter_dimension=0, tiled=True)
    d_projected, head_gains = project_back(
        raw,
        d_q.reshape(-1, q_width),
        d_k.reshape(-1, HEAD_SIZE),
        d_v.reshape(-1, HEAD_SIZE),
        g_q,
        g_k,
        cosine,
        sine,
        q_width,
    )
    in_pair = [(d_projected, w_attn, 0, q_width + 2 * HEAD_SIZE)]
    received = other_core(back_rows(1, in_pair))
    terms = back_rows(0, in_pair, received, corner)
    attention = [(([normed_in], 0), d_projected), (d_branch, attended)]
    going[3] = near_send(*attention)
    terms, arriving[2] = hold(terms, arriving[2])
    sums[2] = own_terms(arriving[2], *mlp[2])
    head_gains = all_sum(head_gains, sizes, ("c",))
    terms, sums[2], arrived_far[1], going[3], head_gains, hidden = hold(
        terms, sums[2], arrived_far[1], going[3], head_gains, hidden
    )
    out_pairs = [(hidden[j], weights[j], 2, chunk) for j in range(CHUNKS)]

    arriving[3] = to_near(going[3])
    arrived_far[2] = to_far(sums[2])
    in_both = other_x(terms[3])
    received = other_core(back_rows(1, out_pairs))
    out_total = back_rows(0, out_pairs, received, corner)
    out_both = other_x(out_total[3])
    sums[3] = own_terms(arriving[3], *attention)
    head_gains = all_sum(head_gains, sizes, ("xl", "zl"))
    in_z = plain_sum(terms[2], in_both)
    back_first = [far_total(sums[j][0], arrived_far[j]) for j in range(CHUNKS - 1)]
    back_first = exchange(jnp.concatenate(back_first, axis=2))
    terms, in_z, sums[3], arrived_far[2], head_gains, out_total, out_both, back_first = hold(
        terms, in_z, sums[3], arrived_far[2], head_gains, out_total, out_both, back_first
    )

    arrived_far[3] = to_far(sums[3])
    back = exchange(far_total(sums[CHUNKS - 1][0], arrived_far[CHUNKS - 1]))
    out_z = plain_sum(out_total[2], out_both)
    output = plain_sum(middle, out_total[0], other_x(out_total[1]), other_z(out_z))
    terms = jnp.stack([terms[0], other_x(terms[1]), other_z(in_z)])
    (token_grad,) = norm_back_step(terms, x_own, d_middle, g_attn, 1)
    token_grad, output = reorder([token_grad, output], places, True)
    head_gains = all_sum(head_gains, sizes, ("y",))
    back, arrived_far[3], head_gains, token_grad, output = hold(
        back, arrived_far[3], head_gains, token_grad, output
    )

    last = exchange(far_total(sums[3][0], arrived_far[3]))
    head_gains = all_sum(head_gains, sizes, ("xh", "zh"))
    grad_gate_up, grad_down, grad_mlp_gain = unpack_chunks(
        back_first, back, w_gate_up_rows, mlp_gain.astype(F32).reshape(owned, 1), chunk
    )
    grad_qkv, grad_out, grad_attn_gain = unpack_attention(
        last, w_qkv_rows, attn_gain.astype(F32).reshape(owned, 1)
    )
    at = device_index(sizes) * small
    grad_q_gain = lax.dynamic_slice(head_gains[0], (at,), (small,))
    grad_k_gain = lax.dynamic_slice(head_gains[1], (at,), (small,))
    return (
        output[None],
        token_grad[None],
        grad_qkv,
        grad_out,
        grad_gate_up,
        grad_down,
        grad_attn_gain.reshape(owned),
        grad_q_gain,
        grad_k_gain,
        grad_mlp_gain.reshape(owned),
    )


def solution(mesh):
    dp, seq = mesh.shape["dp"], mesh.shape["seq"]
    fine = Mesh(mesh.devices.reshape(dp // 4, 2, 2, seq // 4, 2, 2), AXES)
    sizes = dict(fine.shape)
    dp_axes, seq_axes = ("zh", "zl", "y"), ("xh", "xl", "c")
    token, weight, vector = P(dp_axes, seq_axes, None), P(AXES, None), P(AXES)
    wide = P(AXES, None, None)

    def shards(*args):
        return layer(sizes, *args)

    return jax.shard_map(
        shards,
        mesh=fine,
        in_specs=(token, P(dp_axes, seq_axes), weight, weight, wide, weight, vector, vector, vector, vector, token),
        out_specs=(token, token, weight, weight, wide, weight, vector, vector, vector, vector),
        check_vma=False,
    )
```
